32 devices in a mesh: req: 8 (over y, x, core), tensor: 4 (over z).
Axes of the slice: x: 2, y: 2, z: 4, core: 2. Of those that a mesh axis runs over, the one named last changes fastest.
Arguments:
- hidden: bfloat16 [16, 512, 1792], P('req', 'tensor')
- suffix_len: int32 [16], P('req'), may hold values from 1 to 512, as said below
- request_group: int32 [16], P('req'), may hold values from 0 to 31
- group_slot: int32 [32], replicated, may hold values from 0 to 31, each once
- norm_first: float32 [1792], replicated, may hold values from 0.5 to 2
- query_weight: bfloat16 [1792, 256], P(None, 'tensor'), may hold values from -0.125 to 0.125
- key_weight: bfloat16 [1792, 256], P(None, 'tensor'), may hold values from -0.125 to 0.125
- value_weight: bfloat16 [1792, 1792], P(None, 'tensor'), may hold values from -0.125 to 0.125
- filter_gate: bfloat16 [1792, 1792], P(None, 'tensor'), may hold values from -0.125 to 0.125
- filter_taps: float32 [3, 1792], P(None, 'tensor'), may hold values from -3 to 3
- linear_out: bfloat16 [1792, 1792], P('tensor'), may hold values from -0.125 to 0.125
- norm_second: float32 [1792], replicated, may hold values from 0.5 to 1.5
- window_query: bfloat16 [1792, 1792], P(None, 'tensor')
- window_key: bfloat16 [1792, 1792], P(None, 'tensor')
- window_value: bfloat16 [1792, 1792], P(None, 'tensor'), may hold values from -0.125 to 0.125
- window_out: bfloat16 [1792, 1792], P('tensor'), may hold values from -0.125 to 0.125
- norm_third: float32 [1792], replicated, may hold values from 0.5 to 1.5
- gate_weight: bfloat16 [1792, 7168], P(None, 'tensor'), may hold values from -0.125 to 0.125
- up_weight: bfloat16 [1792, 7168], P(None, 'tensor'), may hold values from -0.125 to 0.125
- down_weight: bfloat16 [7168, 1792], P('tensor'), may hold values from -0.0625 to 0.0625
- prefix_sums: float32 [32, 16, 273, 112], P('req', 'tensor'), as said below
- prefix_norms: float32 [32, 16, 273], P('req', 'tensor'), as said below
- prefix_keys: bfloat16 [32, 64, 1792], P('req', None, 'tensor'), may hold values from -6 to 6
- prefix_values: bfloat16 [32, 64, 1792], P('req', None, 'tensor'), may hold values from -6 to 6
- prefix_tail: bfloat16 [32, 2, 1792], P('req', None, 'tensor'), may hold values from -10 to 10
Outputs:
- hidden_out: bfloat16 [16, 512, 1792], P('req', 'tensor')
- final_norm: float32 [16], P('req')
- top_logit: float32 [16], P('req')
The draws below stay inside these ranges and needn't reach their ends.
Inputs may be any that keep to these rules, and one draw needn't show every extreme that they name: `suffix_len`: each request's suffix is either a short one of at most 32 tokens or a long one of more than 384; some request has exactly 512. `group_slot`: each slot holds exactly one group. `prefix_sums`: A sum over 128 prefix tokens of the key feature map times the value. `prefix_norms`: A sum over the same 128 tokens of the key feature map, so its inner product with any feature map is positive.
All inputs are finite; a program needn't handle non-finite values.
Results may differ from the reference program's by a relative error of at most 0.024.
Values may be sent and summed in bfloat16 or wider, within the bound.
No kernel may reach another device: no remote copies, remote signals or barrier semaphores. Data moves between devices by JAX's collectives and lax.ppermute only.
A program may use at most 128 MiB of HBM per device.

```python
import math
import jax
import jax.numpy as jnp
from jax import lax

D = 1792
LH = 16
FD = 16
HS = 112
SH = 16
FF = 7168
WIN = 64
KC = 3
PREFIX = 128
LMAX = 512
REQS = 16
SLOTS = 32
GROUPS = 32
N_TENSOR = 4


def features_drawn(vectors):
    floats = vectors.astype(jnp.float32)
    dimension = floats.shape[-1]
    constant = jnp.ones(floats.shape[:-1] + (1,), jnp.float32)
    linear_part = floats * dimension ** (-0.25)
    square_part = (floats[..., :, None] * floats[..., None, :]).reshape(floats.shape[:-1] + (dimension * dimension,))
    square_part = square_part * (2.0 * dimension) ** (-0.5)
    return jnp.concatenate([constant, linear_part, square_part], axis=-1)


def prefix_terms(key):
    key_draw, value_draw, scale_draw = jax.random.split(jax.random.fold_in(key, 11), 3)
    head_scale = jnp.exp(jax.random.uniform(scale_draw, (SLOTS, LH, 1, 1), jnp.float32, -0.6931, 0.6931))
    past_keys = jax.random.normal(key_draw, (SLOTS, LH, PREFIX, FD), jnp.float32) * head_scale
    past_values = jax.random.normal(value_draw, (SLOTS, LH, PREFIX, HS), jnp.float32)
    mapped = features_drawn(past_keys)
    state_sums = jnp.einsum('ahpf,ahpd->ahfd', mapped, past_values, precision=lax.Precision.HIGHEST)
    return (state_sums, jnp.sum(mapped, axis=2))


def draw_prefix_sums(key, part):
    state_sums, state_norms = prefix_terms(key)
    return state_sums


def draw_prefix_norms(key, part):
    state_sums, state_norms = prefix_terms(key)
    return state_norms


def draw_suffix_len(key, part):
    kind_key, short_key, long_key, pick_key = jax.random.split(jax.random.fold_in(key, 23), 4)
    longish = jax.random.randint(kind_key, (REQS,), 0, 2)
    short_len = jax.random.randint(short_key, (REQS,), 1, LMAX // 16 + 1)
    long_len = LMAX - jax.random.randint(long_key, (REQS,), 0, LMAX // 4)
    picked = jax.random.randint(pick_key, (), 0, REQS)
    lengths = jnp.where(longish == 1, long_len, short_len)
    return jnp.where(jnp.arange(REQS) == picked, LMAX, lengths).astype(jnp.int32)


def draw_hidden(key, part):
    base_key = jax.random.fold_in(jax.random.fold_in(key, 41), 0)
    rows = jax.random.truncated_normal(base_key, -6.0, 6.0, (REQS, LMAX, D), jnp.float32)
    return rows.astype(jnp.bfloat16)


def window_pair(key):
    query_key, own_key = jax.random.split(jax.random.fold_in(key, 31), 2)
    scale = D ** (-0.5)
    query_part = jax.random.truncated_normal(query_key, -4.0, 4.0, (D, SH * HS), jnp.float32) * scale
    own_part = jax.random.truncated_normal(own_key, -4.0, 4.0, (D, SH * HS), jnp.float32) * scale
    key_part = own_part
    return (query_part, key_part)


def draw_window_query(key, part):
    query_part, key_part = window_pair(key)
    return query_part.astype(jnp.bfloat16)


def draw_window_key(key, part):
    query_part, key_part = window_pair(key)
    return key_part.astype(jnp.bfloat16)


def with_ends(entries, key, low, high):
    longest = entries.shape.index(max(entries.shape))
    spots = []
    for shift in (0, 1):
        where = [jax.random.randint(jax.random.fold_in(key, axis), (), 0, length) for axis, length in enumerate(entries.shape)]
        where[longest] = (where[longest] + shift) % entries.shape[longest]
        spots.append(tuple(where))
    return entries.at[spots[0]].set(low).at[spots[1]].set(high)


def shard_levels(stream_key, shape, shards, least, high):
    gain = 1.0
    for dim, shards_of in shards:
        draws = jax.random.uniform(jax.random.fold_in(jax.random.fold_in(stream_key, 6), dim), (shards_of,), jnp.float32, least / len(shards), high / len(shards))
        gain = gain * jnp.repeat(jnp.exp(draws), shape[dim] // shards_of).reshape((-1,) + (1,) * (len(shape) - 1 - dim))
    return gain


def normal_values(stream_key, shape, scale, bound, cuts=(), dtype=jnp.bfloat16):
    gain = shard_levels(stream_key, shape, cuts, -0.22, 0.18) if cuts else 1.0
    array = jax.random.normal(stream_key, shape, jnp.float32) * scale * gain
    return jnp.minimum(jnp.maximum(array, -bound), bound).astype(dtype)


def setup_inputs(seed: int = 0) -> dict:
    key_list = jax.random.split(jax.random.key(seed), 26)
    hidden = draw_hidden(jax.random.fold_in(key_list[25], 71), 0)
    suffix_len = draw_suffix_len(jax.random.fold_in(key_list[25], 71), 0)
    request_group = with_ends(jax.random.randint(key_list[2], (REQS,), 0, GROUPS), jax.random.fold_in(key_list[2], 1), 0, GROUPS - 1).astype(jnp.int32)
    group_slot = jax.random.permutation(key_list[3], GROUPS).astype(jnp.int32)
    norm_first = jnp.clip(jnp.exp(jax.random.uniform(key_list[4], (D,), jnp.float32, math.log(0.5), math.log(2.0))), 0.5, 2.0)
    query_weight = normal_values(key_list[5], (D, LH * FD), D ** -0.5, 0.125, ((1, 4),))
    key_weight = normal_values(key_list[6], (D, LH * FD), D ** -0.5, 0.125, ((1, 4),))
    value_weight = normal_values(key_list[7], (D, LH * HS), D ** -0.5, 0.125, ((1, 4),))
    filter_gate = normal_values(key_list[8], (D, LH * HS), D ** -0.5, 0.125, ((1, 4),))
    filter_taps = normal_values(key_list[9], (KC, LH * HS), 0.6, 3.0, ((1, 4),), jnp.float32)
    linear_out = normal_values(key_list[10], (LH * HS, D), (LH * HS) ** -0.5, 0.125, ((0, 4),))
    norm_second = jnp.clip(1.0 + 0.1 * jax.random.normal(key_list[11], (D,), jnp.float32), 0.5, 1.5)
    window_query = draw_window_query(jax.random.fold_in(key_list[25], 71), 0)
    window_key = draw_window_key(jax.random.fold_in(key_list[25], 71), 0)
    window_value = normal_values(key_list[14], (D, SH * HS), D ** -0.5, 0.125, ((1, 4),))
    window_out = normal_values(key_list[15], (SH * HS, D), (SH * HS) ** -0.5, 0.125, ((0, 4),))
    norm_third = jnp.clip(1.0 + 0.1 * jax.random.normal(key_list[16], (D,), jnp.float32), 0.5, 1.5)
    gate_weight = normal_values(key_list[17], (D, FF), D ** -0.5, 0.125, ((1, 4),))
    up_weight = normal_values(key_list[18], (D, FF), D ** -0.5, 0.125, ((1, 4),))
    down_weight = normal_values(key_list[19], (FF, D), FF ** -0.5, 0.0625, ((0, 4),))
    prefix_sums = draw_prefix_sums(jax.random.fold_in(key_list[25], 71), 0)
    prefix_norms = draw_prefix_norms(jax.random.fold_in(key_list[25], 71), 0)
    prefix_keys = normal_values(key_list[22], (SLOTS, WIN, SH * HS), 1.0, 6.0, ((0, 8), (2, 4)))
    prefix_values = normal_values(key_list[23], (SLOTS, WIN, SH * HS), 1.0, 6.0, ((0, 8), (2, 4)))
    prefix_tail = normal_values(key_list[24], (SLOTS, KC - 1, LH * HS), 2.0, 10.0, ((0, 8), (2, 4)))
    return {"hidden": hidden, "suffix_len": suffix_len, "request_group": request_group, "group_slot": group_slot, "norm_first": norm_first, "query_weight": query_weight, "key_weight": key_weight, "value_weight": value_weight, "filter_gate": filter_gate, "filter_taps": filter_taps, "linear_out": linear_out, "norm_second": norm_second, "window_query": window_query, "window_key": window_key, "window_value": window_value, "window_out": window_out, "norm_third": norm_third, "gate_weight": gate_weight, "up_weight": up_weight, "down_weight": down_weight, "prefix_sums": prefix_sums, "prefix_norms": prefix_norms, "prefix_keys": prefix_keys, "prefix_values": prefix_values, "prefix_tail": prefix_tail}


EPS = 1e-05

def rms_norm(row_block, gain_vector):
    floats = row_block.astype(jnp.float32)
    inverse_rms = lax.rsqrt(lax.optimization_barrier(jnp.mean(floats * floats, axis=-1, keepdims=True)) + EPS)
    return (floats * inverse_rms * gain_vector.astype(jnp.float32)).astype(jnp.bfloat16)

def features(vectors):
    floats = vectors.astype(jnp.float32)
    dimension = floats.shape[-1]
    constant = jnp.ones(floats.shape[:-1] + (1,), jnp.float32)
    linear_part = floats * dimension ** (-0.25)
    square_part = (floats[..., :, None] * floats[..., None, :]).reshape(floats.shape[:-1] + (dimension * dimension,))
    square_part = square_part * (2.0 * dimension) ** (-0.5)
    return jnp.concatenate([constant, linear_part, square_part], axis=-1)

def rounded(values):
    return lax.optimization_barrier(values.astype(jnp.bfloat16)).astype(jnp.float32)

def tensor_sum(left_rows, right_matrix):
    row_total, inner_total = left_rows.shape
    share_size = inner_total // N_TENSOR
    pieces = left_rows.astype(jnp.float32).reshape(row_total, N_TENSOR, share_size)
    blocks = right_matrix.astype(jnp.float32).reshape(N_TENSOR, share_size, right_matrix.shape[1])
    partial_sum = jnp.einsum('rnk,nkd->nrd', pieces, blocks)
    return lax.optimization_barrier(jnp.sum(rounded(partial_sum), axis=0))

def reference(hidden, suffix_len, request_group, group_slot, norm_first, query_weight, key_weight, value_weight, filter_gate, filter_taps, linear_out, norm_second, window_query, window_key, window_value, window_out, norm_third, gate_weight, up_weight, down_weight, prefix_sums, prefix_norms, prefix_keys, prefix_values, prefix_tail):
    slot_ids = group_slot[request_group].astype(jnp.int32)
    position = jnp.arange(LMAX)
    causal = position[:, None] >= position[None, :]
    key_place = jnp.arange(WIN + LMAX)
    allowed = (key_place[None, :] > position[:, None]) & (key_place[None, :] <= position[:, None] + WIN)

    def one_request(request):
        row_block, length, slot_index = request
        normed = rms_norm(row_block, norm_first)
        queries = jnp.dot(normed, query_weight, preferred_element_type=jnp.float32).astype(jnp.bfloat16).reshape(LMAX, LH, FD)
        key_rows = jnp.dot(normed, key_weight, preferred_element_type=jnp.float32).astype(jnp.bfloat16).reshape(LMAX, LH, FD)
        values_lin = jnp.dot(normed, value_weight, preferred_element_type=jnp.float32).astype(jnp.bfloat16)
        gating = jnp.dot(normed, filter_gate, preferred_element_type=jnp.float32).astype(jnp.bfloat16)
        extended = jnp.concatenate([prefix_tail[slot_index], values_lin], axis=0).astype(jnp.float32)
        convolved = sum((filter_taps[offset] * extended[KC - 1 - offset:KC - 1 - offset + LMAX] for offset in range(KC)))
        mixed_values = (convolved * jax.nn.silu(gating.astype(jnp.float32))).astype(jnp.bfloat16).reshape(LMAX, LH, HS)
        scores = jnp.einsum('thf,shf->hts', queries.astype(jnp.float32), key_rows.astype(jnp.float32)) * FD ** (-0.5)
        weights_lin = jnp.where(causal[None], 1.0 + scores + 0.5 * scores * scores, 0.0)
        numerator = jnp.einsum('hts,shd->thd', rounded(weights_lin), mixed_values.astype(jnp.float32))
        denominator = jnp.transpose(lax.optimization_barrier(jnp.sum(weights_lin, axis=-1)))
        mapped = features(queries)
        numerator = numerator + jnp.einsum('thf,hfd->thd', mapped, prefix_sums[slot_index], precision=lax.Precision.HIGHEST)
        denominator = denominator + jnp.einsum('thf,hf->th', mapped, prefix_norms[slot_index], precision=lax.Precision.HIGHEST)
        linear_rows = (numerator / denominator[..., None]).astype(jnp.bfloat16).reshape(LMAX, LH * HS)
        first_out = (row_block.astype(jnp.float32) + tensor_sum(linear_rows, linear_out)).astype(jnp.bfloat16)
        normed = rms_norm(first_out, norm_second)
        window_q = jnp.dot(normed, window_query, preferred_element_type=jnp.float32).astype(jnp.bfloat16).reshape(LMAX, SH, HS)
        window_k = jnp.dot(normed, window_key, preferred_element_type=jnp.float32).astype(jnp.bfloat16)
        window_v = jnp.dot(normed, window_value, preferred_element_type=jnp.float32).astype(jnp.bfloat16)
        all_keys = jnp.concatenate([prefix_keys[slot_index], window_k], axis=0).reshape(WIN + LMAX, SH, HS)
        all_values = jnp.concatenate([prefix_values[slot_index], window_v], axis=0).reshape(WIN + LMAX, SH, HS)
        logits = jnp.einsum('thd,phd->htp', window_q.astype(jnp.float32), all_keys.astype(jnp.float32)) * HS ** (-0.5)
        logits = jnp.where(allowed[None], logits, -jnp.inf)
        row_max = lax.optimization_barrier(jnp.max(logits, axis=-1, keepdims=True))
        exponent = jnp.exp(logits - row_max)
        probabilities = (exponent / lax.optimization_barrier(jnp.sum(exponent, axis=-1, keepdims=True))).astype(jnp.bfloat16)
        attended = jnp.einsum('htp,phd->thd', probabilities.astype(jnp.float32), all_values.astype(jnp.float32)).astype(jnp.bfloat16).reshape(LMAX, SH * HS)
        second_out = (first_out.astype(jnp.float32) + tensor_sum(attended, window_out)).astype(jnp.bfloat16)
        final_mask = position == length - 1
        best_logit = jnp.max(jnp.where(final_mask[None, :], row_max[..., 0], -jnp.inf))
        normed = rms_norm(second_out, norm_third)
        gate_rows = jnp.dot(normed, gate_weight, preferred_element_type=jnp.float32)
        up_rows = jnp.dot(normed, up_weight, preferred_element_type=jnp.float32)
        inner_rows = (jax.nn.silu(gate_rows) * up_rows).astype(jnp.bfloat16)
        third_out = (second_out.astype(jnp.float32) + tensor_sum(inner_rows, down_weight)).astype(jnp.bfloat16)
        live = position < length
        masked = jnp.where(live[:, None], third_out, jnp.zeros_like(third_out))
        third_f = third_out.astype(jnp.float32)
        squares = jnp.sum(jnp.where(live[:, None], third_f * third_f, 0.0))
        row_norm = jnp.sqrt(squares / D)
        return (masked, row_norm, best_logit)
    hidden_out, final_norm, top_logit = lax.map(one_request, (hidden, suffix_len, slot_ids))
    return (hidden_out, final_norm, top_logit)
```

```python
import jax
import jax.numpy as jnp
from jax import lax
from jax.sharding import PartitionSpec as P

D = 1792
FD = 16
HS = 112
WIN = 64
KC = 3
LMAX = 512
PAIRS = FD // 2 + 1

EPS = 1e-05
BF = jnp.bfloat16
F32 = jnp.float32


def rms_norm(rows, gain):
    floats = rows.astype(F32)
    inverse_rms = lax.rsqrt(jnp.mean(floats * floats, axis=-1, keepdims=True) + EPS)
    return (floats * inverse_rms * gain).astype(BF)


def dot(left, right):
    return jnp.dot(left, right, preferred_element_type=F32)


def folded_features(queries):
    floats = jnp.transpose(queries.astype(F32), (1, 0, 2))
    parts = [jnp.ones(floats.shape[:-1] + (1,), F32), floats * FD ** (-0.25)]
    for shift in range(PAIRS):
        parts.append(floats * jnp.roll(floats, -shift, axis=-1) * (2.0 * FD) ** (-0.5))
    return jnp.concatenate(parts, axis=-1)


def fold_matrix():
    row = jnp.arange(1 + FD + PAIRS * FD)[:, None]
    column = jnp.arange(1 + FD + FD * FD)[None, :]
    shift, first = (row - 1 - FD) // FD, (row - 1 - FD) % FD
    second = (first + shift) % FD
    major, minor = (column - 1 - FD) // FD, (column - 1 - FD) % FD
    straight = (major == first) & (minor == second)
    swapped = (major == second) & (minor == first) & (shift > 0) & (shift < FD // 2)
    squares = (row > FD) & (column > FD) & (straight | swapped)
    return jnp.where((row == column) & (row <= FD) | squares, 1.0, 0.0).astype(F32)


def line_gather(rows, axis, count):
    here = lax.axis_index(axis)
    size = rows.shape[0]
    up = down = rows
    ups, downs = [], []
    for step in range(1, count):
        up = lax.ppermute(up, axis, [(i, i + 1) for i in range(step - 1, count - 1)])
        down = lax.ppermute(down, axis, [(i + 1, i) for i in range(count - step)])
        ups.append(up)
        downs.append(down)
    around = jnp.concatenate(ups[::-1] + [rows] + downs)
    return lax.dynamic_slice_in_dim(around, (count - 1 - here) * size, count * size, 0)


def line_scatter(partial, axis, count):
    here = lax.axis_index(axis)
    size = partial.shape[0] // count

    def block(index):
        return lax.dynamic_slice_in_dim(partial, index * size, size, 0)

    up = down = None
    for step in range(1, count):
        to_up = block(jnp.minimum(here + count - step, count - 1))
        to_down = block(jnp.maximum(here - count + step, 0))
        if up is not None:
            to_up, to_down = to_up + up, to_down + down
        up = lax.ppermute(to_up, axis, [(i, i + 1) for i in range(step)])
        down = lax.ppermute(to_down, axis, [(i + 1, i) for i in range(count - 1 - step, count - 1)])
    return block(here).astype(F32) + up.astype(F32) + down.astype(F32)


def middle_exchange(partial, stream, axis):
    here = lax.axis_index(axis)
    half = partial.shape[0] // 2
    low = here < 2
    middle = (here == 1) | (here == 2)

    def near_far(rows):
        first, second = rows[:half], rows[half:]
        return jnp.where(low, first, second), jnp.where(low, second, first)

    inward, across, outward = [(0, 1), (3, 2)], [(1, 2), (2, 1)], [(1, 0), (2, 3)]
    near, far = near_far(partial)
    far_in = lax.ppermute(far, axis, inward)
    near_in = lax.ppermute(near, axis, inward)
    crossed = lax.ppermute(far + far_in, axis, across)
    total = near.astype(F32) + near_in.astype(F32) + crossed.astype(F32)
    own = (near_far(stream)[0].astype(F32) + total).astype(BF)
    other = lax.ppermute(own, axis, across)
    own_out = lax.ppermute(own, axis, outward)
    other_out = lax.ppermute(other, axis, outward)
    near = jnp.where(middle, own, own_out)
    far = jnp.where(middle, other, other_out)
    return jnp.concatenate([jnp.where(low, near, far), jnp.where(low, far, near)])


def settle(partial, stream, axis, count):
    if count == 4:
        return middle_exchange(partial, stream, axis)
    here = lax.axis_index(axis)
    size = partial.shape[0] // count
    mine = lax.dynamic_slice_in_dim(stream, here * size, size, 0)
    total = line_scatter(partial, axis, count)
    return line_gather((mine.astype(F32) + total).astype(BF), axis, count)


def bring_home(packs, axis, count):
    here = lax.axis_index(axis)
    bit = 1
    while bit < count:
        pairs = packs.reshape((packs.shape[0] // 2, 2) + packs.shape[1:])
        upper = (here & bit) != 0
        keep = jnp.where(upper, pairs[:, 1], pairs[:, 0])
        send = jnp.where(upper, pairs[:, 0], pairs[:, 1])
        packs = keep + lax.ppermute(send, axis, [(i, i ^ bit) for i in range(count)])
        bit *= 2
    return packs[0]


def make(req_count, tensor_count):
    def per_device(
        hidden,
        suffix_len,
        request_group,
        group_slot,
        norm_first,
        query_weight,
        key_weight,
        value_weight,
        filter_gate,
        filter_taps,
        linear_out,
        norm_second,
        window_query,
        window_key,
        window_value,
        window_out,
        norm_third,
        gate_weight,
        up_weight,
        down_weight,
        prefix_sums,
        prefix_norms,
        prefix_keys,
        prefix_values,
        prefix_tail,
    ):
        requests_here = hidden.shape[0]
        share_rows = hidden.shape[1]
        slots_here, heads = prefix_sums.shape[:2]
        width = heads * HS

        groups = lax.all_gather(request_group, "req", axis=0, tiled=True)
        matches = jnp.arange(group_slot.shape[0])[None, :] == groups[:, None]
        slots = jnp.sum(jnp.where(matches, group_slot[None, :], 0), axis=1)
        fold = fold_matrix()
        sums = jnp.einsum("fg,ahgd->afhd", fold, prefix_sums, precision=lax.Precision.HIGHEST)
        terms = sums.shape[1]
        norms = jnp.einsum("fg,ahg->afh", fold, prefix_norms, precision=lax.Precision.HIGHEST)
        norms = jnp.pad(norms.reshape(slots_here, -1), ((0, 0), (0, 2 * width - terms * heads)))
        pack = jnp.concatenate(
            [
                sums.reshape(slots_here, terms, width).astype(BF),
                norms.reshape(slots_here, 2, width).astype(BF),
                prefix_keys,
                prefix_values,
                prefix_tail,
            ],
            axis=1,
        )
        rows = pack.shape[1]
        pack = jnp.pad(pack, ((0, 0), (0, -rows % 32), (0, 0)))
        half = pack.shape[1] // 2
        pack = jnp.concatenate([pack[:, :half], pack[:, half:]], axis=2)
        local = slots - lax.axis_index("req") * slots_here
        owned = (local >= 0) & (local < slots_here)
        sent = jnp.take(pack, jnp.clip(local, 0, slots_here - 1), axis=0)
        sent = jnp.where(owned[:, None, None], sent, jnp.zeros_like(sent))
        sent = sent.reshape((req_count, requests_here) + sent.shape[1:])
        states = bring_home(sent, "req", req_count)
        states = jnp.concatenate([states[:, :, :width], states[:, :, width:]], axis=1)

        position = jnp.arange(LMAX)
        causal = position[:, None] >= position[None, :]
        bands = LMAX // WIN
        band_row = jnp.arange(WIN)[:, None]
        band_key = jnp.arange(2 * WIN)[None, :]
        allowed = (band_key > band_row) & (band_key <= band_row + WIN)

        def linear_part(request, stream):
            state = states[request]
            state_sums = state[:terms].reshape(terms, heads, HS)
            state_norms = state[terms : terms + 2].reshape(-1)[: terms * heads].reshape(terms, heads)
            tail = state[terms + 2 + 2 * WIN : terms + 2 + 2 * WIN + KC - 1]
            normed = rms_norm(stream, norm_first)
            queries = dot(normed, query_weight).astype(BF).reshape(LMAX, heads, FD)
            key_rows = dot(normed, key_weight).astype(BF).reshape(LMAX, heads, FD)
            values = dot(normed, value_weight).astype(BF)
            gating = dot(normed, filter_gate).astype(BF)
            extended = jnp.concatenate([tail, values], axis=0).astype(F32)
            convolved = sum(
                filter_taps[offset] * extended[KC - 1 - offset : KC - 1 - offset + LMAX]
                for offset in range(KC)
            )
            mixed = (convolved * jax.nn.silu(gating.astype(F32))).astype(BF)
            mixed = mixed.reshape(LMAX, heads, HS)
            scores = jnp.einsum("thf,shf->hts", queries, key_rows, preferred_element_type=F32)
            scores = scores * FD ** (-0.5)
            weights = jnp.where(causal, 1.0 + scores + 0.5 * scores * scores, 0.0)
            mapped = folded_features(queries)
            numerator = jnp.einsum(
                "hts,shd->thd", weights.astype(BF), mixed, preferred_element_type=F32
            ) + jnp.einsum(
                "htf,fhd->thd", mapped.astype(BF), state_sums, preferred_element_type=F32
            )
            denominator = jnp.sum(weights, axis=-1) + jnp.sum(
                mapped * jnp.transpose(state_norms).astype(F32)[:, None, :], axis=-1
            )
            linear_rows = (numerator / jnp.transpose(denominator)[..., None]).astype(BF)
            return dot(linear_rows.reshape(LMAX, width), linear_out).astype(BF)

        def window_part(request, stream):
            state = states[request]
            normed = rms_norm(stream, norm_second)
            queries = dot(normed, window_query).astype(BF).reshape(bands, WIN, heads, HS)
            key_rows = dot(normed, window_key).astype(BF)
            value_rows = dot(normed, window_value).astype(BF)
            start = terms + 2

            def paired(prefix, rows):
                blocks = jnp.concatenate([prefix, rows]).reshape(bands + 1, WIN, heads, HS)
                return jnp.concatenate([blocks[:-1], blocks[1:]], axis=1)

            key_pairs = paired(state[start : start + WIN], key_rows)
            value_pairs = paired(state[start + WIN : start + 2 * WIN], value_rows)
            logits = jnp.einsum(
                "bthd,bphd->bhtp", queries, key_pairs, preferred_element_type=F32
            ) * HS ** (-0.5)
            logits = jnp.where(allowed, logits, -jnp.inf)
            row_max = jnp.max(logits, axis=-1, keepdims=True)
            exponent = jnp.exp(logits - row_max)
            chances = (exponent / jnp.sum(exponent, axis=-1, keepdims=True)).astype(BF)
            attended = jnp.einsum(
                "bhtp,bphd->bthd", chances, value_pairs, preferred_element_type=F32
            ).astype(BF)
            final = (position == suffix_len[request] - 1).reshape(bands, 1, WIN)
            top = jnp.max(jnp.where(final, row_max[..., 0], -jnp.inf))
            return dot(attended.reshape(LMAX, width), window_out).astype(BF), top

        def hidden_part(stream):
            normed = rms_norm(stream, norm_third)
            inner = (jax.nn.silu(dot(normed, gate_weight)) * dot(normed, up_weight)).astype(BF)
            return dot(inner, down_weight).astype(BF)

        here = lax.axis_index("tensor")
        row_start = here * share_rows
        rows_here = row_start + jnp.arange(share_rows)
        outs, squares, tops = [], [], []
        for request in range(requests_here):
            stream = line_gather(hidden[request], "tensor", tensor_count)
            partial = linear_part(request, stream)
            stream = settle(partial, stream, "tensor", tensor_count)
            partial, top = window_part(request, stream)
            stream = settle(partial, stream, "tensor", tensor_count)
            partial = hidden_part(stream)
            total = line_scatter(partial, "tensor", tensor_count)
            mine = lax.dynamic_slice_in_dim(stream, row_start, share_rows, 0).astype(F32)
            mine = (mine + total).astype(BF)
            live = (rows_here < suffix_len[request])[:, None]
            outs.append(jnp.where(live, mine, jnp.zeros_like(mine)))
            floats = mine.astype(F32)
            squares.append(jnp.sum(jnp.where(live, floats * floats, 0.0)))
            tops.append(top)
        scalars = lax.all_gather(jnp.stack(squares + tops), "tensor")
        total = jnp.sum(scalars[:, :requests_here], axis=0)
        top_logit = jnp.max(scalars[:, requests_here:], axis=0)
        return jnp.stack(outs), jnp.sqrt(total / D), top_logit

    return per_device


def solution(mesh):
    return jax.shard_map(
        make(mesh.shape["req"], mesh.shape["tensor"]),
        mesh=mesh,
        in_specs=(
            P("req", "tensor", None),
            P("req"),
            P("req"),
            P(),
            P(),
            P(None, "tensor"),
            P(None, "tensor"),
            P(None, "tensor"),
            P(None, "tensor"),
            P(None, "tensor"),
            P("tensor", None),
            P(),
            P(None, "tensor"),
            P(None, "tensor"),
            P(None, "tensor"),
            P("tensor", None),
            P(),
            P(None, "tensor"),
            P(None, "tensor"),
            P("tensor", None),
            P("req", "tensor", None, None),
            P("req", "tensor", None),
            P("req", None, "tensor"),
            P("req", None, "tensor"),
            P("req", None, "tensor"),
        ),
        out_specs=(P("req", "tensor", None), P("req"), P("req")),
        check_vma=False,
    )
```

```python
import functools

import jax
import jax.numpy as jnp
import numpy as np
from jax import lax
from jax.experimental import pallas as pl
from jax.experimental.pallas import tpu as pltpu
from jax.sharding import PartitionSpec as P

D = 1792
FD = 16
HS = 112
WIN = 64
KC = 3
LMAX = 512
PAIRS = FD // 2 + 1
SQUARES = PAIRS * FD
FEATURES = 256
HEAD = 128
STATE_KEYS = 176
STATE_VALUES = STATE_KEYS + WIN
STATE_ROWS = STATE_VALUES + WIN

EPS = 1e-05
BF = jnp.bfloat16
F32 = jnp.float32
MIB = 1 << 20
ANY = pl.BlockSpec(memory_space=pl.ANY)
SMEM = pl.BlockSpec(memory_space=pltpu.SMEM)
VMEM = pl.BlockSpec(memory_space=pltpu.VMEM)


def rms_norm(rows, gain):
    floats = rows.astype(F32)
    inverse_rms = lax.rsqrt(jnp.mean(floats * floats, axis=-1, keepdims=True) + EPS)
    return (floats * inverse_rms * gain).astype(BF)


def dot(left, right):
    return jnp.dot(left, right, preferred_element_type=F32)


def dot_t(left, right):
    return lax.dot_general(left, right, (((1,), (1,)), ((), ())), preferred_element_type=F32)


def fold_matrix():
    fold = np.zeros((SQUARES + FD + 1, 1 + FD + FD * FD), np.float32)
    for shift in range(PAIRS):
        for i in range(FD):
            j = (i + shift) % FD
            fold[shift * FD + i, 1 + FD + i * FD + j] = 1.0
            if 0 < shift < FD // 2:
                fold[shift * FD + i, 1 + FD + j * FD + i] = 1.0
    for i in range(FD):
        fold[SQUARES + i, 1 + i] = 1.0
    fold[SQUARES + FD, 0] = 1.0
    return fold


def feature_maps(heads):
    left = np.zeros((heads, HEAD, FEATURES), np.float32)
    right = np.zeros((heads, HEAD, FEATURES), np.float32)
    plus = np.zeros((8, FEATURES), np.float32)
    for head in range(heads):
        for i in range(FD):
            for shift in range(PAIRS):
                left[head, head * FD + i, shift * FD + i] = 1.0
                right[head, head * FD + (i + shift) % FD, shift * FD + i] = 1.0
            left[head, head * FD + i, SQUARES + i] = 1.0
    plus[1, SQUARES : SQUARES + FD] = 1.0
    plus[0:2, SQUARES + FD] = 1.0
    plus[2, :SQUARES] = (2.0 * FD) ** (-0.5)
    plus[2, SQUARES : SQUARES + FD] = FD ** (-0.25)
    plus[2, SQUARES + FD] = 1.0
    return left, right, plus


def copies(plan, sems):
    made = []
    for number, (condition, source, target) in enumerate(plan):
        copy = pltpu.make_async_copy(source, target, sems.at[number])
        pl.when(condition)(copy.start)
        made.append((condition, copy))

    def wait():
        for condition, copy in made:
            pl.when(condition)(copy.wait)

    return wait


def half_pieces(segments):
    pieces = ([], [])
    buffer_row = 0
    for start, rows in segments:
        for half in range(2):
            pieces[half].append((start + half * rows // 2, rows // 2, buffer_row))
        buffer_row += rows // 2
    return pieces, buffer_row


def put_halves(segments, info, source, near, far, sems):
    pieces, _ = half_pieces(segments)
    plan = []
    for half in range(2):
        for natural, rows, at in pieces[half]:
            for low in (0, 1):
                target = near if half == 1 - low else far
                plan.append((info[1] == low, source.at[pl.ds(natural, rows)], target.at[pl.ds(at, rows)]))
    copies(plan, sems)()


def halves_plan(segments, info, own, own_out, other, other_out, target):
    pieces, _ = half_pieces(segments)
    plan = []
    for low in (0, 1):
        for middle in (0, 1):
            near, far = (own, other) if middle else (own_out, other_out)
            for half in range(2):
                source = near if half == 1 - low else far
                for natural, rows, at in pieces[half]:
                    plan.append(
                        (
                            (info[1] == low) & (info[2] == middle),
                            source.at[pl.ds(at, rows)],
                            target.at[pl.ds(natural, rows)],
                        )
                    )
    return plan


def lane_of_ones(shape):
    return (lax.broadcasted_iota(jnp.int32, shape, 1) & (HEAD - 1)) == HS


def linear_kernel(segments, shards, heads, prev, *refs):
    refs = list(refs)
    info, own, ups, downs = refs[0], refs[1], refs[2:5], refs[5:8]
    states = refs[8 : 8 + len(segments)]
    refs = refs[8 + len(segments) :]
    gain, taps, left, right, plus, weight, out_weight = refs[:7]
    refs = refs[7:]
    if prev:
        prev_key, prev_mixed, prev_value = refs[:3]
        refs = refs[3:]
    refs = refs[1:]
    near, far, stay, key_out, mixed_out, value_out = refs[:6]
    x, w, ow, q, k, m, y, sems, wsems = refs[6:]
    width = heads * HEAD
    total = x.shape[0]
    plan = []
    for segment, shard, row, rows in shards:
        for here in range(4):
            source = own if here == shard else (ups[here - shard - 1] if here > shard else downs[shard - here - 1])
            plan.append(
                (
                    info[0] == here,
                    source.at[info[4 + segment], pl.ds(0, rows)],
                    x.at[pl.ds(row, rows)],
                )
            )
    wait_x = copies(plan, sems)
    weight_copy = pltpu.make_async_copy(weight, w, wsems.at[0])
    out_copy = pltpu.make_async_copy(out_weight, ow, wsems.at[1])
    weight_copy.start()
    out_copy.start()
    if prev:
        k[pl.ds(0, prev), :] = prev_key[...]
        m[pl.ds(0, prev), :] = prev_mixed[...]
    wait_x()
    weight_copy.wait()
    tap = taps[...]
    for number, (start, rows) in enumerate(segments):
        base = prev if number == 0 else 0
        tile = min(rows, 256)
        if base:
            ends = prev_value[...].astype(F32)
            last2, last = ends[14:15], ends[15:16]
        else:
            ends = states[number][pl.ds(SQUARES + FD, 16), :].astype(F32)
            last2, last = ends[1:2], ends[2:3]
        for at in range(start, start + rows, tile):
            normed = rms_norm(x[pl.ds(at, tile), :], gain[...])
            q[pl.ds(at, tile), :] = dot(normed, w[:, :HEAD]).astype(BF)
            k[pl.ds(prev + at, tile), :] = dot(normed, w[:, HEAD : 2 * HEAD]).astype(BF)
            v = dot(normed, w[:, 2 * HEAD : 2 * HEAD + width]).astype(BF).astype(F32)
            u = dot(normed, w[:, 2 * HEAD + width :]).astype(BF).astype(F32)
            row = lax.broadcasted_iota(jnp.int32, v.shape, 0)
            back1 = jnp.where(row == 0, last, pltpu.roll(v, 1, 0))
            back2 = jnp.where(row == 0, last2, jnp.where(row == 1, last, pltpu.roll(v, 2, 0)))
            last2, last = v[tile - 2 : tile - 1], v[tile - 1 : tile]
            convolved = tap[0:1] * v + tap[1:2] * back1 + tap[2:3] * back2
            mixed = convolved * (u / (1.0 + jnp.exp(-u)))
            m[pl.ds(prev + at, tile), :] = jnp.where(lane_of_ones(v.shape), 1.0, mixed).astype(BF)
            if number == 0 and at + tile == start + rows:
                value_out[...] = v[tile - 16 :].astype(BF)
    out_copy.wait()
    for number, (start, rows) in enumerate(segments):
        base = prev if number == 0 else 0
        tile = min(rows, 256)
        first = 0 if number == 0 else prev + start
        for at in range(start, start + rows, tile):
            queries = q[pl.ds(at, tile), :]
            lane = lax.broadcasted_iota(jnp.int32, queries.shape, 1)
            for head in range(heads):
                columns = pl.ds(head * HEAD, HEAD)
                mapped = (
                    (dot(queries, left[head]) + plus[0:1, :])
                    * (dot(queries, right[head]) + plus[1:2, :])
                    * plus[2:3, :]
                )
                total_rows = dot(mapped.astype(BF), states[number][pl.ds(0, FEATURES), columns])
                own_lanes = (lane >= head * FD) & (lane < (head + 1) * FD)
                masked = jnp.where(own_lanes, queries, jnp.zeros_like(queries))
                for key_at in range(first, prev + at + tile, tile):
                    a = dot_t(masked, k[pl.ds(key_at, tile), :]) * FD ** (-0.5)
                    weights = 1.0 + a + 0.5 * a * a
                    if key_at == prev + at:
                        causal = lax.broadcasted_iota(jnp.int32, a.shape, 0) >= lax.broadcasted_iota(
                            jnp.int32, a.shape, 1
                        )
                        weights = jnp.where(causal, weights, 0.0)
                    total_rows += dot(weights.astype(BF), m[pl.ds(key_at, tile), columns])
                y[pl.ds(at, tile), columns] = (total_rows / total_rows[:, HS : HS + 1]).astype(BF)
    key_out[...] = k[pl.ds(prev, key_out.shape[0]), :]
    mixed_out[...] = m[pl.ds(prev, mixed_out.shape[0]), :]
    pieces, _ = half_pieces(segments)
    plan = []
    for low in (0, 1):
        for natural, rows, at in pieces[1 - low]:
            plan.append((info[1] == low, x.at[pl.ds(natural, rows)], stay.at[pl.ds(at, rows)]))
    copies(plan, sems)()
    for start, rows in segments:
        tile = min(rows, 256)
        for at in range(start, start + rows, tile):
            x[pl.ds(at, tile), :] = dot(y[pl.ds(at, tile), :], ow[...]).astype(BF)
    put_halves(segments, info, x, near, far, sems)


def window_kernel(segments, heads, prev, *refs):
    refs = list(refs)
    info, own, own_out, other, other_out = refs[:5]
    states = refs[5 : 5 + len(segments)]
    refs = refs[5 + len(segments) :]
    gain, weight, out_weight = refs[:3]
    refs = refs[3:]
    if prev:
        prev_keys, prev_values = refs[:2]
        refs = refs[2:]
    refs = refs[1:]
    near, far, top, key_out, value_out = refs[:5]
    x, w, ow, q, k, v, y, sems, wsems = refs[5:]
    width = heads * HEAD
    wait_x = copies(halves_plan(segments, info, own, own_out, other, other_out, x), sems)
    weight_copy = pltpu.make_async_copy(weight, w, wsems.at[0])
    out_copy = pltpu.make_async_copy(out_weight, ow, wsems.at[1])
    weight_copy.start()
    out_copy.start()
    wait_x()
    weight_copy.wait()
    best = []
    for number, (start, rows) in enumerate(segments):
        shift = WIN * (number + 1)
        if prev and number == 0:
            k[pl.ds(0, WIN), :] = prev_keys[...]
            v[pl.ds(0, WIN), :] = prev_values[...]
        else:
            old = states[number][pl.ds(STATE_VALUES, WIN), :]
            k[pl.ds(start + shift - WIN, WIN), :] = states[number][pl.ds(STATE_KEYS, WIN), :]
            v[pl.ds(start + shift - WIN, WIN), :] = jnp.where(
                lane_of_ones(old.shape), jnp.ones_like(old), old
            )
        tile = min(rows, 256)
        for at in range(start, start + rows, tile):
            normed = rms_norm(x[pl.ds(at, tile), :], gain[...])
            q[pl.ds(at, tile), :] = dot(normed, w[:, :width]).astype(BF)
            k[pl.ds(shift + at, tile), :] = dot(normed, w[:, width : 2 * width]).astype(BF)
            values = dot(normed, w[:, 2 * width :])
            v[pl.ds(shift + at, tile), :] = jnp.where(lane_of_ones(values.shape), 1.0, values).astype(BF)
        final = info[6 + number] - 1
        tile = min(rows, 128)
        best_here = jnp.full((1, 1), -jnp.inf, F32)
        for at in range(start, start + rows, tile):
            keys_here = tile + WIN
            row = lax.broadcasted_iota(jnp.int32, (tile, keys_here), 0)
            place = lax.broadcasted_iota(jnp.int32, (tile, keys_here), 1)
            allowed = (place > row) & (place <= row + WIN)
            for head in range(heads):
                columns = pl.ds(head * HEAD, HEAD)
                e = dot_t(q[pl.ds(at, tile), columns], k[pl.ds(shift - WIN + at, keys_here), columns])
                e = jnp.where(allowed, e * HS ** (-0.5), -jnp.inf)
                row_max = jnp.max(e, axis=-1, keepdims=True)
                chances = jnp.exp(e - row_max).astype(BF)
                o = dot(chances, v[pl.ds(shift - WIN + at, keys_here), columns])
                y[pl.ds(at, tile), columns] = (o / o[:, HS : HS + 1]).astype(BF)
                at_final = lax.broadcasted_iota(jnp.int32, row_max.shape, 0) + (at - start) == final
                best_here = jnp.maximum(
                    best_here, jnp.max(jnp.where(at_final, row_max, -jnp.inf), axis=0, keepdims=True)
                )
        best.append(best_here)
    end = segments[0][1]
    key_out[...] = k[pl.ds(end, WIN), :]
    value_out[...] = v[pl.ds(end, WIN), :]
    for number in range(len(segments)):
        top[pl.ds(number * 8, 8), :] = jnp.broadcast_to(best[number], (8, 128))
    out_copy.wait()
    for start, rows in segments:
        tile = min(rows, 256)
        for at in range(start, start + rows, tile):
            x[pl.ds(at, tile), :] = dot(y[pl.ds(at, tile), :], ow[...]).astype(BF)
    put_halves(segments, info, x, near, far, sems)


def hidden_kernel(segments, info, own, own_out, other, other_out, gain, gate, up, down, dep, near, far, x, n, total, sems):
    step = pl.program_id(0)
    rows = x.shape[0]
    tile = rows if rows < 512 else rows // 2

    @pl.when(step == 0)
    def _():
        copies(halves_plan(segments, info, own, own_out, other, other_out, x), sems)()
        for at in range(0, rows, tile):
            n[pl.ds(at, tile), :] = rms_norm(x[pl.ds(at, tile), :], gain[...])

    for at in range(0, rows, tile):
        normed = n[pl.ds(at, tile), :]
        opened = dot(normed, gate[...])
        inner = (opened / (1.0 + jnp.exp(-opened)) * dot(normed, up[...])).astype(BF)
        part = dot(inner, down[...])

        @pl.when(step == 0)
        def _(at=at, part=part):
            total[pl.ds(at, tile), :] = part

        @pl.when(step > 0)
        def _(at=at, part=part):
            total[pl.ds(at, tile), :] += part

    @pl.when(step == pl.num_programs(0) - 1)
    def _():
        for at in range(0, rows, tile):
            x[pl.ds(at, tile), :] = total[pl.ds(at, tile), :].astype(BF)
        put_halves(segments, info, x, near, far, sems)


def call(body, outs, specs, scratch, operands, flops, moved, limit, grid=None):
    return pl.pallas_call(
        body,
        grid=grid or (),
        out_shape=[jax.ShapeDtypeStruct(shape, dtype) for shape, dtype, _ in outs],
        in_specs=specs,
        out_specs=[spec for _, _, spec in outs],
        scratch_shapes=scratch,
        compiler_params=pltpu.CompilerParams(vmem_limit_bytes=limit * MIB),
        cost_estimate=pl.CostEstimate(flops=flops, bytes_accessed=moved, transcendentals=0),
    )(*operands)


def run_linear(segments, shards, heads, prev, info, own, ups, downs, states, consts, weights, before, dep):
    total = sum(rows for _, rows in segments)
    width = heads * HEAD
    gain, taps, weight, out_weight = weights
    half = (total // 2, D)
    scratch = [
        pltpu.VMEM((total, D), BF),
        pltpu.VMEM(weight.shape, BF),
        pltpu.VMEM(out_weight.shape, BF),
        pltpu.VMEM((total, HEAD), BF),
        pltpu.VMEM((prev + total, HEAD), BF),
        pltpu.VMEM((prev + total, width), BF),
        pltpu.VMEM((total, width), BF),
        pltpu.SemaphoreType.DMA((20,)),
        pltpu.SemaphoreType.DMA((2,)),
    ]
    rows = segments[0][1]
    outs = [(half, BF, ANY)] * 3 + [((rows, HEAD), BF, VMEM), ((rows, width), BF, VMEM), ((16, width), BF, VMEM)]
    operands = [info, own, *ups, *downs, *states, gain, taps, *consts, weight, out_weight, *before, dep]
    specs = [SMEM] + [ANY] * 7 + [VMEM] * (len(states) + 2 + 3) + [ANY] * 2 + [VMEM] * len(before) + [ANY]
    return call(
        functools.partial(linear_kernel, segments, shards, heads, prev),
        outs, specs, scratch, operands, 2 * total * D * 1792, 12 * MIB, 40,
    )


def run_window(segments, heads, prev, info, parts, states, weights, before, dep):
    total = sum(rows for _, rows in segments)
    width = heads * HEAD
    gain, weight, out_weight = weights
    half = (total // 2, D)
    scratch = [
        pltpu.VMEM((total, D), BF),
        pltpu.VMEM(weight.shape, BF),
        pltpu.VMEM(out_weight.shape, BF),
        pltpu.VMEM((total, width), BF),
        pltpu.VMEM((total + WIN * len(segments), width), BF),
        pltpu.VMEM((total + WIN * len(segments), width), BF),
        pltpu.VMEM((total, width), BF),
        pltpu.SemaphoreType.DMA((20,)),
        pltpu.SemaphoreType.DMA((2,)),
    ]
    outs = [(half, BF, ANY)] * 2 + [((8 * len(segments), 128), F32, VMEM)] + [((WIN, width), BF, VMEM)] * 2
    operands = [info, *parts, *states, gain, weight, out_weight, *before, dep]
    specs = [SMEM] + [ANY] * 4 + [VMEM] * (len(states) + 1) + [ANY] * 2 + [VMEM] * len(before) + [ANY]
    return call(
        functools.partial(window_kernel, segments, heads, prev),
        outs, specs, scratch, operands, 2 * total * D * 2048, 12 * MIB, 40,
    )


def run_hidden(segments, info, parts, weights, dep):
    total = sum(rows for _, rows in segments)
    gain, gate, up, down = weights
    half = (total // 2, D)
    units = gate.shape[1]
    block = 256
    specs = [SMEM] + [ANY] * 4 + [
        pl.BlockSpec((1, D), lambda i: (0, 0)),
        pl.BlockSpec((D, block), lambda i: (0, i)),
        pl.BlockSpec((D, block), lambda i: (0, i)),
        pl.BlockSpec((block, D), lambda i: (i, 0)),
        ANY,
    ]
    scratch = [
        pltpu.VMEM((total, D), BF),
        pltpu.VMEM((total, D), BF),
        pltpu.VMEM((total, D), F32),
        pltpu.SemaphoreType.DMA((20,)),
    ]
    return call(
        functools.partial(hidden_kernel, segments),
        [(half, BF, ANY)] * 2, specs, scratch, [info, *parts, gain, gate, up, down, dep],
        2 * total * D * units * 3, 24 * MIB, 40, (units // block,),
    )


INWARD, ACROSS, OUTWARD = [(0, 1), (3, 2)], [(1, 2), (2, 1)], [(1, 0), (2, 3)]


def to_middle(near, far, stay):
    far_in = lax.ppermute(far, "tensor", INWARD)
    near_in = lax.ppermute(near, "tensor", INWARD)
    crossed = lax.ppermute(far + far_in, "tensor", ACROSS)
    return (stay.astype(F32) + (near.astype(F32) + near_in.astype(F32) + crossed.astype(F32))).astype(BF)


def from_middle(own):
    other = lax.ppermute(own, "tensor", ACROSS)
    own_out = lax.ppermute(own, "tensor", OUTWARD)
    other_out = lax.ppermute(other, "tensor", OUTWARD)
    return own, own_out, other, other_out


def pick_axis(array, axis, index):
    return jnp.where(index, lax.index_in_dim(array, 1, axis, False), lax.index_in_dim(array, 0, axis, False))


def slot_states(request_group, group_slot, sums, norms, keys, values, tail, count):
    here = lax.axis_index("req")
    slots_here, heads = sums.shape[:2]
    width = heads * HEAD
    requests = request_group.shape[0]
    groups = lax.all_gather(request_group, "req", axis=0, tiled=True)
    matches = jnp.arange(group_slot.shape[0])[None, :] == groups[:, None]
    slots = jnp.sum(jnp.where(matches, group_slot[None, :], 0), axis=1)

    def padded(rows):
        rows = rows.reshape(slots_here, rows.shape[1], heads, HS)
        return jnp.pad(rows, ((0, 0), (0, 0), (0, 0), (0, HEAD - HS))).reshape(slots_here, -1, width)

    fold = jnp.asarray(fold_matrix())
    folded = jnp.einsum("fg,ahgd->afhd", fold, sums, precision=lax.Precision.HIGHEST)
    folded_norms = jnp.einsum("fg,ahg->afh", fold, norms, precision=lax.Precision.HIGHEST)
    folded = jnp.concatenate([folded, folded_norms[..., None]], axis=-1).astype(BF)
    folded = jnp.pad(folded, ((0, 0), (0, 0), (0, 0), (0, HEAD - HS - 1))).reshape(slots_here, -1, width)
    gap = jnp.zeros((slots_here, STATE_KEYS - SQUARES - FD - 1 - (KC - 1), width), BF)
    pack = jnp.concatenate([folded, padded(tail), gap, padded(keys), padded(values)], axis=1)

    bits = []
    while 1 << len(bits) < count:
        bits.append(len(bits))
    local = (slots - here * slots_here).reshape((2,) * len(bits) + (requests,))

    def chosen(places):
        flat = places.reshape(-1)
        owned = (flat >= 0) & (flat < slots_here)
        rows = jnp.take(pack, jnp.clip(flat, 0, slots_here - 1), axis=0)
        rows = jnp.where(owned[:, None, None], rows, jnp.zeros_like(rows))
        return rows.reshape(places.shape + rows.shape[1:])

    def swap(array, bit):
        return lax.ppermute(array, "req", [(i, i ^ (1 << bit)) for i in range(count)])

    def upper(bit):
        return (here >> bit) & 1 == 1

    axis = len(bits) - 1
    packs = chosen(pick_axis(local, axis, upper(0))) + swap(chosen(pick_axis(local, axis, ~upper(0))), 0)
    halves = []
    cut = STATE_ROWS // 2
    for number in range(2):
        part = packs[..., number * cut : (number + 1) * cut, :]
        left = bits[1:]
        order = left if number == 0 else left[::-1]
        while order:
            bit, order = order[0], order[1:]
            axis = len(left) - 1 - left.index(bit)
            left = [b for b in left if b != bit]
            part = pick_axis(part, axis, upper(bit)) + swap(pick_axis(part, axis, ~upper(bit)), bit)
        halves.append(part)
    return jnp.concatenate(halves, axis=1)


def make_line(req_count):
    def per_device(
        hidden,
        suffix_len,
        request_group,
        group_slot,
        norm_first,
        query_weight,
        key_weight,
        value_weight,
        filter_gate,
        filter_taps,
        linear_out,
        norm_second,
        window_query,
        window_key,
        window_value,
        window_out,
        norm_third,
        gate_weight,
        up_weight,
        down_weight,
        prefix_sums,
        prefix_norms,
        prefix_keys,
        prefix_values,
        prefix_tail,
    ):
        requests = hidden.shape[0]
        heads = prefix_sums.shape[1]
        share = hidden.shape[1]
        here = lax.axis_index("tensor")
        low = here < 2
        middle = (here == 1) | (here == 2)

        ups, downs = [], []
        up = down = hidden
        for step in range(1, 4):
            up = lax.ppermute(up, "tensor", [(i, i + 1) for i in range(step - 1, 3)])
            down = lax.ppermute(down, "tensor", [(i + 1, i) for i in range(4 - step)])
            ups.append(up)
            downs.append(down)
        states = slot_states(
            request_group, group_slot, prefix_sums, prefix_norms, prefix_keys, prefix_values, prefix_tail, req_count
        )

        def wide(matrix):
            matrix = matrix.reshape(matrix.shape[0], heads, HS)
            return jnp.pad(matrix, ((0, 0), (0, 0), (0, HEAD - HS))).reshape(matrix.shape[0], heads * HEAD)

        def tall(matrix):
            matrix = matrix.reshape(heads, HS, matrix.shape[1])
            return jnp.pad(matrix, ((0, 0), (0, HEAD - HS), (0, 0))).reshape(heads * HEAD, -1)

        def lanes(matrix):
            return jnp.pad(matrix, ((0, 0), (0, HEAD - matrix.shape[1])))

        linear_weights = (
            norm_first[None],
            jnp.pad(wide(filter_taps), ((0, 8 - KC), (0, 0))),
            jnp.concatenate(
                [lanes(query_weight), lanes(key_weight), wide(value_weight), wide(filter_gate)], axis=1
            ),
            tall(linear_out),
        )
        window_weights = (
            norm_second[None],
            jnp.concatenate([wide(window_query), wide(window_key), wide(window_value)], axis=1),
            tall(window_out),
        )
        hidden_weights = (norm_third[None], gate_weight, up_weight, down_weight)
        left, right, plus = feature_maps(heads)
        consts = (jnp.asarray(left, BF), jnp.asarray(right, BF), jnp.asarray(plus))

        place = [here, low.astype(jnp.int32), middle.astype(jnp.int32), here * 0]
        segments = ((0, LMAX),)
        shards = tuple((0, s, s * share, share) for s in range(4))
        infos, own, parts, tops = [], [], [], []
        for request in range(requests):
            infos.append(
                jnp.stack(place + [here * 0 + request, here * 0, suffix_len[request], here * 0]).astype(jnp.int32)
            )
        dep = hidden
        for request in range(requests):
            near, far, stay, *_ = run_linear(
                segments, shards, heads, 0, infos[request], hidden, ups, downs,
                [states[request]], consts, linear_weights, [], dep,
            )
            own.append(to_middle(near, far, stay))
            dep = own[-1]
        for request in range(requests):
            parts.append(from_middle(own[request]))
        for request in range(requests):
            near, far, top, *_ = run_window(
                segments, heads, 0, infos[request], parts[request], [states[request]], window_weights, [], dep
            )
            own[request] = to_middle(near, far, own[request])
            dep = own[request]
            tops.append(top[0, 0])
        for request in range(requests):
            parts[request] = from_middle(own[request])
        for request in range(requests):
            near, far = run_hidden(segments, infos[request], parts[request], hidden_weights, dep)
            own[request] = to_middle(near, far, own[request])
            dep = own[request]
        outs, squares = [], []
        rows_here = here * share + jnp.arange(share)
        for request in range(requests):
            first, second = own[request][:share], own[request][share:]
            moved = lax.ppermute(jnp.where(low, first, second), "tensor", OUTWARD)
            mine = jnp.where(middle, jnp.where(low, second, first), moved)
            live = (rows_here < suffix_len[request])[:, None]
            outs.append(jnp.where(live, mine, jnp.zeros_like(mine)))
            floats = mine.astype(F32)
            squares.append(jnp.sum(jnp.where(live, floats * floats, 0.0)))
        scalars = jnp.stack(squares + tops)
        scalars = jnp.broadcast_to(scalars[:, None], (2 * requests, 128))
        everyone = [scalars] + [
            lax.ppermute(scalars, "tensor", [(i, (i + step) % 4) for i in range(4)]) for step in (1, 2, 3)
        ]
        total = sum(each[:requests, 0] for each in everyone)
        top_logit = functools.reduce(jnp.maximum, [each[requests:, 0] for each in everyone])
        return jnp.stack(outs), jnp.sqrt(total / D), top_logit

    return per_device


def folded_features(queries):
    floats = jnp.transpose(queries.astype(F32), (1, 0, 2))
    parts = [jnp.ones(floats.shape[:-1] + (1,), F32), floats * FD ** (-0.25)]
    for shift in range(PAIRS):
        parts.append(floats * jnp.roll(floats, -shift, axis=-1) * (2.0 * FD) ** (-0.5))
    return jnp.concatenate(parts, axis=-1)


def plain_fold_matrix():
    row = jnp.arange(1 + FD + PAIRS * FD)[:, None]
    column = jnp.arange(1 + FD + FD * FD)[None, :]
    shift, first = (row - 1 - FD) // FD, (row - 1 - FD) % FD
    second = (first + shift) % FD
    major, minor = (column - 1 - FD) // FD, (column - 1 - FD) % FD
    straight = (major == first) & (minor == second)
    swapped = (major == second) & (minor == first) & (shift > 0) & (shift < FD // 2)
    squares = (row > FD) & (column > FD) & (straight | swapped)
    return jnp.where((row == column) & (row <= FD) | squares, 1.0, 0.0).astype(F32)


def line_gather(rows, axis, count):
    here = lax.axis_index(axis)
    size = rows.shape[0]
    up = down = rows
    ups, downs = [], []
    for step in range(1, count):
        up = lax.ppermute(up, axis, [(i, i + 1) for i in range(step - 1, count - 1)])
        down = lax.ppermute(down, axis, [(i + 1, i) for i in range(count - step)])
        ups.append(up)
        downs.append(down)
    around = jnp.concatenate(ups[::-1] + [rows] + downs)
    return lax.dynamic_slice_in_dim(around, (count - 1 - here) * size, count * size, 0)


def line_scatter(partial, axis, count):
    here = lax.axis_index(axis)
    size = partial.shape[0] // count

    def block(index):
        return lax.dynamic_slice_in_dim(partial, index * size, size, 0)

    up = down = None
    for step in range(1, count):
        to_up = block(jnp.minimum(here + count - step, count - 1))
        to_down = block(jnp.maximum(here - count + step, 0))
        if up is not None:
            to_up, to_down = to_up + up, to_down + down
        up = lax.ppermute(to_up, axis, [(i, i + 1) for i in range(step)])
        down = lax.ppermute(to_down, axis, [(i + 1, i) for i in range(count - 1 - step, count - 1)])
    return block(here).astype(F32) + up.astype(F32) + down.astype(F32)


def settle(partial, stream, axis, count):
    here = lax.axis_index(axis)
    size = partial.shape[0] // count
    mine = lax.dynamic_slice_in_dim(stream, here * size, size, 0)
    total = line_scatter(partial, axis, count)
    return line_gather((mine.astype(F32) + total).astype(BF), axis, count)


def bring_home(packs, axis, count):
    here = lax.axis_index(axis)
    bit = 1
    while bit < count:
        pairs = packs.reshape((packs.shape[0] // 2, 2) + packs.shape[1:])
        upper = (here & bit) != 0
        keep = jnp.where(upper, pairs[:, 1], pairs[:, 0])
        send = jnp.where(upper, pairs[:, 0], pairs[:, 1])
        packs = keep + lax.ppermute(send, axis, [(i, i ^ bit) for i in range(count)])
        bit *= 2
    return packs[0]


def make_plain(req_count, tensor_count):
    def per_device(
        hidden,
        suffix_len,
        request_group,
        group_slot,
        norm_first,
        query_weight,
        key_weight,
        value_weight,
        filter_gate,
        filter_taps,
        linear_out,
        norm_second,
        window_query,
        window_key,
        window_value,
        window_out,
        norm_third,
        gate_weight,
        up_weight,
        down_weight,
        prefix_sums,
        prefix_norms,
        prefix_keys,
        prefix_values,
        prefix_tail,
    ):
        requests_here = hidden.shape[0]
        share_rows = hidden.shape[1]
        slots_here, heads = prefix_sums.shape[:2]
        width = heads * HS

        groups = lax.all_gather(request_group, "req", axis=0, tiled=True)
        matches = jnp.arange(group_slot.shape[0])[None, :] == groups[:, None]
        slots = jnp.sum(jnp.where(matches, group_slot[None, :], 0), axis=1)
        fold = plain_fold_matrix()
        sums = jnp.einsum("fg,ahgd->afhd", fold, prefix_sums, precision=lax.Precision.HIGHEST)
        terms = sums.shape[1]
        norms = jnp.einsum("fg,ahg->afh", fold, prefix_norms, precision=lax.Precision.HIGHEST)
        norms = jnp.pad(norms.reshape(slots_here, -1), ((0, 0), (0, 2 * width - terms * heads)))
        pack = jnp.concatenate(
            [
                sums.reshape(slots_here, terms, width).astype(BF),
                norms.reshape(slots_here, 2, width).astype(BF),
                prefix_keys,
                prefix_values,
                prefix_tail,
            ],
            axis=1,
        )
        rows = pack.shape[1]
        pack = jnp.pad(pack, ((0, 0), (0, -rows % 32), (0, 0)))
        half = pack.shape[1] // 2
        pack = jnp.concatenate([pack[:, :half], pack[:, half:]], axis=2)
        local = slots - lax.axis_index("req") * slots_here
        owned = (local >= 0) & (local < slots_here)
        sent = jnp.take(pack, jnp.clip(local, 0, slots_here - 1), axis=0)
        sent = jnp.where(owned[:, None, None], sent, jnp.zeros_like(sent))
        sent = sent.reshape((req_count, requests_here) + sent.shape[1:])
        states = bring_home(sent, "req", req_count)
        states = jnp.concatenate([states[:, :, :width], states[:, :, width:]], axis=1)

        position = jnp.arange(LMAX)
        causal = position[:, None] >= position[None, :]
        bands = LMAX // WIN
        band_row = jnp.arange(WIN)[:, None]
        band_key = jnp.arange(2 * WIN)[None, :]
        allowed = (band_key > band_row) & (band_key <= band_row + WIN)

        def linear_part(request, stream):
            state = states[request]
            state_sums = state[:terms].reshape(terms, heads, HS)
            state_norms = state[terms : terms + 2].reshape(-1)[: terms * heads].reshape(terms, heads)
            tail = state[terms + 2 + 2 * WIN : terms + 2 + 2 * WIN + KC - 1]
            normed = rms_norm(stream, norm_first)
            queries = dot(normed, query_weight).astype(BF).reshape(LMAX, heads, FD)
            key_rows = dot(normed, key_weight).astype(BF).reshape(LMAX, heads, FD)
            values = dot(normed, value_weight).astype(BF)
            gating = dot(normed, filter_gate).astype(BF)
            extended = jnp.concatenate([tail, values], axis=0).astype(F32)
            convolved = sum(
                filter_taps[offset] * extended[KC - 1 - offset : KC - 1 - offset + LMAX]
                for offset in range(KC)
            )
            mixed = (convolved * jax.nn.silu(gating.astype(F32))).astype(BF)
            mixed = mixed.reshape(LMAX, heads, HS)
            scores = jnp.einsum("thf,shf->hts", queries, key_rows, preferred_element_type=F32)
            scores = scores * FD ** (-0.5)
            weights = jnp.where(causal, 1.0 + scores + 0.5 * scores * scores, 0.0)
            mapped = folded_features(queries)
            numerator = jnp.einsum(
                "hts,shd->thd", weights.astype(BF), mixed, preferred_element_type=F32
            ) + jnp.einsum(
                "htf,fhd->thd", mapped.astype(BF), state_sums, preferred_element_type=F32
            )
            denominator = jnp.sum(weights, axis=-1) + jnp.sum(
                mapped * jnp.transpose(state_norms).astype(F32)[:, None, :], axis=-1
            )
            linear_rows = (numerator / jnp.transpose(denominator)[..., None]).astype(BF)
            return dot(linear_rows.reshape(LMAX, width), linear_out).astype(BF)

        def window_part(request, stream):
            state = states[request]
            normed = rms_norm(stream, norm_second)
            queries = dot(normed, window_query).astype(BF).reshape(bands, WIN, heads, HS)
            key_rows = dot(normed, window_key).astype(BF)
            value_rows = dot(normed, window_value).astype(BF)
            start = terms + 2

            def paired(prefix, rows):
                blocks = jnp.concatenate([prefix, rows]).reshape(bands + 1, WIN, heads, HS)
                return jnp.concatenate([blocks[:-1], blocks[1:]], axis=1)

            key_pairs = paired(state[start : start + WIN], key_rows)
            value_pairs = paired(state[start + WIN : start + 2 * WIN], value_rows)
            logits = jnp.einsum(
                "bthd,bphd->bhtp", queries, key_pairs, preferred_element_type=F32
            ) * HS ** (-0.5)
            logits = jnp.where(allowed, logits, -jnp.inf)
            row_max = jnp.max(logits, axis=-1, keepdims=True)
            exponent = jnp.exp(logits - row_max)
            chances = (exponent / jnp.sum(exponent, axis=-1, keepdims=True)).astype(BF)
            attended = jnp.einsum(
                "bhtp,bphd->bthd", chances, value_pairs, preferred_element_type=F32
            ).astype(BF)
            final = (position == suffix_len[request] - 1).reshape(bands, 1, WIN)
            top = jnp.max(jnp.where(final, row_max[..., 0], -jnp.inf))
            return dot(attended.reshape(LMAX, width), window_out).astype(BF), top

        def hidden_part(stream):
            normed = rms_norm(stream, norm_third)
            inner = (jax.nn.silu(dot(normed, gate_weight)) * dot(normed, up_weight)).astype(BF)
            return dot(inner, down_weight).astype(BF)

        here = lax.axis_index("tensor")
        row_start = here * share_rows
        rows_here = row_start + jnp.arange(share_rows)
        outs, squares, tops = [], [], []
        for request in range(requests_here):
            stream = line_gather(hidden[request], "tensor", tensor_count)
            partial = linear_part(request, stream)
            stream = settle(partial, stream, "tensor", tensor_count)
            partial, top = window_part(request, stream)
            stream = settle(partial, stream, "tensor", tensor_count)
            partial = hidden_part(stream)
            total = line_scatter(partial, "tensor", tensor_count)
            mine = lax.dynamic_slice_in_dim(stream, row_start, share_rows, 0).astype(F32)
            mine = (mine + total).astype(BF)
            live = (rows_here < suffix_len[request])[:, None]
            outs.append(jnp.where(live, mine, jnp.zeros_like(mine)))
            floats = mine.astype(F32)
            squares.append(jnp.sum(jnp.where(live, floats * floats, 0.0)))
            tops.append(top)
        scalars = lax.all_gather(jnp.stack(squares + tops), "tensor")
        total = jnp.sum(scalars[:, :requests_here], axis=0)
        top_logit = jnp.max(scalars[:, requests_here:], axis=0)
        return jnp.stack(outs), jnp.sqrt(total / D), top_logit

    return per_device


def solution(mesh):
    return jax.shard_map(
        make_line(mesh.shape["req"]) if mesh.shape["tensor"] == 4 else make_plain(mesh.shape["req"], mesh.shape["tensor"]),
        mesh=mesh,
        in_specs=(
            P("req", "tensor", None),
            P("req"),
            P("req"),
            P(),
            P(),
            P(None, "tensor"),
            P(None, "tensor"),
            P(None, "tensor"),
            P(None, "tensor"),
            P(None, "tensor"),
            P("tensor", None),
            P(),
            P(None, "tensor"),
            P(None, "tensor"),
            P(None, "tensor"),
            P("tensor", None),
            P(),
            P(None, "tensor"),
            P(None, "tensor"),
            P("tensor", None),
            P("req", "tensor", None, None),
            P("req", "tensor", None),
            P("req", None, "tensor"),
            P("req", None, "tensor"),
            P("req", None, "tensor"),
        ),
        out_specs=(P("req", "tensor", None), P("req"), P("req")),
        check_vma=False,
    )
```

```python
import functools

import jax
import jax.numpy as jnp
import numpy as np
from jax import lax
from jax.experimental import pallas as pl
from jax.experimental.pallas import tpu as pltpu
from jax.sharding import PartitionSpec as P

D = 1792
FD = 16
HS = 112
WIN = 64
KC = 3
LMAX = 512
SHORT = 32
PAIRS = FD // 2 + 1
SQUARES = PAIRS * FD
FEATURES = 256
HEAD = 128
STATE_KEYS = 176
STATE_VALUES = STATE_KEYS + WIN
STATE_ROWS = STATE_VALUES + WIN

EPS = 1e-05
BF = jnp.bfloat16
F32 = jnp.float32
MIB = 1 << 20
ANY = pl.BlockSpec(memory_space=pl.ANY)
SMEM = pl.BlockSpec(memory_space=pltpu.SMEM)
VMEM = pl.BlockSpec(memory_space=pltpu.VMEM)
HBM = pl.BlockSpec(memory_space=pltpu.HBM)


def rms_norm(rows, gain):
    floats = rows.astype(F32)
    inverse_rms = lax.rsqrt(jnp.mean(floats * floats, axis=-1, keepdims=True) + EPS)
    return (floats * inverse_rms * gain).astype(BF)


def dot(left, right):
    return jnp.dot(left, right, preferred_element_type=F32)


def dot_t(left, right):
    return lax.dot_general(left, right, (((1,), (1,)), ((), ())), preferred_element_type=F32)


def fold_matrix():
    fold = np.zeros((STATE_KEYS, 1 + FD + FD * FD), np.float32)
    for shift in range(PAIRS):
        for i in range(FD):
            j = (i + shift) % FD
            fold[shift * FD + i, 1 + FD + i * FD + j] = 1.0
            if 0 < shift < FD // 2:
                fold[shift * FD + i, 1 + FD + j * FD + i] = 1.0
    for i in range(FD):
        fold[SQUARES + i, 1 + i] = 1.0
    fold[SQUARES + FD, 0] = 1.0
    return fold


def feature_maps(heads):
    left = np.zeros((heads, HEAD, FEATURES), np.float32)
    right = np.zeros((heads, HEAD, FEATURES), np.float32)
    plus = np.zeros((8, FEATURES), np.float32)
    for head in range(heads):
        for i in range(FD):
            for shift in range(PAIRS):
                left[head, head * FD + i, shift * FD + i] = 1.0
                right[head, head * FD + (i + shift) % FD, shift * FD + i] = 1.0
            left[head, head * FD + i, SQUARES + i] = 1.0
    plus[1, SQUARES : SQUARES + FD] = 1.0
    plus[0:2, SQUARES + FD] = 1.0
    plus[2, :SQUARES] = (2.0 * FD) ** (-0.5)
    plus[2, SQUARES : SQUARES + FD] = FD ** (-0.25)
    plus[2, SQUARES + FD] = 1.0
    return left, right, plus


def copies(plan, sems):
    made = []
    for number, (condition, source, target) in enumerate(plan):
        copy = pltpu.make_async_copy(source, target, sems.at[number])
        copy.start() if condition is True else pl.when(condition)(copy.start)
        made.append((condition, copy))

    def wait():
        for condition, copy in made:
            copy.wait() if condition is True else pl.when(condition)(copy.wait)

    return wait


def head_rows(source, target, first, heads):
    return [
        (True, source.at[pl.ds(head * HS, HS)], target.at[pl.ds(first + head * HEAD, HS)]) for head in range(heads)
    ]


def clear(target, pieces):
    for start, rows in pieces:
        target[pl.ds(start, rows), :] = jnp.zeros((rows, target.shape[1]), target.dtype)


def half_pieces(segments):
    pieces = ([], [])
    buffer_row = 0
    for start, rows in segments:
        for half in range(2):
            pieces[half].append((start + half * rows // 2, rows // 2, buffer_row))
        buffer_row += rows // 2
    return pieces, buffer_row


def put_halves(segments, info, source, near, far, sems):
    pieces, _ = half_pieces(segments)
    plan = []
    for half in range(2):
        for natural, rows, at in pieces[half]:
            for low in (0, 1):
                target = near if half == 1 - low else far
                plan.append((info[1] == low, source.at[pl.ds(natural, rows)], target.at[pl.ds(at, rows)]))
    copies(plan, sems)()


def halves_plan(segments, info, own, own_out, other, other_out, target):
    pieces, _ = half_pieces(segments)
    plan = []
    for low in (0, 1):
        for middle in (0, 1):
            near, far = (own, other) if middle else (own_out, other_out)
            for half in range(2):
                source = near if half == 1 - low else far
                for natural, rows, at in pieces[half]:
                    plan.append(
                        (
                            (info[1] == low) & (info[2] == middle),
                            source.at[pl.ds(at, rows)],
                            target.at[pl.ds(natural, rows)],
                        )
                    )
    return plan


def norm_rows(x, n, gain):
    rows = x.shape[0]
    for at in range(0, rows, 128):
        size = min(128, rows - at)
        n[pl.ds(at, size), :] = rms_norm(x[pl.ds(at, size), :], gain)


def lane_of_ones(shape):
    return (lax.broadcasted_iota(jnp.int32, shape, 1) & (HEAD - 1)) == HS


def linear_kernel(segments, shards, heads, prev, *refs):
    refs = list(refs)
    info, own, ups, downs = refs[0], refs[1], refs[2:5], refs[5:8]
    states = refs[8 : 8 + len(segments)]
    refs = refs[8 + len(segments) :]
    gain, taps, left, right, plus = refs[:5]
    query_weight, key_weight, value_weight, gate_weight, out_weight = refs[5:10]
    refs = refs[10:]
    if prev:
        prev_key, prev_mixed, prev_value = refs[:3]
        refs = refs[3:]
    refs = refs[1:]
    near, far, stay, key_out, mixed_out, value_out = refs[:6]
    x, n, u, w, ow, q, k, m, y, sems, wsems, osems = refs[6:]
    width = heads * HEAD
    total = x.shape[0]
    plan = []
    for segment, shard, row, rows in shards:
        for here in range(4):
            source = own if here == shard else (ups[here - shard - 1] if here > shard else downs[shard - here - 1])
            plan.append(
                (
                    info[0] == here,
                    source.at[info[4 + segment], pl.ds(0, rows)],
                    x.at[pl.ds(row, rows)],
                )
            )
    wait_x = copies(plan, sems)
    plan = [(True, query_weight, w.at[pl.ds(0, heads * FD)]), (True, key_weight, w.at[pl.ds(HEAD, heads * FD)])]
    plan += head_rows(value_weight, w, 2 * HEAD, heads) + head_rows(gate_weight, w, 2 * HEAD + width, heads)
    wait_w = copies(plan, wsems)
    wait_out = copies(head_rows(out_weight, ow, 0, heads), osems)
    clear(w, [(heads * FD, HEAD - heads * FD), (HEAD + heads * FD, HEAD - heads * FD)])
    clear(w, [(2 * HEAD + HS + HEAD * head, HEAD - HS) for head in range(2 * heads)])
    clear(ow, [(HS + HEAD * head, HEAD - HS) for head in range(heads)])
    if prev:
        k[pl.ds(0, prev), :] = prev_key[...]
        m[pl.ds(0, prev), :] = prev_mixed[...]
    wait_x()
    norm_rows(x, n, gain[...])
    wait_w()
    q[...] = dot_t(n[...], w[:HEAD]).astype(BF)
    k[pl.ds(prev, total), :] = dot_t(n[...], w[HEAD : 2 * HEAD]).astype(BF)
    y[...] = dot_t(n[...], w[2 * HEAD : 2 * HEAD + width]).astype(BF)
    u[...] = dot_t(n[...], w[2 * HEAD + width :]).astype(BF)
    tap = taps[...]
    for number, (start, rows) in enumerate(segments):
        base = prev if number == 0 else 0
        tile = min(rows, 256)
        if base:
            ends = prev_value[...].astype(F32)
            last2, last = ends[14:15], ends[15:16]
        else:
            ends = states[number][pl.ds(SQUARES + FD, 16), :].astype(F32)
            last2, last = ends[1:2], ends[2:3]
        for at in range(start, start + rows, tile):
            v = y[pl.ds(at, tile), :].astype(F32)
            opened = u[pl.ds(at, tile), :].astype(F32)
            row = lax.broadcasted_iota(jnp.int32, v.shape, 0)
            back1 = jnp.where(row == 0, last, pltpu.roll(v, 1, 0))
            back2 = jnp.where(row == 0, last2, jnp.where(row == 1, last, pltpu.roll(v, 2, 0)))
            last2, last = v[tile - 2 : tile - 1], v[tile - 1 : tile]
            convolved = tap[0:1] * v + tap[1:2] * back1 + tap[2:3] * back2
            mixed = convolved * (opened / (1.0 + jnp.exp(-opened)))
            m[pl.ds(prev + at, tile), :] = jnp.where(lane_of_ones(v.shape), 1.0, mixed).astype(BF)
            if number == 0 and at + tile == start + rows:
                value_out[...] = v[tile - 16 :].astype(BF)
    wait_out()
    for number, (start, rows) in enumerate(segments):
        base = prev if number == 0 else 0
        tile = min(rows, 256)
        first = 0 if number == 0 else prev + start
        for at in range(start, start + rows, tile):
            queries = q[pl.ds(at, tile), :]
            lane = lax.broadcasted_iota(jnp.int32, queries.shape, 1)
            for head in range(heads):
                columns = pl.ds(head * HEAD, HEAD)
                mapped = (
                    (dot(queries, left[head]) + plus[0:1, :])
                    * (dot(queries, right[head]) + plus[1:2, :])
                    * plus[2:3, :]
                )
                total_rows = dot(mapped.astype(BF), states[number][pl.ds(0, FEATURES), columns])
                own_lanes = (lane >= head * FD) & (lane < (head + 1) * FD)
                masked = jnp.where(own_lanes, queries, jnp.zeros_like(queries))
                for key_at in range(first, prev + at + tile, tile):
                    a = dot_t(masked, k[pl.ds(key_at, tile), :]) * FD ** (-0.5)
                    weights = 1.0 + a + 0.5 * a * a
                    if key_at == prev + at:
                        causal = lax.broadcasted_iota(jnp.int32, a.shape, 0) >= lax.broadcasted_iota(
                            jnp.int32, a.shape, 1
                        )
                        weights = jnp.where(causal, weights, 0.0)
                    total_rows += dot(weights.astype(BF), m[pl.ds(key_at, tile), columns])
                y[pl.ds(at, tile), columns] = (total_rows / total_rows[:, HS : HS + 1]).astype(BF)
    key_out[...] = k[pl.ds(prev, key_out.shape[0]), :]
    mixed_out[...] = m[pl.ds(prev, mixed_out.shape[0]), :]
    pieces, _ = half_pieces(segments)
    plan = []
    for low in (0, 1):
        for natural, rows, at in pieces[1 - low]:
            plan.append((info[1] == low, x.at[pl.ds(natural, rows)], stay.at[pl.ds(at, rows)]))
    copies(plan, sems)()
    x[...] = dot(y[...], ow[...]).astype(BF)
    put_halves(segments, info, x, near, far, sems)


def window_kernel(segments, heads, prev, *refs):
    refs = list(refs)
    info, own, own_out, other, other_out = refs[:5]
    states = refs[5 : 5 + len(segments)]
    refs = refs[5 + len(segments) :]
    gain, query_weight, key_weight, value_weight, out_weight = refs[:5]
    refs = refs[5:]
    if prev:
        prev_keys, prev_values = refs[:2]
        refs = refs[2:]
    refs = refs[1:]
    near, far, top, key_out, value_out = refs[:5]
    x, n, w, ow, q, k, v, y, sems, wsems, osems = refs[5:]
    width = heads * HEAD
    wait_x = copies(halves_plan(segments, info, own, own_out, other, other_out, x), sems)
    plan = head_rows(query_weight, w, 0, heads)
    plan += head_rows(key_weight, w, width, heads) + head_rows(value_weight, w, 2 * width, heads)
    wait_w = copies(plan, wsems)
    wait_out = copies(head_rows(out_weight, ow, 0, heads), osems)
    clear(w, [(HS + HEAD * head, HEAD - HS) for head in range(3 * heads)])
    clear(ow, [(HS + HEAD * head, HEAD - HS) for head in range(heads)])
    wait_x()
    norm_rows(x, n, gain[...])
    wait_w()
    q[...] = dot_t(n[...], w[:width]).astype(BF)
    new_keys = dot_t(n[...], w[width : 2 * width]).astype(BF)
    for number, (start, rows) in enumerate(segments):
        k[pl.ds(start + WIN * (number + 1), rows), :] = new_keys[start : start + rows]
    new_values = dot_t(n[...], w[2 * width :])
    new_values = jnp.where(lane_of_ones(new_values.shape), 1.0, new_values).astype(BF)
    for number, (start, rows) in enumerate(segments):
        v[pl.ds(start + WIN * (number + 1), rows), :] = new_values[start : start + rows]
    best = []
    for number, (start, rows) in enumerate(segments):
        shift = WIN * (number + 1)
        if prev and number == 0:
            k[pl.ds(0, WIN), :] = prev_keys[...]
            v[pl.ds(0, WIN), :] = prev_values[...]
        else:
            old = states[number][pl.ds(STATE_VALUES, WIN), :]
            k[pl.ds(start + shift - WIN, WIN), :] = states[number][pl.ds(STATE_KEYS, WIN), :]
            v[pl.ds(start + shift - WIN, WIN), :] = jnp.where(
                lane_of_ones(old.shape), jnp.ones_like(old), old
            )
        final = info[6 + number] - 1
        tile = min(rows, 128)
        best_here = jnp.full((1, 1), -jnp.inf, F32)
        for at in range(start, start + rows, tile):
            keys_here = tile + WIN
            row = lax.broadcasted_iota(jnp.int32, (tile, keys_here), 0)
            place = lax.broadcasted_iota(jnp.int32, (tile, keys_here), 1)
            allowed = (place > row) & (place <= row + WIN)
            for head in range(heads):
                columns = pl.ds(head * HEAD, HEAD)
                e = dot_t(q[pl.ds(at, tile), columns], k[pl.ds(shift - WIN + at, keys_here), columns])
                e = jnp.where(allowed, e * HS ** (-0.5), -jnp.inf)
                row_max = jnp.max(e, axis=-1, keepdims=True)
                chances = jnp.exp(e - row_max).astype(BF)
                o = dot(chances, v[pl.ds(shift - WIN + at, keys_here), columns])
                y[pl.ds(at, tile), columns] = (o / o[:, HS : HS + 1]).astype(BF)
                at_final = lax.broadcasted_iota(jnp.int32, row_max.shape, 0) + (at - start) == final
                best_here = jnp.maximum(
                    best_here, jnp.max(jnp.where(at_final, row_max, -jnp.inf), axis=0, keepdims=True)
                )
        best.append(best_here)
    end = segments[0][1]
    key_out[...] = k[pl.ds(end, WIN), :]
    value_out[...] = v[pl.ds(end, WIN), :]
    for number in range(len(segments)):
        top[pl.ds(number * 8, 8), :] = jnp.broadcast_to(best[number], (8, 128))
    wait_out()
    x[...] = dot(y[...], ow[...]).astype(BF)
    put_halves(segments, info, x, near, far, sems)


def hidden_kernel(segments, *refs):
    info, own, own_out, other, other_out, gain, gate, up, down, dep, near, far = refs[:12]
    x, n, inner, opened, gate_v, up_v, down_v, sems, wsems = refs[12:]
    block = 256
    wait_x = copies(halves_plan(segments, info, own, own_out, other, other_out, x), sems)
    waits = [
        copies([(True, matrix, held)], wsems.at[pl.ds(number, 1)])
        for number, (matrix, held) in enumerate(((gate, gate_v), (up, up_v), (down, down_v)))
    ]
    wait_x()
    norm_rows(x, n, gain[...])
    blocks = [pl.ds(at, block) for at in range(0, inner.shape[1], block)]
    waits[0]()
    for columns in blocks:
        opened[:, columns] = dot(n[...], gate_v[:, columns])
    waits[1]()
    for columns in blocks:
        gated = opened[:, columns]
        inner[:, columns] = (gated / (1.0 + jnp.exp(-gated)) * dot(n[...], up_v[:, columns])).astype(BF)
    waits[2]()
    for at in range(0, x.shape[1], block):
        columns = pl.ds(at, block)
        x[:, columns] = dot(inner[...], down_v[:, columns]).astype(BF)
    put_halves(segments, info, x, near, far, sems)


def call(body, outs, specs, scratch, operands, flops, moved, limit):
    return pl.pallas_call(
        body,
        out_shape=[jax.ShapeDtypeStruct(shape, dtype) for shape, dtype, _ in outs],
        in_specs=specs,
        out_specs=[spec for _, _, spec in outs],
        scratch_shapes=scratch,
        compiler_params=pltpu.CompilerParams(vmem_limit_bytes=limit * MIB),
        cost_estimate=pl.CostEstimate(flops=flops // 1000, bytes_accessed=moved // 1000, transcendentals=0),
    )(*operands)


def run_linear(segments, shards, heads, prev, info, own, ups, downs, states, consts, weights, before, dep):
    total = sum(rows for _, rows in segments)
    width = heads * HEAD
    gain, taps, *matrices = weights
    half = (total // 2, D)
    scratch = [
        pltpu.VMEM((total, D), BF),
        pltpu.VMEM((total, D), BF),
        pltpu.VMEM((total, width), BF),
        pltpu.VMEM((2 * HEAD + 2 * width, D), BF),
        pltpu.VMEM((width, D), BF),
        pltpu.VMEM((total, HEAD), BF),
        pltpu.VMEM((prev + total, HEAD), BF),
        pltpu.VMEM((prev + total, width), BF),
        pltpu.VMEM((total, width), BF),
        pltpu.SemaphoreType.DMA((20,)),
        pltpu.SemaphoreType.DMA((3 * heads,)),
        pltpu.SemaphoreType.DMA((heads,)),
    ]
    rows = segments[0][1]
    outs = [(half, BF, ANY)] * 3 + [((rows, HEAD), BF, VMEM), ((rows, width), BF, VMEM), ((16, width), BF, VMEM)]
    operands = [info, own, *ups, *downs, *states, gain, taps, *consts, *matrices, *before, dep]
    specs = [SMEM] + [ANY] * 7 + [VMEM] * (len(states) + 2 + 3) + [HBM] * 5 + [VMEM] * len(before) + [ANY]
    return call(
        functools.partial(linear_kernel, segments, shards, heads, prev),
        outs, specs, scratch, operands, 2 * total * D * 1792, 12 * MIB, 24,
    )


def run_window(segments, heads, prev, info, parts, states, weights, before, dep):
    total = sum(rows for _, rows in segments)
    width = heads * HEAD
    gain, *matrices = weights
    half = (total // 2, D)
    scratch = [
        pltpu.VMEM((total, D), BF),
        pltpu.VMEM((total, D), BF),
        pltpu.VMEM((3 * width, D), BF),
        pltpu.VMEM((width, D), BF),
        pltpu.VMEM((total, width), BF),
        pltpu.VMEM((total + WIN * len(segments), width), BF),
        pltpu.VMEM((total + WIN * len(segments), width), BF),
        pltpu.VMEM((total, width), BF),
        pltpu.SemaphoreType.DMA((20,)),
        pltpu.SemaphoreType.DMA((3 * heads,)),
        pltpu.SemaphoreType.DMA((heads,)),
    ]
    outs = [(half, BF, ANY)] * 2 + [((8 * len(segments), 128), F32, VMEM)] + [((WIN, width), BF, VMEM)] * 2
    operands = [info, *parts, *states, gain, *matrices, *before, dep]
    specs = [SMEM] + [ANY] * 4 + [VMEM] * (len(states) + 1) + [HBM] * 4 + [VMEM] * len(before) + [ANY]
    return call(
        functools.partial(window_kernel, segments, heads, prev),
        outs, specs, scratch, operands, 2 * total * D * 2048, 12 * MIB, 24,
    )


def run_hidden(segments, info, parts, weights, dep):
    total = sum(rows for _, rows in segments)
    gain, gate, up, down = weights
    half = (total // 2, D)
    units = gate.shape[1]
    specs = [SMEM] + [ANY] * 4 + [VMEM] + [HBM] * 3 + [ANY]
    scratch = [
        pltpu.VMEM((total, D), BF),
        pltpu.VMEM((total, D), BF),
        pltpu.VMEM((total, units), BF),
        pltpu.VMEM((total, units), F32),
        pltpu.VMEM(gate.shape, BF),
        pltpu.VMEM(up.shape, BF),
        pltpu.VMEM(down.shape, BF),
        pltpu.SemaphoreType.DMA((20,)),
        pltpu.SemaphoreType.DMA((3,)),
    ]
    return call(
        functools.partial(hidden_kernel, segments),
        [(half, BF, ANY)] * 2, specs, scratch, [info, *parts, gain, gate, up, down, dep],
        2 * total * D * units * 3, 24 * MIB, 36,
    )


def after(value, *others):
    nothing = sum(other[(0,) * other.ndim].astype(F32) * 0.0 for other in others)
    return value + nothing.astype(value.dtype)


INWARD, ACROSS, OUTWARD = [(0, 1), (3, 2)], [(1, 2), (2, 1)], [(1, 0), (2, 3)]


def to_middle(near, far, stay):
    far_in = lax.ppermute(far, "tensor", INWARD)
    near_in = lax.ppermute(near, "tensor", INWARD)
    crossed = lax.ppermute(far + far_in, "tensor", ACROSS)
    return (stay.astype(F32) + (near.astype(F32) + near_in.astype(F32) + crossed.astype(F32))).astype(BF)


def first_out(own):
    return lax.ppermute(own, "tensor", ACROSS), lax.ppermute(own, "tensor", OUTWARD)


def pick_axis(array, axis, index):
    return jnp.where(index, lax.index_in_dim(array, 1, axis, False), lax.index_in_dim(array, 0, axis, False))


def pack_kernel(index, folded, tails, keys, values, keep, send, pack, sems):
    slots_here, heads = folded.shape[:2]
    pack[...] = jnp.zeros_like(pack)
    for slot in range(slots_here):
        for head in range(heads):
            wide, narrow = pl.ds(head * HEAD, HEAD), pl.ds(head * HEAD, HS)
            ours = slice(head * HS, (head + 1) * HS)
            pack[slot, pl.ds(0, STATE_KEYS), wide] = folded[slot, head]
            pack[slot, pl.ds(STATE_KEYS, WIN), narrow] = keys[slot, :, ours]
            pack[slot, pl.ds(STATE_VALUES, WIN), narrow] = values[slot, :, ours]
        ends = pl.ds(STATE_KEYS - 16, 16)
        pack[slot, ends, :] = pack[slot, ends, :] + tails[slot]
    made = []
    count = keep.shape[0]
    for number in range(2 * count):
        target = keep if number < count else send
        made.append(pltpu.make_async_copy(pack.at[index[number]], target.at[number % count], sems.at[number]))
        made[-1].start()
    for copy in made:
        copy.wait()


def slot_states(request_group, group_slot, sums, norms, keys, values, tail, count, firsts, seconds):
    here = lax.axis_index("req")
    slots_here, heads = sums.shape[:2]
    width = heads * HEAD
    requests = request_group.shape[0]
    groups = lax.all_gather(request_group, "req", axis=0, tiled=True)
    matches = jnp.arange(group_slot.shape[0])[None, :] == groups[:, None]
    slots = jnp.sum(jnp.where(matches, group_slot[None, :], 0), axis=1)

    fold = jnp.asarray(fold_matrix())
    folded = jnp.einsum("fg,ahgd->ahfd", fold, sums, precision=lax.Precision.HIGHEST).astype(BF)
    folded_norms = jnp.einsum("fg,ahg->ahf", fold, norms, precision=lax.Precision.HIGHEST).astype(BF)
    folded = jnp.concatenate([folded, folded_norms[..., None]], axis=-1)
    folded = jnp.pad(folded, ((0, 0), (0, 0), (0, 0), (0, HEAD - HS - 1)))
    tails = tail.reshape(slots_here, KC - 1, heads, HS)
    tails = jnp.pad(tails, ((0, 0), (0, 0), (0, 0), (0, HEAD - HS))).reshape(slots_here, KC - 1, width)
    tails = jnp.pad(tails, ((0, 0), (1, 16 - KC), (0, 0)))

    bits = []
    while 1 << len(bits) < count:
        bits.append(len(bits))
    local = (slots - here * slots_here).reshape((2,) * len(bits) + (requests,))
    local = jnp.where((local >= 0) & (local < slots_here), local, slots_here)

    def swap(array, bit):
        return lax.ppermute(array, "req", [(i, i ^ (1 << bit)) for i in range(count)])

    def upper(bit):
        return (here >> bit) & 1 == 1

    axis = len(bits) - 1
    entries = count // 2 * requests
    index = [pick_axis(local, axis, upper(0)).reshape(-1), pick_axis(local, axis, ~upper(0)).reshape(-1)]
    index = after(jnp.concatenate(index), *firsts)
    shape = (entries, STATE_ROWS, width)
    keep, send = pl.pallas_call(
        pack_kernel,
        out_shape=[jax.ShapeDtypeStruct(shape, BF)] * 2,
        in_specs=[SMEM] + [VMEM] * 4,
        out_specs=[ANY] * 2,
        scratch_shapes=[
            pltpu.VMEM((slots_here + 1, STATE_ROWS, width), BF),
            pltpu.SemaphoreType.DMA((2 * entries,)),
        ],
        compiler_params=pltpu.CompilerParams(vmem_limit_bytes=12 * MIB),
    )(index, folded, tails, keys, values)
    packs = (keep + swap(send, 0)).reshape((2,) * (len(bits) - 1) + (requests, STATE_ROWS, width))
    halves = []
    cut = STATE_ROWS // 2
    for number in range(2):
        part = packs[..., number * cut : (number + 1) * cut, :]
        left = bits[1:]
        order = left if number == 0 else left[::-1]
        while order:
            bit, order = order[0], order[1:]
            axis = len(left) - 1 - left.index(bit)
            left = [b for b in left if b != bit]
            if not order:
                part = after(part, *seconds)
            part = pick_axis(part, axis, upper(bit)) + swap(pick_axis(part, axis, ~upper(bit)), bit)
        halves.append(part)
    return jnp.concatenate(halves, axis=1)


def make_line(req_count):
    def per_device(
        hidden,
        suffix_len,
        request_group,
        group_slot,
        norm_first,
        query_weight,
        key_weight,
        value_weight,
        filter_gate,
        filter_taps,
        linear_out,
        norm_second,
        window_query,
        window_key,
        window_value,
        window_out,
        norm_third,
        gate_weight,
        up_weight,
        down_weight,
        prefix_sums,
        prefix_norms,
        prefix_keys,
        prefix_values,
        prefix_tail,
    ):
        requests = hidden.shape[0]
        heads = prefix_sums.shape[1]
        share = hidden.shape[1]
        here = lax.axis_index("tensor")
        low = here < 2
        middle = (here == 1) | (here == 2)

        both = (suffix_len[0] > SHORT) & (suffix_len[1] > SHORT)
        long = jnp.where(both, 0, (suffix_len[1] > SHORT).astype(jnp.int32))
        short = 1 - long

        ups, downs = [], []
        up = down = hidden
        for step in range(1, 4):
            up = lax.ppermute(up, "tensor", [(i, i + 1) for i in range(step - 1, 3)])
            down = lax.ppermute(down, "tensor", [(i + 1, i) for i in range(4 - step)])
            ups.append(up)
            downs.append(down)
        states = slot_states(
            request_group, group_slot, prefix_sums, prefix_norms, prefix_keys, prefix_values, prefix_tail, req_count,
            (ups[0], downs[0]), (ups[1], downs[1]),
        )

        def wide(matrix):
            matrix = matrix.reshape(matrix.shape[0], heads, HS)
            return jnp.pad(matrix, ((0, 0), (0, 0), (0, HEAD - HS))).reshape(matrix.shape[0], heads * HEAD)

        linear_weights = (
            norm_first[None],
            jnp.pad(wide(filter_taps), ((0, 8 - KC), (0, 0))),
            query_weight.T,
            key_weight.T,
            value_weight.T,
            filter_gate.T,
            linear_out,
        )
        window_weights = (norm_second[None], window_query.T, window_key.T, window_value.T, window_out)
        hidden_weights = (norm_third[None], gate_weight, up_weight, down_weight)
        left, right, plus = feature_maps(heads)
        consts = (jnp.asarray(left, BF), jnp.asarray(right, BF), jnp.asarray(plus))

        place = [here, low.astype(jnp.int32), middle.astype(jnp.int32), here * 0]
        quarters = tuple((0, s, s * share, share) for s in range(4))
        rows_here = here * share + jnp.arange(share)

        def info(indices):
            indices = [jnp.int32(0) + index for index in indices] * 2
            lengths = [suffix_len[index] for index in indices[:2]]
            return jnp.stack(place + indices[:2] + lengths).astype(jnp.int32)

        def run(streams, segments, shards):
            count = len(streams)
            infos = [info(indices) for indices in streams]
            parts, own, tops = [None] * count, [None] * count, [None] * count
            waiting = None
            dep = hidden
            for layer in range(3):
                for number, indices in enumerate(streams):
                    mine = [states[index] for index in indices]
                    if waiting is not None and count > 1:
                        late, late_own = waiting
                        other, own_out = first_out(late_own)
                    elif layer > 0:
                        other, own_out = first_out(own[number])
                        parts[number] = (own[number], own_out, other, lax.ppermute(other, "tensor", OUTWARD))
                    if layer == 0:
                        near, far, stay, *_ = run_linear(
                            segments, shards, heads, 0, infos[number], hidden, ups, downs,
                            mine, consts, linear_weights, [], dep,
                        )
                    elif layer == 1:
                        stay = own[number]
                        near, far, tops[number], *_ = run_window(
                            segments, heads, 0, infos[number], parts[number], mine, window_weights, [], dep
                        )
                    else:
                        stay = own[number]
                        near, far = run_hidden(segments, infos[number], parts[number], hidden_weights, dep)
                    if waiting is not None and count > 1:
                        far = after(far, other, own_out)
                        parts[late] = (late_own, own_out, other, lax.ppermute(other, "tensor", OUTWARD))
                    own[number] = to_middle(near, far, stay)
                    dep = own[number]
                    waiting = (number, own[number]) if layer < 2 else None
            return own, tops

        def live(rows, length):
            return jnp.where((rows_here < length)[:, None], rows, jnp.zeros_like(rows))

        half_row = jnp.where(low, 0, LMAX // 2)

        def square_sum(rows, first, length):
            floats = rows.astype(F32)
            counted = middle & (first + jnp.arange(rows.shape[0]) < length)
            return jnp.sum(jnp.where(counted[:, None], floats * floats, 0.0))

        def all_long():
            own, tops = run([(0,), (1,)], ((0, LMAX),), quarters)
            outs, squares = [], []
            for request in range(requests):
                squares.append(square_sum(own[request], half_row, suffix_len[request]))
                first, second = own[request][:share], own[request][share:]
                moved = lax.ppermute(jnp.where(low, first, second), "tensor", OUTWARD)
                outs.append(live(jnp.where(middle, jnp.where(low, second, first), moved), suffix_len[request]))
            return jnp.stack(outs), jnp.stack(squares + [top[0, 0] for top in tops])

        def one_long():
            own, tops = run(
                [(long, short)], ((0, LMAX), (LMAX, SHORT)), quarters + ((1, 0, LMAX, SHORT),)
            )
            own, top = own[0], tops[0]
            first, second, last = own[:share], own[share : 2 * share], own[2 * share :]
            moved = lax.ppermute(jnp.concatenate([jnp.where(low, first, second), last]), "tensor", OUTWARD)
            rest = lax.ppermute(last, "tensor", [(2, 0)])
            mine = jnp.where(middle, jnp.where(low, second, first), moved[:share])
            long_out = live(mine, suffix_len[long])
            mine = jnp.concatenate([moved[share:], rest, jnp.zeros((share - SHORT, D), BF)])
            short_out = live(mine, suffix_len[short])
            long_square = square_sum(own[: 2 * share], half_row, suffix_len[long])
            short_square = square_sum(last, jnp.where(low, 0, SHORT // 2), suffix_len[short])

            def ordered(of_long, of_short):
                return [jnp.where(long == request, of_long, of_short) for request in range(2)]

            return (
                jnp.stack(ordered(long_out, short_out)),
                jnp.stack(ordered(long_square, short_square) + ordered(top[0, 0], top[8, 0])),
            )

        outs, scalars = lax.cond(both, all_long, one_long)
        scalars = jnp.broadcast_to(scalars[:, None], (2 * requests, 128))
        everyone = [scalars] + [
            lax.ppermute(scalars, "tensor", [(i, (i + step) % 4) for i in range(4)]) for step in (1, 2, 3)
        ]
        total = sum(each[:requests, 0] for each in everyone)
        top_logit = functools.reduce(jnp.maximum, [each[requests:, 0] for each in everyone])
        return outs, jnp.sqrt(total / D), top_logit

    return per_device


def folded_features(queries):
    floats = jnp.transpose(queries.astype(F32), (1, 0, 2))
    parts = [jnp.ones(floats.shape[:-1] + (1,), F32), floats * FD ** (-0.25)]
    for shift in range(PAIRS):
        parts.append(floats * jnp.roll(floats, -shift, axis=-1) * (2.0 * FD) ** (-0.5))
    return jnp.concatenate(parts, axis=-1)


def plain_fold_matrix():
    row = jnp.arange(1 + FD + PAIRS * FD)[:, None]
    column = jnp.arange(1 + FD + FD * FD)[None, :]
    shift, first = (row - 1 - FD) // FD, (row - 1 - FD) % FD
    second = (first + shift) % FD
    major, minor = (column - 1 - FD) // FD, (column - 1 - FD) % FD
    straight = (major == first) & (minor == second)
    swapped = (major == second) & (minor == first) & (shift > 0) & (shift < FD // 2)
    squares = (row > FD) & (column > FD) & (straight | swapped)
    return jnp.where((row == column) & (row <= FD) | squares, 1.0, 0.0).astype(F32)


def line_gather(rows, axis, count):
    here = lax.axis_index(axis)
    size = rows.shape[0]
    up = down = rows
    ups, downs = [], []
    for step in range(1, count):
        up = lax.ppermute(up, axis, [(i, i + 1) for i in range(step - 1, count - 1)])
        down = lax.ppermute(down, axis, [(i + 1, i) for i in range(count - step)])
        ups.append(up)
        downs.append(down)
    around = jnp.concatenate(ups[::-1] + [rows] + downs)
    return lax.dynamic_slice_in_dim(around, (count - 1 - here) * size, count * size, 0)


def line_scatter(partial, axis, count):
    here = lax.axis_index(axis)
    size = partial.shape[0] // count

    def block(index):
        return lax.dynamic_slice_in_dim(partial, index * size, size, 0)

    up = down = None
    for step in range(1, count):
        to_up = block(jnp.minimum(here + count - step, count - 1))
        to_down = block(jnp.maximum(here - count + step, 0))
        if up is not None:
            to_up, to_down = to_up + up, to_down + down
        up = lax.ppermute(to_up, axis, [(i, i + 1) for i in range(step)])
        down = lax.ppermute(to_down, axis, [(i + 1, i) for i in range(count - 1 - step, count - 1)])
    return block(here).astype(F32) + up.astype(F32) + down.astype(F32)


def settle(partial, stream, axis, count):
    here = lax.axis_index(axis)
    size = partial.shape[0] // count
    mine = lax.dynamic_slice_in_dim(stream, here * size, size, 0)
    total = line_scatter(partial, axis, count)
    return line_gather((mine.astype(F32) + total).astype(BF), axis, count)


def bring_home(packs, axis, count):
    here = lax.axis_index(axis)
    bit = 1
    while bit < count:
        pairs = packs.reshape((packs.shape[0] // 2, 2) + packs.shape[1:])
        upper = (here & bit) != 0
        keep = jnp.where(upper, pairs[:, 1], pairs[:, 0])
        send = jnp.where(upper, pairs[:, 0], pairs[:, 1])
        packs = keep + lax.ppermute(send, axis, [(i, i ^ bit) for i in range(count)])
        bit *= 2
    return packs[0]


def make_plain(req_count, tensor_count):
    def per_device(
        hidden,
        suffix_len,
        request_group,
        group_slot,
        norm_first,
        query_weight,
        key_weight,
        value_weight,
        filter_gate,
        filter_taps,
        linear_out,
        norm_second,
        window_query,
        window_key,
        window_value,
        window_out,
        norm_third,
        gate_weight,
        up_weight,
        down_weight,
        prefix_sums,
        prefix_norms,
        prefix_keys,
        prefix_values,
        prefix_tail,
    ):
        requests_here = hidden.shape[0]
        share_rows = hidden.shape[1]
        slots_here, heads = prefix_sums.shape[:2]
        width = heads * HS

        groups = lax.all_gather(request_group, "req", axis=0, tiled=True)
        matches = jnp.arange(group_slot.shape[0])[None, :] == groups[:, None]
        slots = jnp.sum(jnp.where(matches, group_slot[None, :], 0), axis=1)
        fold = plain_fold_matrix()
        sums = jnp.einsum("fg,ahgd->afhd", fold, prefix_sums, precision=lax.Precision.HIGHEST)
        terms = sums.shape[1]
        norms = jnp.einsum("fg,ahg->afh", fold, prefix_norms, precision=lax.Precision.HIGHEST)
        norms = jnp.pad(norms.reshape(slots_here, -1), ((0, 0), (0, 2 * width - terms * heads)))
        pack = jnp.concatenate(
            [
                sums.reshape(slots_here, terms, width).astype(BF),
                norms.reshape(slots_here, 2, width).astype(BF),
                prefix_keys,
                prefix_values,
                prefix_tail,
            ],
            axis=1,
        )
        rows = pack.shape[1]
        pack = jnp.pad(pack, ((0, 0), (0, -rows % 32), (0, 0)))
        half = pack.shape[1] // 2
        pack = jnp.concatenate([pack[:, :half], pack[:, half:]], axis=2)
        local = slots - lax.axis_index("req") * slots_here
        owned = (local >= 0) & (local < slots_here)
        sent = jnp.take(pack, jnp.clip(local, 0, slots_here - 1), axis=0)
        sent = jnp.where(owned[:, None, None], sent, jnp.zeros_like(sent))
        sent = sent.reshape((req_count, requests_here) + sent.shape[1:])
        states = bring_home(sent, "req", req_count)
        states = jnp.concatenate([states[:, :, :width], states[:, :, width:]], axis=1)

        position = jnp.arange(LMAX)
        causal = position[:, None] >= position[None, :]
        bands = LMAX // WIN
        band_row = jnp.arange(WIN)[:, None]
        band_key = jnp.arange(2 * WIN)[None, :]
        allowed = (band_key > band_row) & (band_key <= band_row + WIN)

        def linear_part(request, stream):
            state = states[request]
            state_sums = state[:terms].reshape(terms, heads, HS)
            state_norms = state[terms : terms + 2].reshape(-1)[: terms * heads].reshape(terms, heads)
            tail = state[terms + 2 + 2 * WIN : terms + 2 + 2 * WIN + KC - 1]
            normed = rms_norm(stream, norm_first)
            queries = dot(normed, query_weight).astype(BF).reshape(LMAX, heads, FD)
            key_rows = dot(normed, key_weight).astype(BF).reshape(LMAX, heads, FD)
            values = dot(normed, value_weight).astype(BF)
            gating = dot(normed, filter_gate).astype(BF)
            extended = jnp.concatenate([tail, values], axis=0).astype(F32)
            convolved = sum(
                filter_taps[offset] * extended[KC - 1 - offset : KC - 1 - offset + LMAX]
                for offset in range(KC)
            )
            mixed = (convolved * jax.nn.silu(gating.astype(F32))).astype(BF)
            mixed = mixed.reshape(LMAX, heads, HS)
            scores = jnp.einsum("thf,shf->hts", queries, key_rows, preferred_element_type=F32)
            scores = scores * FD ** (-0.5)
            weights = jnp.where(causal, 1.0 + scores + 0.5 * scores * scores, 0.0)
            mapped = folded_features(queries)
            numerator = jnp.einsum(
                "hts,shd->thd", weights.astype(BF), mixed, preferred_element_type=F32
            ) + jnp.einsum(
                "htf,fhd->thd", mapped.astype(BF), state_sums, preferred_element_type=F32
            )
            denominator = jnp.sum(weights, axis=-1) + jnp.sum(
                mapped * jnp.transpose(state_norms).astype(F32)[:, None, :], axis=-1
            )
            linear_rows = (numerator / jnp.transpose(denominator)[..., None]).astype(BF)
            return dot(linear_rows.reshape(LMAX, width), linear_out).astype(BF)

        def window_part(request, stream):
            state = states[request]
            normed = rms_norm(stream, norm_second)
            queries = dot(normed, window_query).astype(BF).reshape(bands, WIN, heads, HS)
            key_rows = dot(normed, window_key).astype(BF)
            value_rows = dot(normed, window_value).astype(BF)
            start = terms + 2

            def paired(prefix, rows):
                blocks = jnp.concatenate([prefix, rows]).reshape(bands + 1, WIN, heads, HS)
                return jnp.concatenate([blocks[:-1], blocks[1:]], axis=1)

            key_pairs = paired(state[start : start + WIN], key_rows)
            value_pairs = paired(state[start + WIN : start + 2 * WIN], value_rows)
            logits = jnp.einsum(
                "bthd,bphd->bhtp", queries, key_pairs, preferred_element_type=F32
            ) * HS ** (-0.5)
            logits = jnp.where(allowed, logits, -jnp.inf)
            row_max = jnp.max(logits, axis=-1, keepdims=True)
            exponent = jnp.exp(logits - row_max)
            chances = (exponent / jnp.sum(exponent, axis=-1, keepdims=True)).astype(BF)
            attended = jnp.einsum(
                "bhtp,bphd->bthd", chances, value_pairs, preferred_element_type=F32
            ).astype(BF)
            final = (position == suffix_len[request] - 1).reshape(bands, 1, WIN)
            top = jnp.max(jnp.where(final, row_max[..., 0], -jnp.inf))
            return dot(attended.reshape(LMAX, width), window_out).astype(BF), top

        def hidden_part(stream):
            normed = rms_norm(stream, norm_third)
            inner = (jax.nn.silu(dot(normed, gate_weight)) * dot(normed, up_weight)).astype(BF)
            return dot(inner, down_weight).astype(BF)

        here = lax.axis_index("tensor")
        row_start = here * share_rows
        rows_here = row_start + jnp.arange(share_rows)
        outs, squares, tops = [], [], []
        for request in range(requests_here):
            stream = line_gather(hidden[request], "tensor", tensor_count)
            partial = linear_part(request, stream)
            stream = settle(partial, stream, "tensor", tensor_count)
            partial, top = window_part(request, stream)
            stream = settle(partial, stream, "tensor", tensor_count)
            partial = hidden_part(stream)
            total = line_scatter(partial, "tensor", tensor_count)
            mine = lax.dynamic_slice_in_dim(stream, row_start, share_rows, 0).astype(F32)
            mine = (mine + total).astype(BF)
            live = (rows_here < suffix_len[request])[:, None]
            outs.append(jnp.where(live, mine, jnp.zeros_like(mine)))
            floats = mine.astype(F32)
            squares.append(jnp.sum(jnp.where(live, floats * floats, 0.0)))
            tops.append(top)
        scalars = lax.all_gather(jnp.stack(squares + tops), "tensor")
        total = jnp.sum(scalars[:, :requests_here], axis=0)
        top_logit = jnp.max(scalars[:, requests_here:], axis=0)
        return jnp.stack(outs), jnp.sqrt(total / D), top_logit

    return per_device


def solution(mesh):
    return jax.shard_map(
        make_line(mesh.shape["req"]) if mesh.shape["tensor"] == 4 else make_plain(mesh.shape["req"], mesh.shape["tensor"]),
        mesh=mesh,
        in_specs=(
            P("req", "tensor", None),
            P("req"),
            P("req"),
            P(),
            P(),
            P(None, "tensor"),
            P(None, "tensor"),
            P(None, "tensor"),
            P(None, "tensor"),
            P(None, "tensor"),
            P("tensor", None),
            P(),
            P(None, "tensor"),
            P(None, "tensor"),
            P(None, "tensor"),
            P("tensor", None),
            P(),
            P(None, "tensor"),
            P(None, "tensor"),
            P("tensor", None),
            P("req", "tensor", None, None),
            P("req", "tensor", None),
            P("req", None, "tensor"),
            P("req", None, "tensor"),
            P("req", None, "tensor"),
        ),
        out_specs=(P("req", "tensor", None), P("req"), P("req")),
        check_vma=False,
    )
```

```python
import functools

import jax
import jax.numpy as jnp
import numpy as np
from jax import lax
from jax.experimental import pallas as pl
from jax.experimental.pallas import tpu as pltpu
from jax.sharding import PartitionSpec as P

D = 1792
FD = 16
HS = 112
WIN = 64
KC = 3
LMAX = 512
SHORT = 32
PAIRS = FD // 2 + 1
SQUARES = PAIRS * FD
FEATURES = 256
HEAD = 128
STATE_KEYS = 176
STATE_VALUES = STATE_KEYS + WIN
STATE_ROWS = STATE_VALUES + WIN

EPS = 1e-05
BF = jnp.bfloat16
F32 = jnp.float32
MIB = 1 << 20
ANY = pl.BlockSpec(memory_space=pl.ANY)
SMEM = pl.BlockSpec(memory_space=pltpu.SMEM)
VMEM = pl.BlockSpec(memory_space=pltpu.VMEM)
HBM = pl.BlockSpec(memory_space=pltpu.HBM)


def rms_norm(rows, gain):
    floats = rows.astype(F32)
    inverse_rms = lax.rsqrt(jnp.mean(floats * floats, axis=-1, keepdims=True) + EPS)
    return (floats * inverse_rms * gain).astype(BF)


def dot(left, right):
    return jnp.dot(left, right, preferred_element_type=F32)


def dot_t(left, right):
    return lax.dot_general(left, right, (((1,), (1,)), ((), ())), preferred_element_type=F32)


def fold_matrix():
    fold = np.zeros((STATE_KEYS, 1 + FD + FD * FD), np.float32)
    for shift in range(PAIRS):
        for i in range(FD):
            j = (i + shift) % FD
            fold[shift * FD + i, 1 + FD + i * FD + j] = 1.0
            if 0 < shift < FD // 2:
                fold[shift * FD + i, 1 + FD + j * FD + i] = 1.0
    for i in range(FD):
        fold[SQUARES + i, 1 + i] = 1.0
    fold[SQUARES + FD, 0] = 1.0
    return fold


def feature_maps(heads):
    left = np.zeros((heads, HEAD, FEATURES), np.float32)
    right = np.zeros((heads, HEAD, FEATURES), np.float32)
    plus = np.zeros((8, FEATURES), np.float32)
    for head in range(heads):
        for i in range(FD):
            for shift in range(PAIRS):
                left[head, head * FD + i, shift * FD + i] = 1.0
                right[head, head * FD + (i + shift) % FD, shift * FD + i] = 1.0
            left[head, head * FD + i, SQUARES + i] = 1.0
    plus[1, SQUARES : SQUARES + FD] = 1.0
    plus[0:2, SQUARES + FD] = 1.0
    plus[2, :SQUARES] = (2.0 * FD) ** (-0.5)
    plus[2, SQUARES : SQUARES + FD] = FD ** (-0.25)
    plus[2, SQUARES + FD] = 1.0
    return left, right, plus


def copies(plan, sems):
    made = []
    for number, (condition, source, target) in enumerate(plan):
        copy = pltpu.make_async_copy(source, target, sems.at[number])
        copy.start() if condition is True else pl.when(condition)(copy.start)
        made.append((condition, copy))

    def wait():
        for condition, copy in made:
            copy.wait() if condition is True else pl.when(condition)(copy.wait)

    return wait


def head_rows(source, target, first, heads):
    return [
        (True, source.at[pl.ds(head * HS, HS)], target.at[pl.ds(first + head * HEAD, HS)]) for head in range(heads)
    ]


def clear(target, pieces):
    for start, rows in pieces:
        target[pl.ds(start, rows), :] = jnp.zeros((rows, target.shape[1]), target.dtype)


def half_pieces(segments):
    pieces = ([], [])
    buffer_row = 0
    for start, rows in segments:
        for half in range(2):
            pieces[half].append((start + half * rows // 2, rows // 2, buffer_row))
        buffer_row += rows // 2
    return pieces, buffer_row


def put_halves(segments, info, source, near, far, sems):
    pieces, _ = half_pieces(segments)
    plan = []
    for half in range(2):
        for natural, rows, at in pieces[half]:
            for low in (0, 1):
                target = near if half == 1 - low else far
                plan.append((info[1] == low, source.at[pl.ds(natural, rows)], target.at[pl.ds(at, rows)]))
    copies(plan, sems)()


def halves_plan(segments, info, own, own_out, other, other_out, target):
    pieces, _ = half_pieces(segments)
    plan = []
    for low in (0, 1):
        for middle in (0, 1):
            near, far = (own, other) if middle else (own_out, other_out)
            for half in range(2):
                source = near if half == 1 - low else far
                for natural, rows, at in pieces[half]:
                    plan.append(
                        (
                            (info[1] == low) & (info[2] == middle),
                            source.at[pl.ds(at, rows)],
                            target.at[pl.ds(natural, rows)],
                        )
                    )
    return plan


def norm_rows(x, n, gain):
    rows = x.shape[0]
    for at in range(0, rows, 128):
        size = min(128, rows - at)
        n[pl.ds(at, size), :] = rms_norm(x[pl.ds(at, size), :], gain)


def lane_of_ones(shape):
    return (lax.broadcasted_iota(jnp.int32, shape, 1) & (HEAD - 1)) == HS


def linear_kernel(segments, shards, heads, prev, *refs):
    refs = list(refs)
    info, own, ups, downs = refs[0], refs[1], refs[2:5], refs[5:8]
    states = refs[8 : 8 + len(segments)]
    refs = refs[8 + len(segments) :]
    gain, taps, left, right, plus = refs[:5]
    query_weight, key_weight, value_weight, gate_weight, out_weight = refs[5:10]
    refs = refs[10:]
    if prev:
        prev_key, prev_mixed, prev_value = refs[:3]
        refs = refs[3:]
    refs = refs[2:]
    near, far, stay, key_out, mixed_out, value_out = refs[:6]
    x, n, u, w, ow, q, k, m, y, sems, wsems, osems = refs[6:]
    width = heads * HEAD
    total = x.shape[0]
    plan = []
    for segment, shard, row, rows in shards:
        for here in range(4):
            source = own if here == shard else (ups[here - shard - 1] if here > shard else downs[shard - here - 1])
            plan.append(
                (
                    info[0] == here,
                    source.at[info[4 + segment], pl.ds(0, rows)],
                    x.at[pl.ds(row, rows)],
                )
            )
    wait_x = copies(plan, sems)
    plan = [(True, query_weight, w.at[pl.ds(0, heads * FD)]), (True, key_weight, w.at[pl.ds(HEAD, heads * FD)])]
    plan += head_rows(value_weight, w, 2 * HEAD, heads) + head_rows(gate_weight, w, 2 * HEAD + width, heads)
    wait_w = copies(plan, wsems)
    wait_out = copies(head_rows(out_weight, ow, 0, heads), osems)
    clear(w, [(heads * FD, HEAD - heads * FD), (HEAD + heads * FD, HEAD - heads * FD)])
    clear(w, [(2 * HEAD + HS + HEAD * head, HEAD - HS) for head in range(2 * heads)])
    clear(ow, [(HS + HEAD * head, HEAD - HS) for head in range(heads)])
    if prev:
        k[pl.ds(0, prev), :] = prev_key[...]
        m[pl.ds(0, prev), :] = prev_mixed[...]
    wait_x()
    norm_rows(x, n, gain[...])
    wait_w()
    q[...] = dot_t(n[...], w[:HEAD]).astype(BF)
    k[pl.ds(prev, total), :] = dot_t(n[...], w[HEAD : 2 * HEAD]).astype(BF)
    y[...] = dot_t(n[...], w[2 * HEAD : 2 * HEAD + width]).astype(BF)
    u[...] = dot_t(n[...], w[2 * HEAD + width :]).astype(BF)
    tap = taps[...]
    for number, (start, rows) in enumerate(segments):
        base = prev if number == 0 else 0
        tile = min(rows, 256)
        if base:
            ends = prev_value[...].astype(F32)
            last2, last = ends[14:15], ends[15:16]
        else:
            ends = states[number][pl.ds(SQUARES + FD, 16), :].astype(F32)
            last2, last = ends[1:2], ends[2:3]
        for at in range(start, start + rows, tile):
            v = y[pl.ds(at, tile), :].astype(F32)
            opened = u[pl.ds(at, tile), :].astype(F32)
            row = lax.broadcasted_iota(jnp.int32, v.shape, 0)
            back1 = jnp.where(row == 0, last, pltpu.roll(v, 1, 0))
            back2 = jnp.where(row == 0, last2, jnp.where(row == 1, last, pltpu.roll(v, 2, 0)))
            last2, last = v[tile - 2 : tile - 1], v[tile - 1 : tile]
            convolved = tap[0:1] * v + tap[1:2] * back1 + tap[2:3] * back2
            mixed = convolved * (opened / (1.0 + jnp.exp(-opened)))
            m[pl.ds(prev + at, tile), :] = jnp.where(lane_of_ones(v.shape), 1.0, mixed).astype(BF)
            if number == 0 and at + tile == start + rows:
                value_out[...] = v[tile - 16 :].astype(BF)
    wait_out()
    for number, (start, rows) in enumerate(segments):
        base = prev if number == 0 else 0
        tile = min(rows, 256)
        first = 0 if number == 0 else prev + start
        for at in range(start, start + rows, tile):
            queries = q[pl.ds(at, tile), :]
            lane = lax.broadcasted_iota(jnp.int32, queries.shape, 1)
            for head in range(heads):
                columns = pl.ds(head * HEAD, HEAD)
                mapped = (
                    (dot(queries, left[head]) + plus[0:1, :])
                    * (dot(queries, right[head]) + plus[1:2, :])
                    * plus[2:3, :]
                )
                total_rows = dot(mapped.astype(BF), states[number][pl.ds(0, FEATURES), columns])
                own_lanes = (lane >= head * FD) & (lane < (head + 1) * FD)
                masked = jnp.where(own_lanes, queries, jnp.zeros_like(queries))
                for key_at in range(first, prev + at + tile, tile):
                    a = dot_t(masked, k[pl.ds(key_at, tile), :]) * FD ** (-0.5)
                    weights = 1.0 + a + 0.5 * a * a
                    if key_at == prev + at:
                        causal = lax.broadcasted_iota(jnp.int32, a.shape, 0) >= lax.broadcasted_iota(
                            jnp.int32, a.shape, 1
                        )
                        weights = jnp.where(causal, weights, 0.0)
                    total_rows += dot(weights.astype(BF), m[pl.ds(key_at, tile), columns])
                y[pl.ds(at, tile), columns] = (total_rows / total_rows[:, HS : HS + 1]).astype(BF)
    key_out[...] = k[pl.ds(prev, key_out.shape[0]), :]
    mixed_out[...] = m[pl.ds(prev, mixed_out.shape[0]), :]
    pieces, _ = half_pieces(segments)
    plan = []
    for low in (0, 1):
        for natural, rows, at in pieces[1 - low]:
            plan.append((info[1] == low, x.at[pl.ds(natural, rows)], stay.at[pl.ds(at, rows)]))
    copies(plan, sems)()
    x[...] = dot(y[...], ow[...]).astype(BF)
    put_halves(segments, info, x, near, far, sems)


def window_kernel(segments, heads, prev, *refs):
    refs = list(refs)
    info, own, own_out, other, other_out = refs[:5]
    states = refs[5 : 5 + len(segments)]
    refs = refs[5 + len(segments) :]
    gain, query_weight, key_weight, value_weight, out_weight = refs[:5]
    refs = refs[5:]
    if prev:
        prev_keys, prev_values = refs[:2]
        refs = refs[2:]
    refs = refs[2:]
    near, far, top, key_out, value_out = refs[:5]
    x, n, w, ow, q, k, v, y, sems, wsems, osems = refs[5:]
    width = heads * HEAD
    wait_x = copies(halves_plan(segments, info, own, own_out, other, other_out, x), sems)
    plan = head_rows(query_weight, w, 0, heads)
    plan += head_rows(key_weight, w, width, heads) + head_rows(value_weight, w, 2 * width, heads)
    wait_w = copies(plan, wsems)
    wait_out = copies(head_rows(out_weight, ow, 0, heads), osems)
    clear(w, [(HS + HEAD * head, HEAD - HS) for head in range(3 * heads)])
    clear(ow, [(HS + HEAD * head, HEAD - HS) for head in range(heads)])
    wait_x()
    norm_rows(x, n, gain[...])
    wait_w()
    q[...] = dot_t(n[...], w[:width]).astype(BF)
    new_keys = dot_t(n[...], w[width : 2 * width]).astype(BF)
    for number, (start, rows) in enumerate(segments):
        k[pl.ds(start + WIN * (number + 1), rows), :] = new_keys[start : start + rows]
    new_values = dot_t(n[...], w[2 * width :])
    new_values = jnp.where(lane_of_ones(new_values.shape), 1.0, new_values).astype(BF)
    for number, (start, rows) in enumerate(segments):
        v[pl.ds(start + WIN * (number + 1), rows), :] = new_values[start : start + rows]
    best = []
    for number, (start, rows) in enumerate(segments):
        shift = WIN * (number + 1)
        if prev and number == 0:
            k[pl.ds(0, WIN), :] = prev_keys[...]
            v[pl.ds(0, WIN), :] = prev_values[...]
        else:
            old = states[number][pl.ds(STATE_VALUES, WIN), :]
            k[pl.ds(start + shift - WIN, WIN), :] = states[number][pl.ds(STATE_KEYS, WIN), :]
            v[pl.ds(start + shift - WIN, WIN), :] = jnp.where(
                lane_of_ones(old.shape), jnp.ones_like(old), old
            )
        final = info[6 + number] - 1
        tile = min(rows, 128)
        best_here = jnp.full((1, 1), -jnp.inf, F32)
        for at in range(start, start + rows, tile):
            keys_here = tile + WIN
            row = lax.broadcasted_iota(jnp.int32, (tile, keys_here), 0)
            place = lax.broadcasted_iota(jnp.int32, (tile, keys_here), 1)
            allowed = (place > row) & (place <= row + WIN)
            for head in range(heads):
                columns = pl.ds(head * HEAD, HEAD)
                e = dot_t(q[pl.ds(at, tile), columns], k[pl.ds(shift - WIN + at, keys_here), columns])
                e = jnp.where(allowed, e * HS ** (-0.5), -jnp.inf)
                row_max = jnp.max(e, axis=-1, keepdims=True)
                chances = jnp.exp(e - row_max).astype(BF)
                o = dot(chances, v[pl.ds(shift - WIN + at, keys_here), columns])
                y[pl.ds(at, tile), columns] = (o / o[:, HS : HS + 1]).astype(BF)
                at_final = lax.broadcasted_iota(jnp.int32, row_max.shape, 0) + (at - start) == final
                best_here = jnp.maximum(
                    best_here, jnp.max(jnp.where(at_final, row_max, -jnp.inf), axis=0, keepdims=True)
                )
        best.append(best_here)
    end = segments[0][1]
    key_out[...] = k[pl.ds(end, WIN), :]
    value_out[...] = v[pl.ds(end, WIN), :]
    for number in range(len(segments)):
        top[pl.ds(number * 8, 8), :] = jnp.broadcast_to(best[number], (8, 128))
    wait_out()
    x[...] = dot(y[...], ow[...]).astype(BF)
    put_halves(segments, info, x, near, far, sems)


def hidden_kernel(segments, *refs):
    info, own, own_out, other, other_out, gain, gate, up, down, _, _, near, far = refs[:13]
    x, n, inner, opened, gate_v, up_v, down_v, sems, wsems = refs[13:]
    block = 256
    wait_x = copies(halves_plan(segments, info, own, own_out, other, other_out, x), sems)
    waits = [
        copies([(True, matrix, held)], wsems.at[pl.ds(number, 1)])
        for number, (matrix, held) in enumerate(((gate, gate_v), (up, up_v), (down, down_v)))
    ]
    wait_x()
    norm_rows(x, n, gain[...])
    blocks = [pl.ds(at, block) for at in range(0, inner.shape[1], block)]
    waits[0]()
    for columns in blocks:
        opened[:, columns] = dot(n[...], gate_v[:, columns])
    waits[1]()
    for columns in blocks:
        gated = opened[:, columns]
        inner[:, columns] = (gated / (1.0 + jnp.exp(-gated)) * dot(n[...], up_v[:, columns])).astype(BF)
    waits[2]()
    for at in range(0, x.shape[1], block):
        columns = pl.ds(at, block)
        x[:, columns] = dot(inner[...], down_v[:, columns]).astype(BF)
    put_halves(segments, info, x, near, far, sems)


def call(body, outs, specs, scratch, operands, flops, moved, limit):
    return pl.pallas_call(
        body,
        out_shape=[jax.ShapeDtypeStruct(shape, dtype) for shape, dtype, _ in outs],
        in_specs=specs,
        out_specs=[spec for _, _, spec in outs],
        scratch_shapes=scratch,
        compiler_params=pltpu.CompilerParams(vmem_limit_bytes=limit * MIB),
        cost_estimate=pl.CostEstimate(flops=flops // 1000, bytes_accessed=moved // 1000, transcendentals=0),
    )(*operands)


def run_linear(segments, shards, heads, prev, info, own, ups, downs, states, consts, weights, before, deps):
    total = sum(rows for _, rows in segments)
    width = heads * HEAD
    gain, taps, *matrices = weights
    half = (total // 2, D)
    scratch = [
        pltpu.VMEM((total, D), BF),
        pltpu.VMEM((total, D), BF),
        pltpu.VMEM((total, width), BF),
        pltpu.VMEM((2 * HEAD + 2 * width, D), BF),
        pltpu.VMEM((width, D), BF),
        pltpu.VMEM((total, HEAD), BF),
        pltpu.VMEM((prev + total, HEAD), BF),
        pltpu.VMEM((prev + total, width), BF),
        pltpu.VMEM((total, width), BF),
        pltpu.SemaphoreType.DMA((20,)),
        pltpu.SemaphoreType.DMA((3 * heads,)),
        pltpu.SemaphoreType.DMA((heads,)),
    ]
    rows = segments[0][1]
    outs = [(half, BF, ANY)] * 3 + [((rows, HEAD), BF, VMEM), ((rows, width), BF, VMEM), ((16, width), BF, VMEM)]
    operands = [info, own, *ups, *downs, *states, gain, taps, *consts, *matrices, *before, *deps]
    specs = [SMEM] + [ANY] * 7 + [VMEM] * (len(states) + 2 + 3) + [HBM] * 5 + [VMEM] * len(before) + [ANY] * 2
    return call(
        functools.partial(linear_kernel, segments, shards, heads, prev),
        outs, specs, scratch, operands, 2 * total * D * 1792, 12 * MIB, 24,
    )


def run_window(segments, heads, prev, info, parts, states, weights, before, deps):
    total = sum(rows for _, rows in segments)
    width = heads * HEAD
    gain, *matrices = weights
    half = (total // 2, D)
    scratch = [
        pltpu.VMEM((total, D), BF),
        pltpu.VMEM((total, D), BF),
        pltpu.VMEM((3 * width, D), BF),
        pltpu.VMEM((width, D), BF),
        pltpu.VMEM((total, width), BF),
        pltpu.VMEM((total + WIN * len(segments), width), BF),
        pltpu.VMEM((total + WIN * len(segments), width), BF),
        pltpu.VMEM((total, width), BF),
        pltpu.SemaphoreType.DMA((20,)),
        pltpu.SemaphoreType.DMA((3 * heads,)),
        pltpu.SemaphoreType.DMA((heads,)),
    ]
    outs = [(half, BF, ANY)] * 2 + [((8 * len(segments), 128), F32, VMEM)] + [((WIN, width), BF, VMEM)] * 2
    operands = [info, *parts, *states, gain, *matrices, *before, *deps]
    specs = [SMEM] + [ANY] * 4 + [VMEM] * (len(states) + 1) + [HBM] * 4 + [VMEM] * len(before) + [ANY] * 2
    return call(
        functools.partial(window_kernel, segments, heads, prev),
        outs, specs, scratch, operands, 2 * total * D * 2048, 12 * MIB, 24,
    )


def run_hidden(segments, info, parts, weights, deps):
    total = sum(rows for _, rows in segments)
    gain, gate, up, down = weights
    half = (total // 2, D)
    units = gate.shape[1]
    specs = [SMEM] + [ANY] * 4 + [VMEM] + [HBM] * 3 + [ANY] * 2
    scratch = [
        pltpu.VMEM((total, D), BF),
        pltpu.VMEM((total, D), BF),
        pltpu.VMEM((total, units), BF),
        pltpu.VMEM((total, units), F32),
        pltpu.VMEM(gate.shape, BF),
        pltpu.VMEM(up.shape, BF),
        pltpu.VMEM(down.shape, BF),
        pltpu.SemaphoreType.DMA((20,)),
        pltpu.SemaphoreType.DMA((3,)),
    ]
    return call(
        functools.partial(hidden_kernel, segments),
        [(half, BF, ANY)] * 2, specs, scratch, [info, *parts, gain, gate, up, down, *deps],
        2 * total * D * units * 3, 24 * MIB, 36,
    )


def after(value, *others):
    nothing = sum(other[(0,) * other.ndim].astype(F32) * 0.0 for other in others)
    return value + nothing.astype(value.dtype)


INWARD, ACROSS, OUTWARD = [(0, 1), (3, 2)], [(1, 2), (2, 1)], [(1, 0), (2, 3)]


def to_middle(near, far, stay):
    far_in = lax.ppermute(far, "tensor", INWARD)
    near_in = lax.ppermute(near, "tensor", INWARD)
    crossed = lax.ppermute(far + far_in, "tensor", ACROSS)
    return (stay.astype(F32) + (near.astype(F32) + near_in.astype(F32) + crossed.astype(F32))).astype(BF)


SAME = [(0, 0), (3, 3)]


def trailing(other, own_out, other_out):
    trail = lax.ppermute(other[:16, :128], "tensor", SAME)
    trail = lax.ppermute(trail, "tensor", SAME)
    trail = lax.ppermute(trail + own_out[:16, :128], "tensor", SAME)
    return lax.ppermute(trail + other_out[:16, :128], "tensor", SAME)


def first_out(own):
    return lax.ppermute(own, "tensor", ACROSS), lax.ppermute(own, "tensor", OUTWARD)


def pick_axis(array, axis, index):
    return jnp.where(index, lax.index_in_dim(array, 1, axis, False), lax.index_in_dim(array, 0, axis, False))


def pack_kernel(index, folded, tails, keys, values, keep, send, pack, sems):
    slots_here, heads = folded.shape[:2]
    pack[...] = jnp.zeros_like(pack)
    for slot in range(slots_here):
        for head in range(heads):
            wide, narrow = pl.ds(head * HEAD, HEAD), pl.ds(head * HEAD, HS)
            ours = slice(head * HS, (head + 1) * HS)
            pack[slot, pl.ds(0, STATE_KEYS), wide] = folded[slot, head]
            pack[slot, pl.ds(STATE_KEYS, WIN), narrow] = keys[slot, :, ours]
            pack[slot, pl.ds(STATE_VALUES, WIN), narrow] = values[slot, :, ours]
        ends = pl.ds(STATE_KEYS - 16, 16)
        pack[slot, ends, :] = pack[slot, ends, :] + tails[slot]
    made = []
    count = keep.shape[0]
    for number in range(2 * count):
        target = keep if number < count else send
        made.append(pltpu.make_async_copy(pack.at[index[number]], target.at[number % count], sems.at[number]))
        made[-1].start()
    for copy in made:
        copy.wait()


def slot_states(request_group, group_slot, sums, norms, keys, values, tail, count, firsts, seconds):
    here = lax.axis_index("req")
    slots_here, heads = sums.shape[:2]
    width = heads * HEAD
    requests = request_group.shape[0]
    groups = lax.all_gather(request_group, "req", axis=0, tiled=True)
    matches = jnp.arange(group_slot.shape[0])[None, :] == groups[:, None]
    slots = jnp.sum(jnp.where(matches, group_slot[None, :], 0), axis=1)

    fold = jnp.asarray(fold_matrix())
    folded = jnp.einsum("fg,ahgd->ahfd", fold, sums, precision=lax.Precision.HIGHEST).astype(BF)
    folded_norms = jnp.einsum("fg,ahg->ahf", fold, norms, precision=lax.Precision.HIGHEST).astype(BF)
    folded = jnp.concatenate([folded, folded_norms[..., None]], axis=-1)
    folded = jnp.pad(folded, ((0, 0), (0, 0), (0, 0), (0, HEAD - HS - 1)))
    tails = tail.reshape(slots_here, KC - 1, heads, HS)
    tails = jnp.pad(tails, ((0, 0), (0, 0), (0, 0), (0, HEAD - HS))).reshape(slots_here, KC - 1, width)
    tails = jnp.pad(tails, ((0, 0), (1, 16 - KC), (0, 0)))

    bits = []
    while 1 << len(bits) < count:
        bits.append(len(bits))
    local = (slots - here * slots_here).reshape((2,) * len(bits) + (requests,))
    local = jnp.where((local >= 0) & (local < slots_here), local, slots_here)

    def swap(array, bit):
        return lax.ppermute(array, "req", [(i, i ^ (1 << bit)) for i in range(count)])

    def upper(bit):
        return (here >> bit) & 1 == 1

    axis = len(bits) - 1
    entries = count // 2 * requests
    index = [pick_axis(local, axis, upper(0)).reshape(-1), pick_axis(local, axis, ~upper(0)).reshape(-1)]
    index = after(jnp.concatenate(index), *firsts)
    shape = (entries, STATE_ROWS, width)
    keep, send = pl.pallas_call(
        pack_kernel,
        out_shape=[jax.ShapeDtypeStruct(shape, BF)] * 2,
        in_specs=[SMEM] + [VMEM] * 4,
        out_specs=[ANY] * 2,
        scratch_shapes=[
            pltpu.VMEM((slots_here + 1, STATE_ROWS, width), BF),
            pltpu.SemaphoreType.DMA((2 * entries,)),
        ],
        compiler_params=pltpu.CompilerParams(vmem_limit_bytes=12 * MIB),
    )(index, folded, tails, keys, values)
    packs = (keep + swap(send, 0)).reshape((2,) * (len(bits) - 1) + (requests, STATE_ROWS, width))
    halves = []
    cut = STATE_ROWS // 2
    for number in range(2):
        part = packs[..., number * cut : (number + 1) * cut, :]
        left = bits[1:]
        order = left if number == 0 else left[::-1]
        while order:
            bit, order = order[0], order[1:]
            axis = len(left) - 1 - left.index(bit)
            left = [b for b in left if b != bit]
            if not order:
                part = after(part, *seconds)
            part = pick_axis(part, axis, upper(bit)) + swap(pick_axis(part, axis, ~upper(bit)), bit)
        halves.append(part)
    return jnp.concatenate(halves, axis=1)


def make_line(req_count):
    def per_device(
        hidden,
        suffix_len,
        request_group,
        group_slot,
        norm_first,
        query_weight,
        key_weight,
        value_weight,
        filter_gate,
        filter_taps,
        linear_out,
        norm_second,
        window_query,
        window_key,
        window_value,
        window_out,
        norm_third,
        gate_weight,
        up_weight,
        down_weight,
        prefix_sums,
        prefix_norms,
        prefix_keys,
        prefix_values,
        prefix_tail,
    ):
        requests = hidden.shape[0]
        heads = prefix_sums.shape[1]
        share = hidden.shape[1]
        here = lax.axis_index("tensor")
        low = here < 2
        middle = (here == 1) | (here == 2)

        both = (suffix_len[0] > SHORT) & (suffix_len[1] > SHORT)
        long = jnp.where(both, 0, (suffix_len[1] > SHORT).astype(jnp.int32))
        short = 1 - long

        ups, downs = [], []
        up = down = hidden
        for step in range(1, 4):
            up = lax.ppermute(up, "tensor", [(i, i + 1) for i in range(step - 1, 3)])
            down = lax.ppermute(down, "tensor", [(i + 1, i) for i in range(4 - step)])
            ups.append(up)
            downs.append(down)
        states = slot_states(
            request_group, group_slot, prefix_sums, prefix_norms, prefix_keys, prefix_values, prefix_tail, req_count,
            (ups[0], downs[0]), (ups[1], downs[1]),
        )

        def wide(matrix):
            matrix = matrix.reshape(matrix.shape[0], heads, HS)
            return jnp.pad(matrix, ((0, 0), (0, 0), (0, HEAD - HS))).reshape(matrix.shape[0], heads * HEAD)

        linear_weights = (
            norm_first[None],
            jnp.pad(wide(filter_taps), ((0, 8 - KC), (0, 0))),
            query_weight.T,
            key_weight.T,
            value_weight.T,
            filter_gate.T,
            linear_out,
        )
        window_weights = (norm_second[None], window_query.T, window_key.T, window_value.T, window_out)
        hidden_weights = (norm_third[None], gate_weight, up_weight, down_weight)
        left, right, plus = feature_maps(heads)
        consts = (jnp.asarray(left, BF), jnp.asarray(right, BF), jnp.asarray(plus))

        place = [here, low.astype(jnp.int32), middle.astype(jnp.int32), here * 0]
        quarters = tuple((0, s, s * share, share) for s in range(4))
        rows_here = here * share + jnp.arange(share)

        def info(indices):
            indices = [jnp.int32(0) + index for index in indices] * 2
            lengths = [suffix_len[index] for index in indices[:2]]
            return jnp.stack(place + indices[:2] + lengths).astype(jnp.int32)

        def run(streams, segments, shards):
            count = len(streams)
            infos = [info(indices) for indices in streams]
            parts, own, tops = [None] * count, [None] * count, [None] * count
            trails = [None] * count
            waiting = None
            dep = hidden
            for layer in range(3):
                for number, indices in enumerate(streams):
                    mine = [states[index] for index in indices]
                    if waiting is not None and count > 1:
                        late, late_own = waiting
                        other, own_out = first_out(late_own)
                    elif layer > 0:
                        other, own_out = first_out(own[number])
                        parts[number] = (own[number], own_out, other, lax.ppermute(other, "tensor", OUTWARD))
                    deps = (dep, dep if layer == 0 or count == 1 else trails[number])
                    if layer == 0:
                        near, far, stay, *_ = run_linear(
                            segments, shards, heads, 0, infos[number], hidden, ups, downs,
                            mine, consts, linear_weights, [], deps,
                        )
                    elif layer == 1:
                        stay = own[number]
                        near, far, tops[number], *_ = run_window(
                            segments, heads, 0, infos[number], parts[number], mine, window_weights, [], deps
                        )
                    else:
                        stay = own[number]
                        near, far = run_hidden(segments, infos[number], parts[number], hidden_weights, deps)
                    if waiting is not None and count > 1:
                        parts[late] = (late_own, own_out, other, lax.ppermute(other, "tensor", OUTWARD))
                        trails[late] = trailing(other, own_out, parts[late][3])
                    own[number] = to_middle(near, far, stay)
                    dep = own[number]
                    waiting = (number, own[number]) if layer < 2 else None
            return own, tops

        def live(rows, length):
            return jnp.where((rows_here < length)[:, None], rows, jnp.zeros_like(rows))

        half_row = jnp.where(low, 0, LMAX // 2)

        def square_sum(rows, first, length):
            floats = rows.astype(F32)
            counted = middle & (first + jnp.arange(rows.shape[0]) < length)
            return jnp.sum(jnp.where(counted[:, None], floats * floats, 0.0))

        def all_long():
            own, tops = run([(0,), (1,)], ((0, LMAX),), quarters)
            outs, squares = [], []
            for request in range(requests):
                squares.append(square_sum(own[request], half_row, suffix_len[request]))
                first, second = own[request][:share], own[request][share:]
                moved = lax.ppermute(jnp.where(low, first, second), "tensor", OUTWARD)
                outs.append(live(jnp.where(middle, jnp.where(low, second, first), moved), suffix_len[request]))
            return jnp.stack(outs), jnp.stack(squares + [top[0, 0] for top in tops])

        def one_long():
            own, tops = run(
                [(long, short)], ((0, LMAX), (LMAX, SHORT)), quarters + ((1, 0, LMAX, SHORT),)
            )
            own, top = own[0], tops[0]
            first, second, last = own[:share], own[share : 2 * share], own[2 * share :]
            moved = lax.ppermute(jnp.concatenate([jnp.where(low, first, second), last]), "tensor", OUTWARD)
            rest = lax.ppermute(last, "tensor", [(2, 0)])
            mine = jnp.where(middle, jnp.where(low, second, first), moved[:share])
            long_out = live(mine, suffix_len[long])
            mine = jnp.concatenate([moved[share:], rest, jnp.zeros((share - SHORT, D), BF)])
            short_out = live(mine, suffix_len[short])
            long_square = square_sum(own[: 2 * share], half_row, suffix_len[long])
            short_square = square_sum(last, jnp.where(low, 0, SHORT // 2), suffix_len[short])

            def ordered(of_long, of_short):
                return [jnp.where(long == request, of_long, of_short) for request in range(2)]

            return (
                jnp.stack(ordered(long_out, short_out)),
                jnp.stack(ordered(long_square, short_square) + ordered(top[0, 0], top[8, 0])),
            )

        outs, scalars = lax.cond(both, all_long, one_long)
        scalars = jnp.broadcast_to(scalars[:, None], (2 * requests, 128))
        everyone = [scalars] + [
            lax.ppermute(scalars, "tensor", [(i, (i + step) % 4) for i in range(4)]) for step in (1, 2, 3)
        ]
        total = sum(each[:requests, 0] for each in everyone)
        top_logit = functools.reduce(jnp.maximum, [each[requests:, 0] for each in everyone])
        return outs, jnp.sqrt(total / D), top_logit

    return per_device


def folded_features(queries):
    floats = jnp.transpose(queries.astype(F32), (1, 0, 2))
    parts = [jnp.ones(floats.shape[:-1] + (1,), F32), floats * FD ** (-0.25)]
    for shift in range(PAIRS):
        parts.append(floats * jnp.roll(floats, -shift, axis=-1) * (2.0 * FD) ** (-0.5))
    return jnp.concatenate(parts, axis=-1)


def plain_fold_matrix():
    row = jnp.arange(1 + FD + PAIRS * FD)[:, None]
    column = jnp.arange(1 + FD + FD * FD)[None, :]
    shift, first = (row - 1 - FD) // FD, (row - 1 - FD) % FD
    second = (first + shift) % FD
    major, minor = (column - 1 - FD) // FD, (column - 1 - FD) % FD
    straight = (major == first) & (minor == second)
    swapped = (major == second) & (minor == first) & (shift > 0) & (shift < FD // 2)
    squares = (row > FD) & (column > FD) & (straight | swapped)
    return jnp.where((row == column) & (row <= FD) | squares, 1.0, 0.0).astype(F32)


def line_gather(rows, axis, count):
    here = lax.axis_index(axis)
    size = rows.shape[0]
    up = down = rows
    ups, downs = [], []
    for step in range(1, count):
        up = lax.ppermute(up, axis, [(i, i + 1) for i in range(step - 1, count - 1)])
        down = lax.ppermute(down, axis, [(i + 1, i) for i in range(count - step)])
        ups.append(up)
        downs.append(down)
    around = jnp.concatenate(ups[::-1] + [rows] + downs)
    return lax.dynamic_slice_in_dim(around, (count - 1 - here) * size, count * size, 0)


def line_scatter(partial, axis, count):
    here = lax.axis_index(axis)
    size = partial.shape[0] // count

    def block(index):
        return lax.dynamic_slice_in_dim(partial, index * size, size, 0)

    up = down = None
    for step in range(1, count):
        to_up = block(jnp.minimum(here + count - step, count - 1))
        to_down = block(jnp.maximum(here - count + step, 0))
        if up is not None:
            to_up, to_down = to_up + up, to_down + down
        up = lax.ppermute(to_up, axis, [(i, i + 1) for i in range(step)])
        down = lax.ppermute(to_down, axis, [(i + 1, i) for i in range(count - 1 - step, count - 1)])
    return block(here).astype(F32) + up.astype(F32) + down.astype(F32)


def settle(partial, stream, axis, count):
    here = lax.axis_index(axis)
    size = partial.shape[0] // count
    mine = lax.dynamic_slice_in_dim(stream, here * size, size, 0)
    total = line_scatter(partial, axis, count)
    return line_gather((mine.astype(F32) + total).astype(BF), axis, count)


def bring_home(packs, axis, count):
    here = lax.axis_index(axis)
    bit = 1
    while bit < count:
        pairs = packs.reshape((packs.shape[0] // 2, 2) + packs.shape[1:])
        upper = (here & bit) != 0
        keep = jnp.where(upper, pairs[:, 1], pairs[:, 0])
        send = jnp.where(upper, pairs[:, 0], pairs[:, 1])
        packs = keep + lax.ppermute(send, axis, [(i, i ^ bit) for i in range(count)])
        bit *= 2
    return packs[0]


def make_plain(req_count, tensor_count):
    def per_device(
        hidden,
        suffix_len,
        request_group,
        group_slot,
        norm_first,
        query_weight,
        key_weight,
        value_weight,
        filter_gate,
        filter_taps,
        linear_out,
        norm_second,
        window_query,
        window_key,
        window_value,
        window_out,
        norm_third,
        gate_weight,
        up_weight,
        down_weight,
        prefix_sums,
        prefix_norms,
        prefix_keys,
        prefix_values,
        prefix_tail,
    ):
        requests_here = hidden.shape[0]
        share_rows = hidden.shape[1]
        slots_here, heads = prefix_sums.shape[:2]
        width = heads * HS

        groups = lax.all_gather(request_group, "req", axis=0, tiled=True)
        matches = jnp.arange(group_slot.shape[0])[None, :] == groups[:, None]
        slots = jnp.sum(jnp.where(matches, group_slot[None, :], 0), axis=1)
        fold = plain_fold_matrix()
        sums = jnp.einsum("fg,ahgd->afhd", fold, prefix_sums, precision=lax.Precision.HIGHEST)
        terms = sums.shape[1]
        norms = jnp.einsum("fg,ahg->afh", fold, prefix_norms, precision=lax.Precision.HIGHEST)
        norms = jnp.pad(norms.reshape(slots_here, -1), ((0, 0), (0, 2 * width - terms * heads)))
        pack = jnp.concatenate(
            [
                sums.reshape(slots_here, terms, width).astype(BF),
                norms.reshape(slots_here, 2, width).astype(BF),
                prefix_keys,
                prefix_values,
                prefix_tail,
            ],
            axis=1,
        )
        rows = pack.shape[1]
        pack = jnp.pad(pack, ((0, 0), (0, -rows % 32), (0, 0)))
        half = pack.shape[1] // 2
        pack = jnp.concatenate([pack[:, :half], pack[:, half:]], axis=2)
        local = slots - lax.axis_index("req") * slots_here
        owned = (local >= 0) & (local < slots_here)
        sent = jnp.take(pack, jnp.clip(local, 0, slots_here - 1), axis=0)
        sent = jnp.where(owned[:, None, None], sent, jnp.zeros_like(sent))
        sent = sent.reshape((req_count, requests_here) + sent.shape[1:])
        states = bring_home(sent, "req", req_count)
        states = jnp.concatenate([states[:, :, :width], states[:, :, width:]], axis=1)

        position = jnp.arange(LMAX)
        causal = position[:, None] >= position[None, :]
        bands = LMAX // WIN
        band_row = jnp.arange(WIN)[:, None]
        band_key = jnp.arange(2 * WIN)[None, :]
        allowed = (band_key > band_row) & (band_key <= band_row + WIN)

        def linear_part(request, stream):
            state = states[request]
            state_sums = state[:terms].reshape(terms, heads, HS)
            state_norms = state[terms : terms + 2].reshape(-1)[: terms * heads].reshape(terms, heads)
            tail = state[terms + 2 + 2 * WIN : terms + 2 + 2 * WIN + KC - 1]
            normed = rms_norm(stream, norm_first)
            queries = dot(normed, query_weight).astype(BF).reshape(LMAX, heads, FD)
            key_rows = dot(normed, key_weight).astype(BF).reshape(LMAX, heads, FD)
            values = dot(normed, value_weight).astype(BF)
            gating = dot(normed, filter_gate).astype(BF)
            extended = jnp.concatenate([tail, values], axis=0).astype(F32)
            convolved = sum(
                filter_taps[offset] * extended[KC - 1 - offset : KC - 1 - offset + LMAX]
                for offset in range(KC)
            )
            mixed = (convolved * jax.nn.silu(gating.astype(F32))).astype(BF)
            mixed = mixed.reshape(LMAX, heads, HS)
            scores = jnp.einsum("thf,shf->hts", queries, key_rows, preferred_element_type=F32)
            scores = scores * FD ** (-0.5)
            weights = jnp.where(causal, 1.0 + scores + 0.5 * scores * scores, 0.0)
            mapped = folded_features(queries)
            numerator = jnp.einsum(
                "hts,shd->thd", weights.astype(BF), mixed, preferred_element_type=F32
            ) + jnp.einsum(
                "htf,fhd->thd", mapped.astype(BF), state_sums, preferred_element_type=F32
            )
            denominator = jnp.sum(weights, axis=-1) + jnp.sum(
                mapped * jnp.transpose(state_norms).astype(F32)[:, None, :], axis=-1
            )
            linear_rows = (numerator / jnp.transpose(denominator)[..., None]).astype(BF)
            return dot(linear_rows.reshape(LMAX, width), linear_out).astype(BF)

        def window_part(request, stream):
            state = states[request]
            normed = rms_norm(stream, norm_second)
            queries = dot(normed, window_query).astype(BF).reshape(bands, WIN, heads, HS)
            key_rows = dot(normed, window_key).astype(BF)
            value_rows = dot(normed, window_value).astype(BF)
            start = terms + 2

            def paired(prefix, rows):
                blocks = jnp.concatenate([prefix, rows]).reshape(bands + 1, WIN, heads, HS)
                return jnp.concatenate([blocks[:-1], blocks[1:]], axis=1)

            key_pairs = paired(state[start : start + WIN], key_rows)
            value_pairs = paired(state[start + WIN : start + 2 * WIN], value_rows)
            logits = jnp.einsum(
                "bthd,bphd->bhtp", queries, key_pairs, preferred_element_type=F32
            ) * HS ** (-0.5)
            logits = jnp.where(allowed, logits, -jnp.inf)
            row_max = jnp.max(logits, axis=-1, keepdims=True)
            exponent = jnp.exp(logits - row_max)
            chances = (exponent / jnp.sum(exponent, axis=-1, keepdims=True)).astype(BF)
            attended = jnp.einsum(
                "bhtp,bphd->bthd", chances, value_pairs, preferred_element_type=F32
            ).astype(BF)
            final = (position == suffix_len[request] - 1).reshape(bands, 1, WIN)
            top = jnp.max(jnp.where(final, row_max[..., 0], -jnp.inf))
            return dot(attended.reshape(LMAX, width), window_out).astype(BF), top

        def hidden_part(stream):
            normed = rms_norm(stream, norm_third)
            inner = (jax.nn.silu(dot(normed, gate_weight)) * dot(normed, up_weight)).astype(BF)
            return dot(inner, down_weight).astype(BF)

        here = lax.axis_index("tensor")
        row_start = here * share_rows
        rows_here = row_start + jnp.arange(share_rows)
        outs, squares, tops = [], [], []
        for request in range(requests_here):
            stream = line_gather(hidden[request], "tensor", tensor_count)
            partial = linear_part(request, stream)
            stream = settle(partial, stream, "tensor", tensor_count)
            partial, top = window_part(request, stream)
            stream = settle(partial, stream, "tensor", tensor_count)
            partial = hidden_part(stream)
            total = line_scatter(partial, "tensor", tensor_count)
            mine = lax.dynamic_slice_in_dim(stream, row_start, share_rows, 0).astype(F32)
            mine = (mine + total).astype(BF)
            live = (rows_here < suffix_len[request])[:, None]
            outs.append(jnp.where(live, mine, jnp.zeros_like(mine)))
            floats = mine.astype(F32)
            squares.append(jnp.sum(jnp.where(live, floats * floats, 0.0)))
            tops.append(top)
        scalars = lax.all_gather(jnp.stack(squares + tops), "tensor")
        total = jnp.sum(scalars[:, :requests_here], axis=0)
        top_logit = jnp.max(scalars[:, requests_here:], axis=0)
        return jnp.stack(outs), jnp.sqrt(total / D), top_logit

    return per_device


def solution(mesh):
    return jax.shard_map(
        make_line(mesh.shape["req"]) if mesh.shape["tensor"] == 4 else make_plain(mesh.shape["req"], mesh.shape["tensor"]),
        mesh=mesh,
        in_specs=(
            P("req", "tensor", None),
            P("req"),
            P("req"),
            P(),
            P(),
            P(None, "tensor"),
            P(None, "tensor"),
            P(None, "tensor"),
            P(None, "tensor"),
            P(None, "tensor"),
            P("tensor", None),
            P(),
            P(None, "tensor"),
            P(None, "tensor"),
            P(None, "tensor"),
            P("tensor", None),
            P(),
            P(None, "tensor"),
            P(None, "tensor"),
            P("tensor", None),
            P("req", "tensor", None, None),
            P("req", "tensor", None),
            P("req", None, "tensor"),
            P("req", None, "tensor"),
            P("req", None, "tensor"),
        ),
        out_specs=(P("req", "tensor", None), P("req"), P("req")),
        check_vma=False,
    )
```

```python
import functools

import jax
import jax.numpy as jnp
import numpy as np
from jax import lax
from jax.experimental import pallas as pl
from jax.experimental.pallas import tpu as pltpu
from jax.sharding import PartitionSpec as P

D = 1792
FD = 16
HS = 112
WIN = 64
KC = 3
LMAX = 512
SHORT = 32
PAIRS = FD // 2 + 1
SQUARES = PAIRS * FD
FEATURES = 256
HEAD = 128
STATE_KEYS = 176
STATE_VALUES = STATE_KEYS + WIN
STATE_ROWS = STATE_VALUES + WIN

EPS = 1e-05
BF = jnp.bfloat16
F32 = jnp.float32
MIB = 1 << 20
ANY = pl.BlockSpec(memory_space=pl.ANY)
SMEM = pl.BlockSpec(memory_space=pltpu.SMEM)
VMEM = pl.BlockSpec(memory_space=pltpu.VMEM)
HBM = pl.BlockSpec(memory_space=pltpu.HBM)


def rms_norm(rows, gain):
    floats = rows.astype(F32)
    inverse_rms = lax.rsqrt(jnp.mean(floats * floats, axis=-1, keepdims=True) + EPS)
    return (floats * inverse_rms * gain).astype(BF)


def dot(left, right):
    return jnp.dot(left, right, preferred_element_type=F32)


def dot_t(left, right):
    return lax.dot_general(left, right, (((1,), (1,)), ((), ())), preferred_element_type=F32)


def fold_matrix():
    fold = np.zeros((STATE_KEYS, 1 + FD + FD * FD), np.float32)
    for shift in range(PAIRS):
        for i in range(FD):
            j = (i + shift) % FD
            fold[shift * FD + i, 1 + FD + i * FD + j] = 1.0
            if 0 < shift < FD // 2:
                fold[shift * FD + i, 1 + FD + j * FD + i] = 1.0
    for i in range(FD):
        fold[SQUARES + i, 1 + i] = 1.0
    fold[SQUARES + FD, 0] = 1.0
    return fold


def feature_maps(heads):
    left = np.zeros((heads, HEAD, FEATURES), np.float32)
    right = np.zeros((heads, HEAD, FEATURES), np.float32)
    plus = np.zeros((8, FEATURES), np.float32)
    for head in range(heads):
        for i in range(FD):
            for shift in range(PAIRS):
                left[head, head * FD + i, shift * FD + i] = 1.0
                right[head, head * FD + (i + shift) % FD, shift * FD + i] = 1.0
            left[head, head * FD + i, SQUARES + i] = 1.0
    plus[1, SQUARES : SQUARES + FD] = 1.0
    plus[0:2, SQUARES + FD] = 1.0
    plus[2, :SQUARES] = (2.0 * FD) ** (-0.5)
    plus[2, SQUARES : SQUARES + FD] = FD ** (-0.25)
    plus[2, SQUARES + FD] = 1.0
    return left, right, plus


def copies(plan, sems):
    made = []
    for number, (condition, source, target) in enumerate(plan):
        copy = pltpu.make_async_copy(source, target, sems.at[number])
        copy.start() if condition is True else pl.when(condition)(copy.start)
        made.append((condition, copy))

    def wait():
        for condition, copy in made:
            copy.wait() if condition is True else pl.when(condition)(copy.wait)

    return wait


def head_rows(source, target, first, heads):
    return [
        (True, source.at[pl.ds(head * HS, HS)], target.at[pl.ds(first + head * HEAD, HS)]) for head in range(heads)
    ]


def clear(target, pieces):
    for start, rows in pieces:
        target[pl.ds(start, rows), :] = jnp.zeros((rows, target.shape[1]), target.dtype)


def half_pieces(segments):
    pieces = ([], [])
    buffer_row = 0
    for start, rows in segments:
        for half in range(2):
            pieces[half].append((start + half * rows // 2, rows // 2, buffer_row))
        buffer_row += rows // 2
    return pieces, buffer_row


def put_halves(segments, info, source, near, far, sems):
    pieces, _ = half_pieces(segments)
    plan = []
    for half in range(2):
        for natural, rows, at in pieces[half]:
            for low in (0, 1):
                target = near if half == 1 - low else far
                plan.append((info[1] == low, source.at[pl.ds(natural, rows)], target.at[pl.ds(at, rows)]))
    copies(plan, sems)()


def halves_plan(segments, info, own, own_out, other, other_out, target):
    pieces, _ = half_pieces(segments)
    plan = []
    for low in (0, 1):
        for middle in (0, 1):
            near, far = (own, other) if middle else (own_out, other_out)
            for half in range(2):
                source = near if half == 1 - low else far
                for natural, rows, at in pieces[half]:
                    plan.append(
                        (
                            (info[1] == low) & (info[2] == middle),
                            source.at[pl.ds(at, rows)],
                            target.at[pl.ds(natural, rows)],
                        )
                    )
    return plan


def norm_rows(x, n, gain):
    rows = x.shape[0]
    for at in range(0, rows, 128):
        size = min(128, rows - at)
        n[pl.ds(at, size), :] = rms_norm(x[pl.ds(at, size), :], gain)


def lane_of_ones(shape):
    return (lax.broadcasted_iota(jnp.int32, shape, 1) & (HEAD - 1)) == HS


def linear_kernel(segments, shards, heads, prev, *refs):
    refs = list(refs)
    info, own, ups, downs = refs[0], refs[1], refs[2:5], refs[5:8]
    states = refs[8 : 8 + len(segments)]
    refs = refs[8 + len(segments) :]
    gain, taps, left, right, plus = refs[:5]
    query_weight, key_weight, value_weight, gate_weight, out_weight = refs[5:10]
    refs = refs[10:]
    if prev:
        prev_key, prev_mixed, prev_value = refs[:3]
        refs = refs[3:]
    refs = refs[2:]
    near, far, stay, key_out, mixed_out, value_out = refs[:6]
    x, n, u, w, ow, q, k, m, y, sems, wsems, osems = refs[6:]
    width = heads * HEAD
    total = x.shape[0]
    plan = []
    for segment, shard, row, rows in shards:
        for here in range(4):
            source = own if here == shard else (ups[here - shard - 1] if here > shard else downs[shard - here - 1])
            plan.append(
                (
                    info[0] == here,
                    source.at[info[4 + segment], pl.ds(0, rows)],
                    x.at[pl.ds(row, rows)],
                )
            )
    wait_x = copies(plan, sems)
    plan = [(True, query_weight, w.at[pl.ds(0, heads * FD)]), (True, key_weight, w.at[pl.ds(HEAD, heads * FD)])]
    plan += head_rows(value_weight, w, 2 * HEAD, heads) + head_rows(gate_weight, w, 2 * HEAD + width, heads)
    wait_w = copies(plan, wsems)
    wait_out = copies(head_rows(out_weight, ow, 0, heads), osems)
    clear(w, [(heads * FD, HEAD - heads * FD), (HEAD + heads * FD, HEAD - heads * FD)])
    clear(w, [(2 * HEAD + HS + HEAD * head, HEAD - HS) for head in range(2 * heads)])
    clear(ow, [(HS + HEAD * head, HEAD - HS) for head in range(heads)])
    if prev:
        k[pl.ds(0, prev), :] = prev_key[...]
        m[pl.ds(0, prev), :] = prev_mixed[...]
    wait_x()
    norm_rows(x, n, gain[...])
    wait_w()
    q[...] = dot_t(n[...], w[:HEAD]).astype(BF)
    k[pl.ds(prev, total), :] = dot_t(n[...], w[HEAD : 2 * HEAD]).astype(BF)
    y[...] = dot_t(n[...], w[2 * HEAD : 2 * HEAD + width]).astype(BF)
    u[...] = dot_t(n[...], w[2 * HEAD + width :]).astype(BF)
    tap = taps[...]
    for number, (start, rows) in enumerate(segments):
        base = prev if number == 0 else 0
        tile = min(rows, 256)
        if base:
            ends = prev_value[...].astype(F32)
            last2, last = ends[14:15], ends[15:16]
        else:
            ends = states[number][pl.ds(SQUARES + FD, 16), :].astype(F32)
            last2, last = ends[1:2], ends[2:3]
        for at in range(start, start + rows, tile):
            v = y[pl.ds(at, tile), :].astype(F32)
            opened = u[pl.ds(at, tile), :].astype(F32)
            row = lax.broadcasted_iota(jnp.int32, v.shape, 0)
            back1 = jnp.where(row == 0, last, pltpu.roll(v, 1, 0))
            back2 = jnp.where(row == 0, last2, jnp.where(row == 1, last, pltpu.roll(v, 2, 0)))
            last2, last = v[tile - 2 : tile - 1], v[tile - 1 : tile]
            convolved = tap[0:1] * v + tap[1:2] * back1 + tap[2:3] * back2
            mixed = convolved * (opened / (1.0 + jnp.exp(-opened)))
            m[pl.ds(prev + at, tile), :] = jnp.where(lane_of_ones(v.shape), 1.0, mixed).astype(BF)
            if number == 0 and at + tile == start + rows:
                value_out[...] = v[tile - 16 :].astype(BF)
    wait_out()
    for number, (start, rows) in enumerate(segments):
        base = prev if number == 0 else 0
        tile = min(rows, 256)
        first = 0 if number == 0 else prev + start
        for at in range(start, start + rows, tile):
            queries = q[pl.ds(at, tile), :]
            lane = lax.broadcasted_iota(jnp.int32, queries.shape, 1)
            for head in range(heads):
                columns = pl.ds(head * HEAD, HEAD)
                mapped = (
                    (dot(queries, left[head]) + plus[0:1, :])
                    * (dot(queries, right[head]) + plus[1:2, :])
                    * plus[2:3, :]
                )
                total_rows = dot(mapped.astype(BF), states[number][pl.ds(0, FEATURES), columns])
                own_lanes = (lane >= head * FD) & (lane < (head + 1) * FD)
                masked = jnp.where(own_lanes, queries, jnp.zeros_like(queries))
                for key_at in range(first, prev + at + tile, tile):
                    a = dot_t(masked, k[pl.ds(key_at, tile), :]) * FD ** (-0.5)
                    weights = 1.0 + a + 0.5 * a * a
                    if key_at == prev + at:
                        causal = lax.broadcasted_iota(jnp.int32, a.shape, 0) >= lax.broadcasted_iota(
                            jnp.int32, a.shape, 1
                        )
                        weights = jnp.where(causal, weights, 0.0)
                    total_rows += dot(weights.astype(BF), m[pl.ds(key_at, tile), columns])
                y[pl.ds(at, tile), columns] = (total_rows / total_rows[:, HS : HS + 1]).astype(BF)
    key_out[...] = k[pl.ds(prev, key_out.shape[0]), :]
    mixed_out[...] = m[pl.ds(prev, mixed_out.shape[0]), :]
    pieces, _ = half_pieces(segments)
    plan = []
    for low in (0, 1):
        for natural, rows, at in pieces[1 - low]:
            plan.append((info[1] == low, x.at[pl.ds(natural, rows)], stay.at[pl.ds(at, rows)]))
    copies(plan, sems)()
    x[...] = dot(y[...], ow[...]).astype(BF)
    put_halves(segments, info, x, near, far, sems)


def window_kernel(segments, heads, prev, *refs):
    refs = list(refs)
    info, own, own_out, other, other_out = refs[:5]
    states = refs[5 : 5 + len(segments)]
    refs = refs[5 + len(segments) :]
    gain, query_weight, key_weight, value_weight, out_weight = refs[:5]
    refs = refs[5:]
    if prev:
        prev_keys, prev_values = refs[:2]
        refs = refs[2:]
    refs = refs[2:]
    near, far, top, key_out, value_out = refs[:5]
    x, n, w, ow, q, k, v, y, sems, wsems, osems = refs[5:]
    width = heads * HEAD
    wait_x = copies(halves_plan(segments, info, own, own_out, other, other_out, x), sems)
    plan = head_rows(query_weight, w, 0, heads)
    plan += head_rows(key_weight, w, width, heads) + head_rows(value_weight, w, 2 * width, heads)
    wait_w = copies(plan, wsems)
    wait_out = copies(head_rows(out_weight, ow, 0, heads), osems)
    clear(w, [(HS + HEAD * head, HEAD - HS) for head in range(3 * heads)])
    clear(ow, [(HS + HEAD * head, HEAD - HS) for head in range(heads)])
    wait_x()
    norm_rows(x, n, gain[...])
    wait_w()
    q[...] = dot_t(n[...], w[:width]).astype(BF)
    new_keys = dot_t(n[...], w[width : 2 * width]).astype(BF)
    for number, (start, rows) in enumerate(segments):
        k[pl.ds(start + WIN * (number + 1), rows), :] = new_keys[start : start + rows]
    new_values = dot_t(n[...], w[2 * width :])
    new_values = jnp.where(lane_of_ones(new_values.shape), 1.0, new_values).astype(BF)
    for number, (start, rows) in enumerate(segments):
        v[pl.ds(start + WIN * (number + 1), rows), :] = new_values[start : start + rows]
    best = []
    for number, (start, rows) in enumerate(segments):
        shift = WIN * (number + 1)
        if prev and number == 0:
            k[pl.ds(0, WIN), :] = prev_keys[...]
            v[pl.ds(0, WIN), :] = prev_values[...]
        else:
            old = states[number][pl.ds(STATE_VALUES, WIN), :]
            k[pl.ds(start + shift - WIN, WIN), :] = states[number][pl.ds(STATE_KEYS, WIN), :]
            v[pl.ds(start + shift - WIN, WIN), :] = jnp.where(
                lane_of_ones(old.shape), jnp.ones_like(old), old
            )
        final = info[6 + number] - 1
        tile = min(rows, 128)
        best_here = jnp.full((1, 1), -jnp.inf, F32)
        for at in range(start, start + rows, tile):
            keys_here = tile + WIN
            row = lax.broadcasted_iota(jnp.int32, (tile, keys_here), 0)
            place = lax.broadcasted_iota(jnp.int32, (tile, keys_here), 1)
            allowed = (place > row) & (place <= row + WIN)
            for head in range(heads):
                columns = pl.ds(head * HEAD, HEAD)
                e = dot_t(q[pl.ds(at, tile), columns], k[pl.ds(shift - WIN + at, keys_here), columns])
                e = jnp.where(allowed, e * HS ** (-0.5), -jnp.inf)
                row_max = jnp.max(e, axis=-1, keepdims=True)
                chances = jnp.exp(e - row_max).astype(BF)
                o = dot(chances, v[pl.ds(shift - WIN + at, keys_here), columns])
                y[pl.ds(at, tile), columns] = (o / o[:, HS : HS + 1]).astype(BF)
                at_final = lax.broadcasted_iota(jnp.int32, row_max.shape, 0) + (at - start) == final
                best_here = jnp.maximum(
                    best_here, jnp.max(jnp.where(at_final, row_max, -jnp.inf), axis=0, keepdims=True)
                )
        best.append(best_here)
    end = segments[0][1]
    key_out[...] = k[pl.ds(end, WIN), :]
    value_out[...] = v[pl.ds(end, WIN), :]
    for number in range(len(segments)):
        top[pl.ds(number * 8, 8), :] = jnp.broadcast_to(best[number], (8, 128))
    wait_out()
    x[...] = dot(y[...], ow[...]).astype(BF)
    put_halves(segments, info, x, near, far, sems)


def hidden_kernel(segments, *refs):
    info, own, own_out, other, other_out, gain, gate, up, down, _, _, near, far = refs[:13]
    x, n, inner, opened, gate_v, up_v, down_v, sems, wsems = refs[13:]
    block = 256
    wait_x = copies(halves_plan(segments, info, own, own_out, other, other_out, x), sems)
    waits = [
        copies([(True, matrix, held)], wsems.at[pl.ds(number, 1)])
        for number, (matrix, held) in enumerate(((gate, gate_v), (up, up_v), (down, down_v)))
    ]
    wait_x()
    norm_rows(x, n, gain[...])
    blocks = [pl.ds(at, block) for at in range(0, inner.shape[1], block)]
    waits[0]()
    for columns in blocks:
        opened[:, columns] = dot(n[...], gate_v[:, columns])
    waits[1]()
    for columns in blocks:
        gated = opened[:, columns]
        inner[:, columns] = (gated / (1.0 + jnp.exp(-gated)) * dot(n[...], up_v[:, columns])).astype(BF)
    waits[2]()
    for at in range(0, x.shape[1], block):
        columns = pl.ds(at, block)
        x[:, columns] = dot(inner[...], down_v[:, columns]).astype(BF)
    put_halves(segments, info, x, near, far, sems)


def call(body, outs, specs, scratch, operands, flops, moved, limit):
    return pl.pallas_call(
        body,
        out_shape=[jax.ShapeDtypeStruct(shape, dtype) for shape, dtype, _ in outs],
        in_specs=specs,
        out_specs=[spec for _, _, spec in outs],
        scratch_shapes=scratch,
        compiler_params=pltpu.CompilerParams(vmem_limit_bytes=limit * MIB),
        cost_estimate=pl.CostEstimate(flops=flops // 1000, bytes_accessed=moved // 1000, transcendentals=0),
    )(*operands)


def run_linear(segments, shards, heads, prev, info, own, ups, downs, states, consts, weights, before, deps):
    total = sum(rows for _, rows in segments)
    width = heads * HEAD
    gain, taps, *matrices = weights
    half = (total // 2, D)
    scratch = [
        pltpu.VMEM((total, D), BF),
        pltpu.VMEM((total, D), BF),
        pltpu.VMEM((total, width), BF),
        pltpu.VMEM((2 * HEAD + 2 * width, D), BF),
        pltpu.VMEM((width, D), BF),
        pltpu.VMEM((total, HEAD), BF),
        pltpu.VMEM((prev + total, HEAD), BF),
        pltpu.VMEM((prev + total, width), BF),
        pltpu.VMEM((total, width), BF),
        pltpu.SemaphoreType.DMA((20,)),
        pltpu.SemaphoreType.DMA((3 * heads,)),
        pltpu.SemaphoreType.DMA((heads,)),
    ]
    rows = segments[0][1]
    outs = [(half, BF, ANY)] * 3 + [((rows, HEAD), BF, VMEM), ((rows, width), BF, VMEM), ((16, width), BF, VMEM)]
    operands = [info, own, *ups, *downs, *states, gain, taps, *consts, *matrices, *before, *deps]
    specs = [SMEM] + [ANY] * 7 + [VMEM] * (len(states) + 2 + 3) + [HBM] * 5 + [VMEM] * len(before) + [ANY] * 2
    return call(
        functools.partial(linear_kernel, segments, shards, heads, prev),
        outs, specs, scratch, operands, 2 * total * D * 1792, 12 * MIB, 24,
    )


def run_window(segments, heads, prev, info, parts, states, weights, before, deps):
    total = sum(rows for _, rows in segments)
    width = heads * HEAD
    gain, *matrices = weights
    half = (total // 2, D)
    scratch = [
        pltpu.VMEM((total, D), BF),
        pltpu.VMEM((total, D), BF),
        pltpu.VMEM((3 * width, D), BF),
        pltpu.VMEM((width, D), BF),
        pltpu.VMEM((total, width), BF),
        pltpu.VMEM((total + WIN * len(segments), width), BF),
        pltpu.VMEM((total + WIN * len(segments), width), BF),
        pltpu.VMEM((total, width), BF),
        pltpu.SemaphoreType.DMA((20,)),
        pltpu.SemaphoreType.DMA((3 * heads,)),
        pltpu.SemaphoreType.DMA((heads,)),
    ]
    outs = [(half, BF, ANY)] * 2 + [((8 * len(segments), 128), F32, VMEM)] + [((WIN, width), BF, VMEM)] * 2
    operands = [info, *parts, *states, gain, *matrices, *before, *deps]
    specs = [SMEM] + [ANY] * 4 + [VMEM] * (len(states) + 1) + [HBM] * 4 + [VMEM] * len(before) + [ANY] * 2
    return call(
        functools.partial(window_kernel, segments, heads, prev),
        outs, specs, scratch, operands, 2 * total * D * 2048, 12 * MIB, 24,
    )


def run_hidden(segments, info, parts, weights, deps):
    total = sum(rows for _, rows in segments)
    gain, gate, up, down = weights
    half = (total // 2, D)
    units = gate.shape[1]
    specs = [SMEM] + [ANY] * 4 + [VMEM] + [HBM] * 3 + [ANY] * 2
    scratch = [
        pltpu.VMEM((total, D), BF),
        pltpu.VMEM((total, D), BF),
        pltpu.VMEM((total, units), BF),
        pltpu.VMEM((total, units), F32),
        pltpu.VMEM(gate.shape, BF),
        pltpu.VMEM(up.shape, BF),
        pltpu.VMEM(down.shape, BF),
        pltpu.SemaphoreType.DMA((20,)),
        pltpu.SemaphoreType.DMA((3,)),
    ]
    return call(
        functools.partial(hidden_kernel, segments),
        [(half, BF, ANY)] * 2, specs, scratch, [info, *parts, gain, gate, up, down, *deps],
        2 * total * D * units * 3, 24 * MIB, 36,
    )


def after(value, *others):
    nothing = sum(other[(0,) * other.ndim].astype(F32) * 0.0 for other in others)
    return value + nothing.astype(value.dtype)


INWARD, ACROSS, OUTWARD = [(0, 1), (3, 2)], [(1, 2), (2, 1)], [(1, 0), (2, 3)]


def to_middle(near, far, stay):
    far_in = lax.ppermute(far, "tensor", INWARD)
    near_in = lax.ppermute(near, "tensor", INWARD)
    crossed = lax.ppermute(far + far_in, "tensor", ACROSS)
    return (stay.astype(F32) + (near.astype(F32) + near_in.astype(F32) + crossed.astype(F32))).astype(BF)


SAME = [(0, 0), (3, 3)]


def trailing(other, own_out, other_out):
    trail = lax.ppermute(other[:16, :128], "tensor", SAME)
    trail = lax.ppermute(trail, "tensor", SAME)
    trail = lax.ppermute(trail + own_out[:16, :128], "tensor", SAME)
    return lax.ppermute(trail + other_out[:16, :128], "tensor", SAME)


def first_out(own):
    return lax.ppermute(own, "tensor", ACROSS), lax.ppermute(own, "tensor", OUTWARD)


def pick_axis(array, axis, index):
    return jnp.where(index, lax.index_in_dim(array, 1, axis, False), lax.index_in_dim(array, 0, axis, False))


def pack_kernel(index, folded, tails, keys, values, keep, send, pack, sems):
    slots_here, heads = folded.shape[:2]
    pack[...] = jnp.zeros_like(pack)
    for slot in range(slots_here):
        for head in range(heads):
            wide, narrow = pl.ds(head * HEAD, HEAD), pl.ds(head * HEAD, HS)
            ours = slice(head * HS, (head + 1) * HS)
            pack[slot, pl.ds(0, STATE_KEYS), wide] = folded[slot, head]
            pack[slot, pl.ds(STATE_KEYS, WIN), narrow] = keys[slot, :, ours]
            pack[slot, pl.ds(STATE_VALUES, WIN), narrow] = values[slot, :, ours]
        ends = pl.ds(STATE_KEYS - 16, 16)
        pack[slot, ends, :] = pack[slot, ends, :] + tails[slot]
    made = []
    count = keep.shape[0]
    for number in range(2 * count):
        target = keep if number < count else send
        made.append(pltpu.make_async_copy(pack.at[index[number]], target.at[number % count], sems.at[number]))
        made[-1].start()
    for copy in made:
        copy.wait()


def slot_states(request_group, group_slot, sums, norms, keys, values, tail, count, firsts, seconds):
    here = lax.axis_index("req")
    slots_here, heads = sums.shape[:2]
    width = heads * HEAD
    requests = request_group.shape[0]
    groups = lax.all_gather(request_group, "req", axis=0, tiled=True)
    matches = jnp.arange(group_slot.shape[0])[None, :] == groups[:, None]
    slots = jnp.sum(jnp.where(matches, group_slot[None, :], 0), axis=1)

    fold = jnp.asarray(fold_matrix())
    folded = jnp.einsum("fg,ahgd->ahfd", fold, sums, precision=lax.Precision.HIGHEST).astype(BF)
    folded_norms = jnp.einsum("fg,ahg->ahf", fold, norms, precision=lax.Precision.HIGHEST).astype(BF)
    folded = jnp.concatenate([folded, folded_norms[..., None]], axis=-1)
    folded = jnp.pad(folded, ((0, 0), (0, 0), (0, 0), (0, HEAD - HS - 1)))
    tails = tail.reshape(slots_here, KC - 1, heads, HS)
    tails = jnp.pad(tails, ((0, 0), (0, 0), (0, 0), (0, HEAD - HS))).reshape(slots_here, KC - 1, width)
    tails = jnp.pad(tails, ((0, 0), (1, 16 - KC), (0, 0)))

    bits = []
    while 1 << len(bits) < count:
        bits.append(len(bits))
    local = (slots - here * slots_here).reshape((2,) * len(bits) + (requests,))
    local = jnp.where((local >= 0) & (local < slots_here), local, slots_here)

    def swap(array, bit):
        return lax.ppermute(array, "req", [(i, i ^ (1 << bit)) for i in range(count)])

    def upper(bit):
        return (here >> bit) & 1 == 1

    axis = len(bits) - 1
    entries = count // 2 * requests
    index = [pick_axis(local, axis, upper(0)).reshape(-1), pick_axis(local, axis, ~upper(0)).reshape(-1)]
    index = after(jnp.concatenate(index), *firsts)
    shape = (entries, STATE_ROWS, width)
    keep, send = pl.pallas_call(
        pack_kernel,
        out_shape=[jax.ShapeDtypeStruct(shape, BF)] * 2,
        in_specs=[SMEM] + [VMEM] * 4,
        out_specs=[ANY] * 2,
        scratch_shapes=[
            pltpu.VMEM((slots_here + 1, STATE_ROWS, width), BF),
            pltpu.SemaphoreType.DMA((2 * entries,)),
        ],
        compiler_params=pltpu.CompilerParams(vmem_limit_bytes=12 * MIB),
    )(index, folded, tails, keys, values)
    packs = (keep + swap(send, 0)).reshape((2,) * (len(bits) - 1) + (requests, STATE_ROWS, width))
    halves = []
    cut = STATE_ROWS // 2
    for number in range(2):
        part = packs[..., number * cut : (number + 1) * cut, :]
        left = bits[1:]
        order = left if number == 0 else left[::-1]
        while order:
            bit, order = order[0], order[1:]
            axis = len(left) - 1 - left.index(bit)
            left = [b for b in left if b != bit]
            if not order:
                part = after(part, *seconds)
            part = pick_axis(part, axis, upper(bit)) + swap(pick_axis(part, axis, ~upper(bit)), bit)
        halves.append(part)
    return jnp.concatenate(halves, axis=1)


def make_line(req_count):
    def per_device(
        hidden,
        suffix_len,
        request_group,
        group_slot,
        norm_first,
        query_weight,
        key_weight,
        value_weight,
        filter_gate,
        filter_taps,
        linear_out,
        norm_second,
        window_query,
        window_key,
        window_value,
        window_out,
        norm_third,
        gate_weight,
        up_weight,
        down_weight,
        prefix_sums,
        prefix_norms,
        prefix_keys,
        prefix_values,
        prefix_tail,
    ):
        requests = hidden.shape[0]
        heads = prefix_sums.shape[1]
        share = hidden.shape[1]
        here = lax.axis_index("tensor")
        low = here < 2
        middle = (here == 1) | (here == 2)

        both = (suffix_len[0] > SHORT) & (suffix_len[1] > SHORT)
        long = jnp.where(both, 0, (suffix_len[1] > SHORT).astype(jnp.int32))
        short = 1 - long

        ups, downs = [], []
        up = down = hidden
        for step in range(1, 4):
            up = lax.ppermute(up, "tensor", [(i, i + 1) for i in range(step - 1, 3)])
            down = lax.ppermute(down, "tensor", [(i + 1, i) for i in range(4 - step)])
            ups.append(up)
            downs.append(down)
        states = slot_states(
            request_group, group_slot, prefix_sums, prefix_norms, prefix_keys, prefix_values, prefix_tail, req_count,
            (ups[0], downs[0]), (ups[1], downs[1]),
        )

        def wide(matrix):
            matrix = matrix.reshape(matrix.shape[0], heads, HS)
            return jnp.pad(matrix, ((0, 0), (0, 0), (0, HEAD - HS))).reshape(matrix.shape[0], heads * HEAD)

        linear_weights = (
            norm_first[None],
            jnp.pad(wide(filter_taps), ((0, 8 - KC), (0, 0))),
            query_weight.T,
            key_weight.T,
            value_weight.T,
            filter_gate.T,
            linear_out,
        )
        window_weights = (norm_second[None], window_query.T, window_key.T, window_value.T, window_out)
        hidden_weights = (norm_third[None], gate_weight, up_weight, down_weight)
        left, right, plus = feature_maps(heads)
        consts = (jnp.asarray(left, BF), jnp.asarray(right, BF), jnp.asarray(plus))

        place = [here, low.astype(jnp.int32), middle.astype(jnp.int32), here * 0]
        quarters = tuple((0, s, s * share, share) for s in range(4))
        rows_here = here * share + jnp.arange(share)

        def info(indices):
            indices = [jnp.int32(0) + index for index in indices] * 2
            lengths = [suffix_len[index] for index in indices[:2]]
            return jnp.stack(place + indices[:2] + lengths).astype(jnp.int32)

        def run(streams, segments, shards):
            count = len(streams)
            infos = [info(indices) for indices in streams]
            parts, own, tops = [None] * count, [None] * count, [None] * count
            trails = [None] * count
            waiting = None
            dep = hidden
            for layer in range(3):
                for number, indices in enumerate(streams):
                    mine = [states[index] for index in indices]
                    if waiting is not None and count > 1:
                        late, late_own = waiting
                        other, own_out = first_out(late_own)
                    elif layer > 0:
                        other, own_out = first_out(own[number])
                        parts[number] = (own[number], own_out, other, lax.ppermute(other, "tensor", OUTWARD))
                    deps = (dep, dep if layer == 0 or count == 1 else trails[number])
                    if layer == 0:
                        near, far, stay, *_ = run_linear(
                            segments, shards, heads, 0, infos[number], hidden, ups, downs,
                            mine, consts, linear_weights, [], deps,
                        )
                    elif layer == 1:
                        stay = own[number]
                        near, far, tops[number], *_ = run_window(
                            segments, heads, 0, infos[number], parts[number], mine, window_weights, [], deps
                        )
                    else:
                        stay = own[number]
                        near, far = run_hidden(segments, infos[number], parts[number], hidden_weights, deps)
                    if waiting is not None and count > 1:
                        if layer == 0:
                            far = after(far, late_own)
                        parts[late] = (late_own, own_out, other, lax.ppermute(other, "tensor", OUTWARD))
                        trails[late] = trailing(other, own_out, parts[late][3])
                    own[number] = to_middle(near, far, stay)
                    dep = own[number] if layer > 0 or number == count - 1 else near
                    waiting = (number, own[number]) if layer < 2 else None
            return own, tops

        def live(rows, length):
            return jnp.where((rows_here < length)[:, None], rows, jnp.zeros_like(rows))

        half_row = jnp.where(low, 0, LMAX // 2)

        def square_sum(rows, first, length):
            floats = rows.astype(F32)
            counted = middle & (first + jnp.arange(rows.shape[0]) < length)
            return jnp.sum(jnp.where(counted[:, None], floats * floats, 0.0))

        def all_long():
            own, tops = run([(0,), (1,)], ((0, LMAX),), quarters)
            outs, squares = [], []
            for request in range(requests):
                squares.append(square_sum(own[request], half_row, suffix_len[request]))
                first, second = own[request][:share], own[request][share:]
                moved = lax.ppermute(jnp.where(low, first, second), "tensor", OUTWARD)
                outs.append(live(jnp.where(middle, jnp.where(low, second, first), moved), suffix_len[request]))
            return jnp.stack(outs), jnp.stack(squares + [top[0, 0] for top in tops])

        def one_long():
            own, tops = run(
                [(long, short)], ((0, LMAX), (LMAX, SHORT)), quarters + ((1, 0, LMAX, SHORT),)
            )
            own, top = own[0], tops[0]
            first, second, last = own[:share], own[share : 2 * share], own[2 * share :]
            moved = lax.ppermute(jnp.concatenate([jnp.where(low, first, second), last]), "tensor", OUTWARD)
            rest = lax.ppermute(last, "tensor", [(2, 0)])
            mine = jnp.where(middle, jnp.where(low, second, first), moved[:share])
            long_out = live(mine, suffix_len[long])
            mine = jnp.concatenate([moved[share:], rest, jnp.zeros((share - SHORT, D), BF)])
            short_out = live(mine, suffix_len[short])
            long_square = square_sum(own[: 2 * share], half_row, suffix_len[long])
            short_square = square_sum(last, jnp.where(low, 0, SHORT // 2), suffix_len[short])

            def ordered(of_long, of_short):
                return [jnp.where(long == request, of_long, of_short) for request in range(2)]

            return (
                jnp.stack(ordered(long_out, short_out)),
                jnp.stack(ordered(long_square, short_square) + ordered(top[0, 0], top[8, 0])),
            )

        outs, scalars = lax.cond(both, all_long, one_long)
        scalars = jnp.broadcast_to(scalars[:, None], (2 * requests, 128))
        everyone = [scalars] + [
            lax.ppermute(scalars, "tensor", [(i, (i + step) % 4) for i in range(4)]) for step in (1, 2, 3)
        ]
        total = sum(each[:requests, 0] for each in everyone)
        top_logit = functools.reduce(jnp.maximum, [each[requests:, 0] for each in everyone])
        return outs, jnp.sqrt(total / D), top_logit

    return per_device


def folded_features(queries):
    floats = jnp.transpose(queries.astype(F32), (1, 0, 2))
    parts = [jnp.ones(floats.shape[:-1] + (1,), F32), floats * FD ** (-0.25)]
    for shift in range(PAIRS):
        parts.append(floats * jnp.roll(floats, -shift, axis=-1) * (2.0 * FD) ** (-0.5))
    return jnp.concatenate(parts, axis=-1)


def plain_fold_matrix():
    row = jnp.arange(1 + FD + PAIRS * FD)[:, None]
    column = jnp.arange(1 + FD + FD * FD)[None, :]
    shift, first = (row - 1 - FD) // FD, (row - 1 - FD) % FD
    second = (first + shift) % FD
    major, minor = (column - 1 - FD) // FD, (column - 1 - FD) % FD
    straight = (major == first) & (minor == second)
    swapped = (major == second) & (minor == first) & (shift > 0) & (shift < FD // 2)
    squares = (row > FD) & (column > FD) & (straight | swapped)
    return jnp.where((row == column) & (row <= FD) | squares, 1.0, 0.0).astype(F32)


def line_gather(rows, axis, count):
    here = lax.axis_index(axis)
    size = rows.shape[0]
    up = down = rows
    ups, downs = [], []
    for step in range(1, count):
        up = lax.ppermute(up, axis, [(i, i + 1) for i in range(step - 1, count - 1)])
        down = lax.ppermute(down, axis, [(i + 1, i) for i in range(count - step)])
        ups.append(up)
        downs.append(down)
    around = jnp.concatenate(ups[::-1] + [rows] + downs)
    return lax.dynamic_slice_in_dim(around, (count - 1 - here) * size, count * size, 0)


def line_scatter(partial, axis, count):
    here = lax.axis_index(axis)
    size = partial.shape[0] // count

    def block(index):
        return lax.dynamic_slice_in_dim(partial, index * size, size, 0)

    up = down = None
    for step in range(1, count):
        to_up = block(jnp.minimum(here + count - step, count - 1))
        to_down = block(jnp.maximum(here - count + step, 0))
        if up is not None:
            to_up, to_down = to_up + up, to_down + down
        up = lax.ppermute(to_up, axis, [(i, i + 1) for i in range(step)])
        down = lax.ppermute(to_down, axis, [(i + 1, i) for i in range(count - 1 - step, count - 1)])
    return block(here).astype(F32) + up.astype(F32) + down.astype(F32)


def settle(partial, stream, axis, count):
    here = lax.axis_index(axis)
    size = partial.shape[0] // count
    mine = lax.dynamic_slice_in_dim(stream, here * size, size, 0)
    total = line_scatter(partial, axis, count)
    return line_gather((mine.astype(F32) + total).astype(BF), axis, count)


def bring_home(packs, axis, count):
    here = lax.axis_index(axis)
    bit = 1
    while bit < count:
        pairs = packs.reshape((packs.shape[0] // 2, 2) + packs.shape[1:])
        upper = (here & bit) != 0
        keep = jnp.where(upper, pairs[:, 1], pairs[:, 0])
        send = jnp.where(upper, pairs[:, 0], pairs[:, 1])
        packs = keep + lax.ppermute(send, axis, [(i, i ^ bit) for i in range(count)])
        bit *= 2
    return packs[0]


def make_plain(req_count, tensor_count):
    def per_device(
        hidden,
        suffix_len,
        request_group,
        group_slot,
        norm_first,
        query_weight,
        key_weight,
        value_weight,
        filter_gate,
        filter_taps,
        linear_out,
        norm_second,
        window_query,
        window_key,
        window_value,
        window_out,
        norm_third,
        gate_weight,
        up_weight,
        down_weight,
        prefix_sums,
        prefix_norms,
        prefix_keys,
        prefix_values,
        prefix_tail,
    ):
        requests_here = hidden.shape[0]
        share_rows = hidden.shape[1]
        slots_here, heads = prefix_sums.shape[:2]
        width = heads * HS

        groups = lax.all_gather(request_group, "req", axis=0, tiled=True)
        matches = jnp.arange(group_slot.shape[0])[None, :] == groups[:, None]
        slots = jnp.sum(jnp.where(matches, group_slot[None, :], 0), axis=1)
        fold = plain_fold_matrix()
        sums = jnp.einsum("fg,ahgd->afhd", fold, prefix_sums, precision=lax.Precision.HIGHEST)
        terms = sums.shape[1]
        norms = jnp.einsum("fg,ahg->afh", fold, prefix_norms, precision=lax.Precision.HIGHEST)
        norms = jnp.pad(norms.reshape(slots_here, -1), ((0, 0), (0, 2 * width - terms * heads)))
        pack = jnp.concatenate(
            [
                sums.reshape(slots_here, terms, width).astype(BF),
                norms.reshape(slots_here, 2, width).astype(BF),
                prefix_keys,
                prefix_values,
                prefix_tail,
            ],
            axis=1,
        )
        rows = pack.shape[1]
        pack = jnp.pad(pack, ((0, 0), (0, -rows % 32), (0, 0)))
        half = pack.shape[1] // 2
        pack = jnp.concatenate([pack[:, :half], pack[:, half:]], axis=2)
        local = slots - lax.axis_index("req") * slots_here
        owned = (local >= 0) & (local < slots_here)
        sent = jnp.take(pack, jnp.clip(local, 0, slots_here - 1), axis=0)
        sent = jnp.where(owned[:, None, None], sent, jnp.zeros_like(sent))
        sent = sent.reshape((req_count, requests_here) + sent.shape[1:])
        states = bring_home(sent, "req", req_count)
        states = jnp.concatenate([states[:, :, :width], states[:, :, width:]], axis=1)

        position = jnp.arange(LMAX)
        causal = position[:, None] >= position[None, :]
        bands = LMAX // WIN
        band_row = jnp.arange(WIN)[:, None]
        band_key = jnp.arange(2 * WIN)[None, :]
        allowed = (band_key > band_row) & (band_key <= band_row + WIN)

        def linear_part(request, stream):
            state = states[request]
            state_sums = state[:terms].reshape(terms, heads, HS)
            state_norms = state[terms : terms + 2].reshape(-1)[: terms * heads].reshape(terms, heads)
            tail = state[terms + 2 + 2 * WIN : terms + 2 + 2 * WIN + KC - 1]
            normed = rms_norm(stream, norm_first)
            queries = dot(normed, query_weight).astype(BF).reshape(LMAX, heads, FD)
            key_rows = dot(normed, key_weight).astype(BF).reshape(LMAX, heads, FD)
            values = dot(normed, value_weight).astype(BF)
            gating = dot(normed, filter_gate).astype(BF)
            extended = jnp.concatenate([tail, values], axis=0).astype(F32)
            convolved = sum(
                filter_taps[offset] * extended[KC - 1 - offset : KC - 1 - offset + LMAX]
                for offset in range(KC)
            )
            mixed = (convolved * jax.nn.silu(gating.astype(F32))).astype(BF)
            mixed = mixed.reshape(LMAX, heads, HS)
            scores = jnp.einsum("thf,shf->hts", queries, key_rows, preferred_element_type=F32)
            scores = scores * FD ** (-0.5)
            weights = jnp.where(causal, 1.0 + scores + 0.5 * scores * scores, 0.0)
            mapped = folded_features(queries)
            numerator = jnp.einsum(
                "hts,shd->thd", weights.astype(BF), mixed, preferred_element_type=F32
            ) + jnp.einsum(
                "htf,fhd->thd", mapped.astype(BF), state_sums, preferred_element_type=F32
            )
            denominator = jnp.sum(weights, axis=-1) + jnp.sum(
                mapped * jnp.transpose(state_norms).astype(F32)[:, None, :], axis=-1
            )
            linear_rows = (numerator / jnp.transpose(denominator)[..., None]).astype(BF)
            return dot(linear_rows.reshape(LMAX, width), linear_out).astype(BF)

        def window_part(request, stream):
            state = states[request]
            normed = rms_norm(stream, norm_second)
            queries = dot(normed, window_query).astype(BF).reshape(bands, WIN, heads, HS)
            key_rows = dot(normed, window_key).astype(BF)
            value_rows = dot(normed, window_value).astype(BF)
            start = terms + 2

            def paired(prefix, rows):
                blocks = jnp.concatenate([prefix, rows]).reshape(bands + 1, WIN, heads, HS)
                return jnp.concatenate([blocks[:-1], blocks[1:]], axis=1)

            key_pairs = paired(state[start : start + WIN], key_rows)
            value_pairs = paired(state[start + WIN : start + 2 * WIN], value_rows)
            logits = jnp.einsum(
                "bthd,bphd->bhtp", queries, key_pairs, preferred_element_type=F32
            ) * HS ** (-0.5)
            logits = jnp.where(allowed, logits, -jnp.inf)
            row_max = jnp.max(logits, axis=-1, keepdims=True)
            exponent = jnp.exp(logits - row_max)
            chances = (exponent / jnp.sum(exponent, axis=-1, keepdims=True)).astype(BF)
            attended = jnp.einsum(
                "bhtp,bphd->bthd", chances, value_pairs, preferred_element_type=F32
            ).astype(BF)
            final = (position == suffix_len[request] - 1).reshape(bands, 1, WIN)
            top = jnp.max(jnp.where(final, row_max[..., 0], -jnp.inf))
            return dot(attended.reshape(LMAX, width), window_out).astype(BF), top

        def hidden_part(stream):
            normed = rms_norm(stream, norm_third)
            inner = (jax.nn.silu(dot(normed, gate_weight)) * dot(normed, up_weight)).astype(BF)
            return dot(inner, down_weight).astype(BF)

        here = lax.axis_index("tensor")
        row_start = here * share_rows
        rows_here = row_start + jnp.arange(share_rows)
        outs, squares, tops = [], [], []
        for request in range(requests_here):
            stream = line_gather(hidden[request], "tensor", tensor_count)
            partial = linear_part(request, stream)
            stream = settle(partial, stream, "tensor", tensor_count)
            partial, top = window_part(request, stream)
            stream = settle(partial, stream, "tensor", tensor_count)
            partial = hidden_part(stream)
            total = line_scatter(partial, "tensor", tensor_count)
            mine = lax.dynamic_slice_in_dim(stream, row_start, share_rows, 0).astype(F32)
            mine = (mine + total).astype(BF)
            live = (rows_here < suffix_len[request])[:, None]
            outs.append(jnp.where(live, mine, jnp.zeros_like(mine)))
            floats = mine.astype(F32)
            squares.append(jnp.sum(jnp.where(live, floats * floats, 0.0)))
            tops.append(top)
        scalars = lax.all_gather(jnp.stack(squares + tops), "tensor")
        total = jnp.sum(scalars[:, :requests_here], axis=0)
        top_logit = jnp.max(scalars[:, requests_here:], axis=0)
        return jnp.stack(outs), jnp.sqrt(total / D), top_logit

    return per_device


def solution(mesh):
    return jax.shard_map(
        make_line(mesh.shape["req"]) if mesh.shape["tensor"] == 4 else make_plain(mesh.shape["req"], mesh.shape["tensor"]),
        mesh=mesh,
        in_specs=(
            P("req", "tensor", None),
            P("req"),
            P("req"),
            P(),
            P(),
            P(None, "tensor"),
            P(None, "tensor"),
            P(None, "tensor"),
            P(None, "tensor"),
            P(None, "tensor"),
            P("tensor", None),
            P(),
            P(None, "tensor"),
            P(None, "tensor"),
            P(None, "tensor"),
            P("tensor", None),
            P(),
            P(None, "tensor"),
            P(None, "tensor"),
            P("tensor", None),
            P("req", "tensor", None, None),
            P("req", "tensor", None),
            P("req", None, "tensor"),
            P("req", None, "tensor"),
            P("req", None, "tensor"),
        ),
        out_specs=(P("req", "tensor", None), P("req"), P("req")),
        check_vma=False,
    )
```

```python
import functools

import jax
import jax.numpy as jnp
import numpy as np
from jax import lax
from jax.experimental import pallas as pl
from jax.experimental.pallas import tpu as pltpu
from jax.sharding import PartitionSpec as P

D = 1792
FD = 16
HS = 112
WIN = 64
KC = 3
LMAX = 512
SHORT = 32
PAIRS = FD // 2 + 1
SQUARES = PAIRS * FD
FEATURES = 256
HEAD = 128
STATE_KEYS = 176
STATE_VALUES = STATE_KEYS + WIN
STATE_ROWS = STATE_VALUES + WIN

EPS = 1e-05
BF = jnp.bfloat16
F32 = jnp.float32
MIB = 1 << 20
ANY = pl.BlockSpec(memory_space=pl.ANY)
SMEM = pl.BlockSpec(memory_space=pltpu.SMEM)
VMEM = pl.BlockSpec(memory_space=pltpu.VMEM)
HBM = pl.BlockSpec(memory_space=pltpu.HBM)


def rms_norm(rows, gain):
    floats = rows.astype(F32)
    inverse_rms = lax.rsqrt(jnp.mean(floats * floats, axis=-1, keepdims=True) + EPS)
    return (floats * inverse_rms * gain).astype(BF)


def dot(left, right):
    return jnp.dot(left, right, preferred_element_type=F32)


def dot_t(left, right):
    return lax.dot_general(left, right, (((1,), (1,)), ((), ())), preferred_element_type=F32)


def fold_matrix():
    fold = np.zeros((STATE_KEYS, 1 + FD + FD * FD), np.float32)
    for shift in range(PAIRS):
        for i in range(FD):
            j = (i + shift) % FD
            fold[shift * FD + i, 1 + FD + i * FD + j] = 1.0
            if 0 < shift < FD // 2:
                fold[shift * FD + i, 1 + FD + j * FD + i] = 1.0
    for i in range(FD):
        fold[SQUARES + i, 1 + i] = 1.0
    fold[SQUARES + FD, 0] = 1.0
    return fold


def feature_maps(heads):
    left = np.zeros((heads, HEAD, FEATURES), np.float32)
    right = np.zeros((heads, HEAD, FEATURES), np.float32)
    plus = np.zeros((8, FEATURES), np.float32)
    for head in range(heads):
        for i in range(FD):
            for shift in range(PAIRS):
                left[head, head * FD + i, shift * FD + i] = 1.0
                right[head, head * FD + (i + shift) % FD, shift * FD + i] = 1.0
            left[head, head * FD + i, SQUARES + i] = 1.0
    plus[1, SQUARES : SQUARES + FD] = 1.0
    plus[0:2, SQUARES + FD] = 1.0
    plus[2, :SQUARES] = (2.0 * FD) ** (-0.5)
    plus[2, SQUARES : SQUARES + FD] = FD ** (-0.25)
    plus[2, SQUARES + FD] = 1.0
    return left, right, plus


def copies(plan, sems):
    made = []
    for number, (condition, source, target) in enumerate(plan):
        copy = pltpu.make_async_copy(source, target, sems.at[number])
        copy.start() if condition is True else pl.when(condition)(copy.start)
        made.append((condition, copy))

    def wait():
        for condition, copy in made:
            copy.wait() if condition is True else pl.when(condition)(copy.wait)

    return wait


def head_rows(source, target, first, heads):
    return [
        (True, source.at[pl.ds(head * HS, HS)], target.at[pl.ds(first + head * HEAD, HS)]) for head in range(heads)
    ]


def clear(target, pieces):
    for start, rows in pieces:
        target[pl.ds(start, rows), :] = jnp.zeros((rows, target.shape[1]), target.dtype)


def half_pieces(segments):
    pieces = ([], [])
    buffer_row = 0
    for start, rows in segments:
        for half in range(2):
            pieces[half].append((start + half * rows // 2, rows // 2, buffer_row))
        buffer_row += rows // 2
    return pieces, buffer_row


def put_halves(segments, info, source, near, far, sems):
    pieces, _ = half_pieces(segments)
    plan = []
    for half in range(2):
        for natural, rows, at in pieces[half]:
            for low in (0, 1):
                target = near if half == 1 - low else far
                plan.append((info[1] == low, source.at[pl.ds(natural, rows)], target.at[pl.ds(at, rows)]))
    copies(plan, sems)()


def halves_plan(segments, info, own, own_out, other, other_out, target):
    pieces, _ = half_pieces(segments)
    plan = []
    for low in (0, 1):
        for middle in (0, 1):
            near, far = (own, other) if middle else (own_out, other_out)
            for half in range(2):
                source = near if half == 1 - low else far
                for natural, rows, at in pieces[half]:
                    plan.append(
                        (
                            (info[1] == low) & (info[2] == middle),
                            source.at[pl.ds(at, rows)],
                            target.at[pl.ds(natural, rows)],
                        )
                    )
    return plan


def norm_rows(x, n, gain):
    rows = x.shape[0]
    for at in range(0, rows, 128):
        size = min(128, rows - at)
        n[pl.ds(at, size), :] = rms_norm(x[pl.ds(at, size), :], gain)


def lane_of_ones(shape):
    return (lax.broadcasted_iota(jnp.int32, shape, 1) & (HEAD - 1)) == HS


def linear_kernel(segments, shards, heads, prev, *refs):
    refs = list(refs)
    info, own, ups, downs = refs[0], refs[1], refs[2:5], refs[5:8]
    states = refs[8 : 8 + len(segments)]
    refs = refs[8 + len(segments) :]
    gain, taps, left, right, plus = refs[:5]
    query_weight, key_weight, value_weight, gate_weight, out_weight = refs[5:10]
    refs = refs[10:]
    if prev:
        prev_key, prev_mixed, prev_value = refs[:3]
        refs = refs[3:]
    refs = refs[2:]
    near, far, stay = refs[:3]
    x, n, u, w, ow, q, k, m, y, sems, wsems, osems = refs[3:]
    width = heads * HEAD
    total = x.shape[0]
    plan = []
    for segment, shard, row, rows in shards:
        for here in range(4):
            source = own if here == shard else (ups[here - shard - 1] if here > shard else downs[shard - here - 1])
            plan.append(
                (
                    info[0] == here,
                    source.at[info[4 + segment], pl.ds(0, rows)],
                    x.at[pl.ds(row, rows)],
                )
            )
    wait_x = copies(plan, sems)
    plan = [(True, query_weight, w.at[pl.ds(0, heads * FD)]), (True, key_weight, w.at[pl.ds(HEAD, heads * FD)])]
    plan += head_rows(value_weight, w, 2 * HEAD, heads) + head_rows(gate_weight, w, 2 * HEAD + width, heads)
    wait_w = copies(plan, wsems)
    wait_out = copies(head_rows(out_weight, ow, 0, heads), osems)
    clear(w, [(heads * FD, HEAD - heads * FD), (HEAD + heads * FD, HEAD - heads * FD)])
    clear(w, [(2 * HEAD + HS + HEAD * head, HEAD - HS) for head in range(2 * heads)])
    clear(ow, [(HS + HEAD * head, HEAD - HS) for head in range(heads)])
    if prev:
        k[pl.ds(0, prev), :] = prev_key[...]
        m[pl.ds(0, prev), :] = prev_mixed[...]
    wait_x()
    pieces, _ = half_pieces(segments)
    plan = []
    for low in (0, 1):
        for natural, rows, at in pieces[1 - low]:
            plan.append((info[1] == low, x.at[pl.ds(natural, rows)], stay.at[pl.ds(at, rows)]))
    wait_stay = copies(plan, sems)
    norm_rows(x, n, gain[...])
    wait_w()
    q[...] = dot_t(n[...], w[:HEAD]).astype(BF)
    k[pl.ds(prev, total), :] = dot_t(n[...], w[HEAD : 2 * HEAD]).astype(BF)
    y[...] = dot_t(n[...], w[2 * HEAD : 2 * HEAD + width]).astype(BF)
    u[...] = dot_t(n[...], w[2 * HEAD + width :]).astype(BF)
    tap = taps[...]
    for number, (start, rows) in enumerate(segments):
        base = prev if number == 0 else 0
        tile = min(rows, 256)
        if base:
            ends = prev_value[...].astype(F32)
            last2, last = ends[14:15], ends[15:16]
        else:
            ends = states[number][pl.ds(SQUARES + FD, 16), :].astype(F32)
            last2, last = ends[1:2], ends[2:3]
        for at in range(start, start + rows, tile):
            v = y[pl.ds(at, tile), :].astype(F32)
            opened = u[pl.ds(at, tile), :].astype(F32)
            row = lax.broadcasted_iota(jnp.int32, v.shape, 0)
            back1 = jnp.where(row == 0, last, pltpu.roll(v, 1, 0))
            back2 = jnp.where(row == 0, last2, jnp.where(row == 1, last, pltpu.roll(v, 2, 0)))
            last2, last = v[tile - 2 : tile - 1], v[tile - 1 : tile]
            convolved = tap[0:1] * v + tap[1:2] * back1 + tap[2:3] * back2
            mixed = convolved * (opened / (1.0 + jnp.exp(-opened)))
            m[pl.ds(prev + at, tile), :] = jnp.where(lane_of_ones(v.shape), 1.0, mixed).astype(BF)
    wait_out()
    for number, (start, rows) in enumerate(segments):
        base = prev if number == 0 else 0
        tile = min(rows, 256)
        first = 0 if number == 0 else prev + start
        for at in range(start, start + rows, tile):
            queries = q[pl.ds(at, tile), :]
            lane = lax.broadcasted_iota(jnp.int32, queries.shape, 1)
            for head in range(heads):
                columns = pl.ds(head * HEAD, HEAD)
                mapped = (
                    (dot(queries, left[head]) + plus[0:1, :])
                    * (dot(queries, right[head]) + plus[1:2, :])
                    * plus[2:3, :]
                )
                total_rows = dot(mapped.astype(BF), states[number][pl.ds(0, FEATURES), columns])
                own_lanes = (lane >= head * FD) & (lane < (head + 1) * FD)
                masked = jnp.where(own_lanes, queries, jnp.zeros_like(queries))
                for key_at in range(first, prev + at + tile, tile):
                    a = dot_t(masked, k[pl.ds(key_at, tile), :]) * FD ** (-0.5)
                    weights = 1.0 + a + 0.5 * a * a
                    if key_at == prev + at:
                        causal = lax.broadcasted_iota(jnp.int32, a.shape, 0) >= lax.broadcasted_iota(
                            jnp.int32, a.shape, 1
                        )
                        weights = jnp.where(causal, weights, 0.0)
                    total_rows += dot(weights.astype(BF), m[pl.ds(key_at, tile), columns])
                y[pl.ds(at, tile), columns] = (total_rows / total_rows[:, HS : HS + 1]).astype(BF)
    wait_stay()
    x[...] = dot(y[...], ow[...]).astype(BF)
    put_halves(segments, info, x, near, far, sems)


def window_kernel(segments, heads, prev, *refs):
    refs = list(refs)
    info, own, own_out, other, other_out = refs[:5]
    states = refs[5 : 5 + len(segments)]
    refs = refs[5 + len(segments) :]
    gain, query_weight, key_weight, value_weight, out_weight = refs[:5]
    refs = refs[5:]
    if prev:
        prev_keys, prev_values = refs[:2]
        refs = refs[2:]
    refs = refs[2:]
    near, far, top = refs[:3]
    x, n, w, ow, q, k, v, y, sems, wsems, osems = refs[3:]
    width = heads * HEAD
    wait_x = copies(halves_plan(segments, info, own, own_out, other, other_out, x), sems)
    plan = head_rows(query_weight, w, 0, heads)
    plan += head_rows(key_weight, w, width, heads) + head_rows(value_weight, w, 2 * width, heads)
    wait_w = copies(plan, wsems)
    wait_out = copies(head_rows(out_weight, ow, 0, heads), osems)
    clear(w, [(HS + HEAD * head, HEAD - HS) for head in range(3 * heads)])
    clear(ow, [(HS + HEAD * head, HEAD - HS) for head in range(heads)])
    wait_x()
    norm_rows(x, n, gain[...])
    wait_w()
    q[...] = dot_t(n[...], w[:width]).astype(BF)
    new_keys = dot_t(n[...], w[width : 2 * width]).astype(BF)
    for number, (start, rows) in enumerate(segments):
        k[pl.ds(start + WIN * (number + 1), rows), :] = new_keys[start : start + rows]
    new_values = dot_t(n[...], w[2 * width :])
    new_values = jnp.where(lane_of_ones(new_values.shape), 1.0, new_values).astype(BF)
    for number, (start, rows) in enumerate(segments):
        v[pl.ds(start + WIN * (number + 1), rows), :] = new_values[start : start + rows]
    best = []
    for number, (start, rows) in enumerate(segments):
        shift = WIN * (number + 1)
        if prev and number == 0:
            k[pl.ds(0, WIN), :] = prev_keys[...]
            v[pl.ds(0, WIN), :] = prev_values[...]
        else:
            old = states[number][pl.ds(STATE_VALUES, WIN), :]
            k[pl.ds(start + shift - WIN, WIN), :] = states[number][pl.ds(STATE_KEYS, WIN), :]
            v[pl.ds(start + shift - WIN, WIN), :] = jnp.where(
                lane_of_ones(old.shape), jnp.ones_like(old), old
            )
        final = info[6 + number] - 1
        tile = min(rows, 128)
        best_here = jnp.full((1, 1), -jnp.inf, F32)
        for at in range(start, start + rows, tile):
            keys_here = tile + WIN
            row = lax.broadcasted_iota(jnp.int32, (tile, keys_here), 0)
            place = lax.broadcasted_iota(jnp.int32, (tile, keys_here), 1)
            allowed = (place > row) & (place <= row + WIN)
            for head in range(heads):
                columns = pl.ds(head * HEAD, HEAD)
                e = dot_t(q[pl.ds(at, tile), columns], k[pl.ds(shift - WIN + at, keys_here), columns])
                e = jnp.where(allowed, e * HS ** (-0.5), -jnp.inf)
                row_max = jnp.max(e, axis=-1, keepdims=True)
                chances = jnp.exp(e - row_max).astype(BF)
                o = dot(chances, v[pl.ds(shift - WIN + at, keys_here), columns])
                y[pl.ds(at, tile), columns] = (o / o[:, HS : HS + 1]).astype(BF)
                at_final = lax.broadcasted_iota(jnp.int32, row_max.shape, 0) + (at - start) == final
                best_here = jnp.maximum(
                    best_here, jnp.max(jnp.where(at_final, row_max, -jnp.inf), axis=0, keepdims=True)
                )
        best.append(best_here)
    for number in range(len(segments)):
        top[pl.ds(number * 8, 8), :] = jnp.broadcast_to(best[number], (8, 128))
    wait_out()
    x[...] = dot(y[...], ow[...]).astype(BF)
    put_halves(segments, info, x, near, far, sems)


def hidden_kernel(segments, *refs):
    info, own, own_out, other, other_out, gain, gate, up, down, _, _, near, far = refs[:13]
    x, n, inner, opened, gate_v, up_v, down_v, sems, wsems = refs[13:]
    block = 256
    wait_x = copies(halves_plan(segments, info, own, own_out, other, other_out, x), sems)
    waits = [
        copies([(True, matrix, held)], wsems.at[pl.ds(number, 1)])
        for number, (matrix, held) in enumerate(((gate, gate_v), (up, up_v), (down, down_v)))
    ]
    wait_x()
    norm_rows(x, n, gain[...])
    blocks = [pl.ds(at, block) for at in range(0, inner.shape[1], block)]
    waits[0]()
    for columns in blocks:
        opened[:, columns] = dot(n[...], gate_v[:, columns])
    waits[1]()
    for columns in blocks:
        gated = opened[:, columns]
        inner[:, columns] = (gated / (1.0 + jnp.exp(-gated)) * dot(n[...], up_v[:, columns])).astype(BF)
    waits[2]()
    for at in range(0, x.shape[1], block):
        columns = pl.ds(at, block)
        x[:, columns] = dot(inner[...], down_v[:, columns]).astype(BF)
    put_halves(segments, info, x, near, far, sems)


def call(body, outs, specs, scratch, operands, flops, moved, limit):
    return pl.pallas_call(
        body,
        out_shape=[jax.ShapeDtypeStruct(shape, dtype) for shape, dtype, _ in outs],
        in_specs=specs,
        out_specs=[spec for _, _, spec in outs],
        scratch_shapes=scratch,
        compiler_params=pltpu.CompilerParams(vmem_limit_bytes=limit * MIB),
        cost_estimate=pl.CostEstimate(flops=flops // 1000, bytes_accessed=moved // 1000, transcendentals=0),
    )(*operands)


def run_linear(segments, shards, heads, prev, info, own, ups, downs, states, consts, weights, before, deps):
    total = sum(rows for _, rows in segments)
    width = heads * HEAD
    gain, taps, *matrices = weights
    half = (total // 2, D)
    scratch = [
        pltpu.VMEM((total, D), BF),
        pltpu.VMEM((total, D), BF),
        pltpu.VMEM((total, width), BF),
        pltpu.VMEM((2 * HEAD + 2 * width, D), BF),
        pltpu.VMEM((width, D), BF),
        pltpu.VMEM((total, HEAD), BF),
        pltpu.VMEM((prev + total, HEAD), BF),
        pltpu.VMEM((prev + total, width), BF),
        pltpu.VMEM((total, width), BF),
        pltpu.SemaphoreType.DMA((20,)),
        pltpu.SemaphoreType.DMA((3 * heads,)),
        pltpu.SemaphoreType.DMA((heads,)),
    ]
    outs = [(half, BF, ANY)] * 3
    operands = [info, own, *ups, *downs, *states, gain, taps, *consts, *matrices, *before, *deps]
    specs = [SMEM] + [ANY] * 7 + [VMEM] * (len(states) + 2 + 3) + [HBM] * 5 + [VMEM] * len(before) + [ANY] * 2
    return call(
        functools.partial(linear_kernel, segments, shards, heads, prev),
        outs, specs, scratch, operands, 2 * total * D * 1792, 12 * MIB, 24,
    )


def run_window(segments, heads, prev, info, parts, states, weights, before, deps):
    total = sum(rows for _, rows in segments)
    width = heads * HEAD
    gain, *matrices = weights
    half = (total // 2, D)
    scratch = [
        pltpu.VMEM((total, D), BF),
        pltpu.VMEM((total, D), BF),
        pltpu.VMEM((3 * width, D), BF),
        pltpu.VMEM((width, D), BF),
        pltpu.VMEM((total, width), BF),
        pltpu.VMEM((total + WIN * len(segments), width), BF),
        pltpu.VMEM((total + WIN * len(segments), width), BF),
        pltpu.VMEM((total, width), BF),
        pltpu.SemaphoreType.DMA((20,)),
        pltpu.SemaphoreType.DMA((3 * heads,)),
        pltpu.SemaphoreType.DMA((heads,)),
    ]
    outs = [(half, BF, ANY)] * 2 + [((8 * len(segments), 128), F32, VMEM)]
    operands = [info, *parts, *states, gain, *matrices, *before, *deps]
    specs = [SMEM] + [ANY] * 4 + [VMEM] * (len(states) + 1) + [HBM] * 4 + [VMEM] * len(before) + [ANY] * 2
    return call(
        functools.partial(window_kernel, segments, heads, prev),
        outs, specs, scratch, operands, 2 * total * D * 2048, 12 * MIB, 24,
    )


def run_hidden(segments, info, parts, weights, deps):
    total = sum(rows for _, rows in segments)
    gain, gate, up, down = weights
    half = (total // 2, D)
    units = gate.shape[1]
    specs = [SMEM] + [ANY] * 4 + [VMEM] + [HBM] * 3 + [ANY] * 2
    scratch = [
        pltpu.VMEM((total, D), BF),
        pltpu.VMEM((total, D), BF),
        pltpu.VMEM((total, units), BF),
        pltpu.VMEM((total, units), F32),
        pltpu.VMEM(gate.shape, BF),
        pltpu.VMEM(up.shape, BF),
        pltpu.VMEM(down.shape, BF),
        pltpu.SemaphoreType.DMA((20,)),
        pltpu.SemaphoreType.DMA((3,)),
    ]
    return call(
        functools.partial(hidden_kernel, segments),
        [(half, BF, ANY)] * 2, specs, scratch, [info, *parts, gain, gate, up, down, *deps],
        2 * total * D * units * 3, 24 * MIB, 36,
    )


def after(value, *others):
    nothing = sum(other[(0,) * other.ndim].astype(F32) * 0.0 for other in others)
    return value + nothing.astype(value.dtype)


INWARD, ACROSS, OUTWARD = [(0, 1), (3, 2)], [(1, 2), (2, 1)], [(1, 0), (2, 3)]


def to_middle(near, far, stay):
    far_in = lax.ppermute(far, "tensor", INWARD)
    near_in = lax.ppermute(near, "tensor", INWARD)
    crossed = lax.ppermute(far + far_in, "tensor", ACROSS)
    return (stay.astype(F32) + (near.astype(F32) + near_in.astype(F32) + crossed.astype(F32))).astype(BF)


SAME = [(0, 0), (3, 3)]


def trailing(other, own_out, other_out):
    trail = lax.ppermute(other[:16, :128], "tensor", SAME)
    trail = lax.ppermute(trail, "tensor", SAME)
    trail = lax.ppermute(trail + own_out[:16, :128], "tensor", SAME)
    return lax.ppermute(trail + other_out[:16, :128], "tensor", SAME)


def first_out(own):
    return lax.ppermute(own, "tensor", ACROSS), lax.ppermute(own, "tensor", OUTWARD)


def pick_axis(array, axis, index):
    return jnp.where(index, lax.index_in_dim(array, 1, axis, False), lax.index_in_dim(array, 0, axis, False))


def pack_kernel(index, folded, tails, keys, values, keep, send, pack, sems):
    slots_here, heads = folded.shape[:2]
    pack[...] = jnp.zeros_like(pack)
    for slot in range(slots_here):
        for head in range(heads):
            wide, narrow = pl.ds(head * HEAD, HEAD), pl.ds(head * HEAD, HS)
            ours = slice(head * HS, (head + 1) * HS)
            pack[slot, pl.ds(0, STATE_KEYS), wide] = folded[slot, head]
            pack[slot, pl.ds(STATE_KEYS, WIN), narrow] = keys[slot, :, ours]
            pack[slot, pl.ds(STATE_VALUES, WIN), narrow] = values[slot, :, ours]
        ends = pl.ds(STATE_KEYS - 16, 16)
        pack[slot, ends, :] = pack[slot, ends, :] + tails[slot]
    made = []
    count = keep.shape[0]
    for number in range(2 * count):
        target = keep if number < count else send
        made.append(pltpu.make_async_copy(pack.at[index[number]], target.at[number % count], sems.at[number]))
        made[-1].start()
    for copy in made:
        copy.wait()


def slot_states(request_group, group_slot, sums, norms, keys, values, tail, count, firsts, seconds):
    here = lax.axis_index("req")
    slots_here, heads = sums.shape[:2]
    width = heads * HEAD
    requests = request_group.shape[0]
    groups = lax.all_gather(request_group, "req", axis=0, tiled=True)
    matches = jnp.arange(group_slot.shape[0])[None, :] == groups[:, None]
    slots = jnp.sum(jnp.where(matches, group_slot[None, :], 0), axis=1)

    fold = jnp.asarray(fold_matrix())
    folded = jnp.einsum("fg,ahgd->ahfd", fold, sums, precision=lax.Precision.HIGHEST).astype(BF)
    folded_norms = jnp.einsum("fg,ahg->ahf", fold, norms, precision=lax.Precision.HIGHEST).astype(BF)
    folded = jnp.concatenate([folded, folded_norms[..., None]], axis=-1)
    folded = jnp.pad(folded, ((0, 0), (0, 0), (0, 0), (0, HEAD - HS - 1)))
    tails = tail.reshape(slots_here, KC - 1, heads, HS)
    tails = jnp.pad(tails, ((0, 0), (0, 0), (0, 0), (0, HEAD - HS))).reshape(slots_here, KC - 1, width)
    tails = jnp.pad(tails, ((0, 0), (1, 16 - KC), (0, 0)))

    bits = []
    while 1 << len(bits) < count:
        bits.append(len(bits))
    local = (slots - here * slots_here).reshape((2,) * len(bits) + (requests,))
    local = jnp.where((local >= 0) & (local < slots_here), local, slots_here)

    def swap(array, bit):
        return lax.ppermute(array, "req", [(i, i ^ (1 << bit)) for i in range(count)])

    def upper(bit):
        return (here >> bit) & 1 == 1

    axis = len(bits) - 1
    entries = count // 2 * requests
    index = [pick_axis(local, axis, upper(0)).reshape(-1), pick_axis(local, axis, ~upper(0)).reshape(-1)]
    index = after(jnp.concatenate(index), *firsts)
    shape = (entries, STATE_ROWS, width)
    keep, send = pl.pallas_call(
        pack_kernel,
        out_shape=[jax.ShapeDtypeStruct(shape, BF)] * 2,
        in_specs=[SMEM] + [VMEM] * 4,
        out_specs=[ANY] * 2,
        scratch_shapes=[
            pltpu.VMEM((slots_here + 1, STATE_ROWS, width), BF),
            pltpu.SemaphoreType.DMA((2 * entries,)),
        ],
        compiler_params=pltpu.CompilerParams(vmem_limit_bytes=12 * MIB),
    )(index, folded, tails, keys, values)
    packs = (keep + swap(send, 0)).reshape((2,) * (len(bits) - 1) + (requests, STATE_ROWS, width))
    halves = []
    cut = STATE_ROWS // 2
    for number in range(2):
        part = packs[..., number * cut : (number + 1) * cut, :]
        left = bits[1:]
        order = left if number == 0 else left[::-1]
        while order:
            bit, order = order[0], order[1:]
            axis = len(left) - 1 - left.index(bit)
            left = [b for b in left if b != bit]
            if not order:
                part = after(part, *seconds)
            part = pick_axis(part, axis, upper(bit)) + swap(pick_axis(part, axis, ~upper(bit)), bit)
        halves.append(part)
    return jnp.concatenate(halves, axis=1)


def make_line(req_count):
    def per_device(
        hidden,
        suffix_len,
        request_group,
        group_slot,
        norm_first,
        query_weight,
        key_weight,
        value_weight,
        filter_gate,
        filter_taps,
        linear_out,
        norm_second,
        window_query,
        window_key,
        window_value,
        window_out,
        norm_third,
        gate_weight,
        up_weight,
        down_weight,
        prefix_sums,
        prefix_norms,
        prefix_keys,
        prefix_values,
        prefix_tail,
    ):
        requests = hidden.shape[0]
        heads = prefix_sums.shape[1]
        share = hidden.shape[1]
        here = lax.axis_index("tensor")
        low = here < 2
        middle = (here == 1) | (here == 2)

        both = (suffix_len[0] > SHORT) & (suffix_len[1] > SHORT)
        long = jnp.where(both, 0, (suffix_len[1] > SHORT).astype(jnp.int32))
        short = 1 - long

        ups, downs = [], []
        up = down = hidden
        for step in range(1, 4):
            up = lax.ppermute(up, "tensor", [(i, i + 1) for i in range(step - 1, 3)])
            down = lax.ppermute(down, "tensor", [(i + 1, i) for i in range(4 - step)])
            ups.append(up)
            downs.append(down)
        states = slot_states(
            request_group, group_slot, prefix_sums, prefix_norms, prefix_keys, prefix_values, prefix_tail, req_count,
            (ups[0], downs[0]), (ups[1], downs[1]),
        )

        def wide(matrix):
            matrix = matrix.reshape(matrix.shape[0], heads, HS)
            return jnp.pad(matrix, ((0, 0), (0, 0), (0, HEAD - HS))).reshape(matrix.shape[0], heads * HEAD)

        linear_weights = (
            norm_first[None],
            jnp.pad(wide(filter_taps), ((0, 8 - KC), (0, 0))),
            query_weight.T,
            key_weight.T,
            value_weight.T,
            filter_gate.T,
            linear_out,
        )
        window_weights = (norm_second[None], window_query.T, window_key.T, window_value.T, window_out)
        hidden_weights = (norm_third[None], gate_weight, up_weight, down_weight)
        left, right, plus = feature_maps(heads)
        consts = (jnp.asarray(left, BF), jnp.asarray(right, BF), jnp.asarray(plus))

        place = [here, low.astype(jnp.int32), middle.astype(jnp.int32), here * 0]
        quarters = tuple((0, s, s * share, share) for s in range(4))
        rows_here = here * share + jnp.arange(share)

        def info(indices):
            indices = [jnp.int32(0) + index for index in indices] * 2
            lengths = [suffix_len[index] for index in indices[:2]]
            return jnp.stack(place + indices[:2] + lengths).astype(jnp.int32)

        def run(streams, segments, shards):
            count = len(streams)
            infos = [info(indices) for indices in streams]
            parts, own, tops = [None] * count, [None] * count, [None] * count
            trails = [None] * count
            waiting = None
            dep = hidden
            for layer in range(3):
                for number, indices in enumerate(streams):
                    mine = [states[index] for index in indices]
                    if waiting is not None and count > 1:
                        late, late_own = waiting
                        other, own_out = first_out(late_own)
                    elif layer > 0:
                        other, own_out = first_out(own[number])
                        parts[number] = (own[number], own_out, other, lax.ppermute(other, "tensor", OUTWARD))
                    deps = (dep, dep if layer == 0 or count == 1 else trails[number])
                    if layer == 0:
                        near, far, stay = run_linear(
                            segments, shards, heads, 0, infos[number], hidden, ups, downs,
                            mine, consts, linear_weights, [], deps,
                        )
                    elif layer == 1:
                        stay = own[number]
                        near, far, tops[number] = run_window(
                            segments, heads, 0, infos[number], parts[number], mine, window_weights, [], deps
                        )
                    else:
                        stay = own[number]
                        near, far = run_hidden(segments, infos[number], parts[number], hidden_weights, deps)
                    if waiting is not None and count > 1:
                        if layer == 0:
                            far = after(far, late_own)
                        parts[late] = (late_own, own_out, other, lax.ppermute(other, "tensor", OUTWARD))
                        trails[late] = trailing(other, own_out, parts[late][3])
                    own[number] = to_middle(near, far, stay)
                    dep = own[number] if layer > 0 or number == count - 1 else near
                    waiting = (number, own[number]) if layer < 2 else None
            return own, tops

        def live(rows, length):
            return jnp.where((rows_here < length)[:, None], rows, jnp.zeros_like(rows))

        half_row = jnp.where(low, 0, LMAX // 2)

        def square_sum(rows, first, length):
            floats = rows.astype(F32)
            counted = middle & (first + jnp.arange(rows.shape[0]) < length)
            return jnp.sum(jnp.where(counted[:, None], floats * floats, 0.0))

        def all_long():
            own, tops = run([(0,), (1,)], ((0, LMAX),), quarters)
            outs, squares = [], []
            for request in range(requests):
                squares.append(square_sum(own[request], half_row, suffix_len[request]))
                first, second = own[request][:share], own[request][share:]
                moved = lax.ppermute(jnp.where(low, first, second), "tensor", OUTWARD)
                outs.append(live(jnp.where(middle, jnp.where(low, second, first), moved), suffix_len[request]))
            return jnp.stack(outs), jnp.stack(squares + [top[0, 0] for top in tops])

        def one_long():
            own, tops = run(
                [(long, short)], ((0, LMAX), (LMAX, SHORT)), quarters + ((1, 0, LMAX, SHORT),)
            )
            own, top = own[0], tops[0]
            first, second, last = own[:share], own[share : 2 * share], own[2 * share :]
            moved = lax.ppermute(jnp.concatenate([jnp.where(low, first, second), last]), "tensor", OUTWARD)
            rest = lax.ppermute(last, "tensor", [(2, 0)])
            mine = jnp.where(middle, jnp.where(low, second, first), moved[:share])
            long_out = live(mine, suffix_len[long])
            mine = jnp.concatenate([moved[share:], rest, jnp.zeros((share - SHORT, D), BF)])
            short_out = live(mine, suffix_len[short])
            long_square = square_sum(own[: 2 * share], half_row, suffix_len[long])
            short_square = square_sum(last, jnp.where(low, 0, SHORT // 2), suffix_len[short])

            def ordered(of_long, of_short):
                return [jnp.where(long == request, of_long, of_short) for request in range(2)]

            return (
                jnp.stack(ordered(long_out, short_out)),
                jnp.stack(ordered(long_square, short_square) + ordered(top[0, 0], top[8, 0])),
            )

        outs, scalars = lax.cond(both, all_long, one_long)
        scalars = jnp.broadcast_to(scalars[:, None], (2 * requests, 128))
        everyone = [scalars] + [
            lax.ppermute(scalars, "tensor", [(i, (i + step) % 4) for i in range(4)]) for step in (1, 2, 3)
        ]
        total = sum(each[:requests, 0] for each in everyone)
        top_logit = functools.reduce(jnp.maximum, [each[requests:, 0] for each in everyone])
        return outs, jnp.sqrt(total / D), top_logit

    return per_device


def folded_features(queries):
    floats = jnp.transpose(queries.astype(F32), (1, 0, 2))
    parts = [jnp.ones(floats.shape[:-1] + (1,), F32), floats * FD ** (-0.25)]
    for shift in range(PAIRS):
        parts.append(floats * jnp.roll(floats, -shift, axis=-1) * (2.0 * FD) ** (-0.5))
    return jnp.concatenate(parts, axis=-1)


def plain_fold_matrix():
    row = jnp.arange(1 + FD + PAIRS * FD)[:, None]
    column = jnp.arange(1 + FD + FD * FD)[None, :]
    shift, first = (row - 1 - FD) // FD, (row - 1 - FD) % FD
    second = (first + shift) % FD
    major, minor = (column - 1 - FD) // FD, (column - 1 - FD) % FD
    straight = (major == first) & (minor == second)
    swapped = (major == second) & (minor == first) & (shift > 0) & (shift < FD // 2)
    squares = (row > FD) & (column > FD) & (straight | swapped)
    return jnp.where((row == column) & (row <= FD) | squares, 1.0, 0.0).astype(F32)


def line_gather(rows, axis, count):
    here = lax.axis_index(axis)
    size = rows.shape[0]
    up = down = rows
    ups, downs = [], []
    for step in range(1, count):
        up = lax.ppermute(up, axis, [(i, i + 1) for i in range(step - 1, count - 1)])
        down = lax.ppermute(down, axis, [(i + 1, i) for i in range(count - step)])
        ups.append(up)
        downs.append(down)
    around = jnp.concatenate(ups[::-1] + [rows] + downs)
    return lax.dynamic_slice_in_dim(around, (count - 1 - here) * size, count * size, 0)


def line_scatter(partial, axis, count):
    here = lax.axis_index(axis)
    size = partial.shape[0] // count

    def block(index):
        return lax.dynamic_slice_in_dim(partial, index * size, size, 0)

    up = down = None
    for step in range(1, count):
        to_up = block(jnp.minimum(here + count - step, count - 1))
        to_down = block(jnp.maximum(here - count + step, 0))
        if up is not None:
            to_up, to_down = to_up + up, to_down + down
        up = lax.ppermute(to_up, axis, [(i, i + 1) for i in range(step)])
        down = lax.ppermute(to_down, axis, [(i + 1, i) for i in range(count - 1 - step, count - 1)])
    return block(here).astype(F32) + up.astype(F32) + down.astype(F32)


def settle(partial, stream, axis, count):
    here = lax.axis_index(axis)
    size = partial.shape[0] // count
    mine = lax.dynamic_slice_in_dim(stream, here * size, size, 0)
    total = line_scatter(partial, axis, count)
    return line_gather((mine.astype(F32) + total).astype(BF), axis, count)


def bring_home(packs, axis, count):
    here = lax.axis_index(axis)
    bit = 1
    while bit < count:
        pairs = packs.reshape((packs.shape[0] // 2, 2) + packs.shape[1:])
        upper = (here & bit) != 0
        keep = jnp.where(upper, pairs[:, 1], pairs[:, 0])
        send = jnp.where(upper, pairs[:, 0], pairs[:, 1])
        packs = keep + lax.ppermute(send, axis, [(i, i ^ bit) for i in range(count)])
        bit *= 2
    return packs[0]


def make_plain(req_count, tensor_count):
    def per_device(
        hidden,
        suffix_len,
        request_group,
        group_slot,
        norm_first,
        query_weight,
        key_weight,
        value_weight,
        filter_gate,
        filter_taps,
        linear_out,
        norm_second,
        window_query,
        window_key,
        window_value,
        window_out,
        norm_third,
        gate_weight,
        up_weight,
        down_weight,
        prefix_sums,
        prefix_norms,
        prefix_keys,
        prefix_values,
        prefix_tail,
    ):
        requests_here = hidden.shape[0]
        share_rows = hidden.shape[1]
        slots_here, heads = prefix_sums.shape[:2]
        width = heads * HS

        groups = lax.all_gather(request_group, "req", axis=0, tiled=True)
        matches = jnp.arange(group_slot.shape[0])[None, :] == groups[:, None]
        slots = jnp.sum(jnp.where(matches, group_slot[None, :], 0), axis=1)
        fold = plain_fold_matrix()
        sums = jnp.einsum("fg,ahgd->afhd", fold, prefix_sums, precision=lax.Precision.HIGHEST)
        terms = sums.shape[1]
        norms = jnp.einsum("fg,ahg->afh", fold, prefix_norms, precision=lax.Precision.HIGHEST)
        norms = jnp.pad(norms.reshape(slots_here, -1), ((0, 0), (0, 2 * width - terms * heads)))
        pack = jnp.concatenate(
            [
                sums.reshape(slots_here, terms, width).astype(BF),
                norms.reshape(slots_here, 2, width).astype(BF),
                prefix_keys,
                prefix_values,
                prefix_tail,
            ],
            axis=1,
        )
        rows = pack.shape[1]
        pack = jnp.pad(pack, ((0, 0), (0, -rows % 32), (0, 0)))
        half = pack.shape[1] // 2
        pack = jnp.concatenate([pack[:, :half], pack[:, half:]], axis=2)
        local = slots - lax.axis_index("req") * slots_here
        owned = (local >= 0) & (local < slots_here)
        sent = jnp.take(pack, jnp.clip(local, 0, slots_here - 1), axis=0)
        sent = jnp.where(owned[:, None, None], sent, jnp.zeros_like(sent))
        sent = sent.reshape((req_count, requests_here) + sent.shape[1:])
        states = bring_home(sent, "req", req_count)
        states = jnp.concatenate([states[:, :, :width], states[:, :, width:]], axis=1)

        position = jnp.arange(LMAX)
        causal = position[:, None] >= position[None, :]
        bands = LMAX // WIN
        band_row = jnp.arange(WIN)[:, None]
        band_key = jnp.arange(2 * WIN)[None, :]
        allowed = (band_key > band_row) & (band_key <= band_row + WIN)

        def linear_part(request, stream):
            state = states[request]
            state_sums = state[:terms].reshape(terms, heads, HS)
            state_norms = state[terms : terms + 2].reshape(-1)[: terms * heads].reshape(terms, heads)
            tail = state[terms + 2 + 2 * WIN : terms + 2 + 2 * WIN + KC - 1]
            normed = rms_norm(stream, norm_first)
            queries = dot(normed, query_weight).astype(BF).reshape(LMAX, heads, FD)
            key_rows = dot(normed, key_weight).astype(BF).reshape(LMAX, heads, FD)
            values = dot(normed, value_weight).astype(BF)
            gating = dot(normed, filter_gate).astype(BF)
            extended = jnp.concatenate([tail, values], axis=0).astype(F32)
            convolved = sum(
                filter_taps[offset] * extended[KC - 1 - offset : KC - 1 - offset + LMAX]
                for offset in range(KC)
            )
            mixed = (convolved * jax.nn.silu(gating.astype(F32))).astype(BF)
            mixed = mixed.reshape(LMAX, heads, HS)
            scores = jnp.einsum("thf,shf->hts", queries, key_rows, preferred_element_type=F32)
            scores = scores * FD ** (-0.5)
            weights = jnp.where(causal, 1.0 + scores + 0.5 * scores * scores, 0.0)
            mapped = folded_features(queries)
            numerator = jnp.einsum(
                "hts,shd->thd", weights.astype(BF), mixed, preferred_element_type=F32
            ) + jnp.einsum(
                "htf,fhd->thd", mapped.astype(BF), state_sums, preferred_element_type=F32
            )
            denominator = jnp.sum(weights, axis=-1) + jnp.sum(
                mapped * jnp.transpose(state_norms).astype(F32)[:, None, :], axis=-1
            )
            linear_rows = (numerator / jnp.transpose(denominator)[..., None]).astype(BF)
            return dot(linear_rows.reshape(LMAX, width), linear_out).astype(BF)

        def window_part(request, stream):
            state = states[request]
            normed = rms_norm(stream, norm_second)
            queries = dot(normed, window_query).astype(BF).reshape(bands, WIN, heads, HS)
            key_rows = dot(normed, window_key).astype(BF)
            value_rows = dot(normed, window_value).astype(BF)
            start = terms + 2

            def paired(prefix, rows):
                blocks = jnp.concatenate([prefix, rows]).reshape(bands + 1, WIN, heads, HS)
                return jnp.concatenate([blocks[:-1], blocks[1:]], axis=1)

            key_pairs = paired(state[start : start + WIN], key_rows)
            value_pairs = paired(state[start + WIN : start + 2 * WIN], value_rows)
            logits = jnp.einsum(
                "bthd,bphd->bhtp", queries, key_pairs, preferred_element_type=F32
            ) * HS ** (-0.5)
            logits = jnp.where(allowed, logits, -jnp.inf)
            row_max = jnp.max(logits, axis=-1, keepdims=True)
            exponent = jnp.exp(logits - row_max)
            chances = (exponent / jnp.sum(exponent, axis=-1, keepdims=True)).astype(BF)
            attended = jnp.einsum(
                "bhtp,bphd->bthd", chances, value_pairs, preferred_element_type=F32
            ).astype(BF)
            final = (position == suffix_len[request] - 1).reshape(bands, 1, WIN)
            top = jnp.max(jnp.where(final, row_max[..., 0], -jnp.inf))
            return dot(attended.reshape(LMAX, width), window_out).astype(BF), top

        def hidden_part(stream):
            normed = rms_norm(stream, norm_third)
            inner = (jax.nn.silu(dot(normed, gate_weight)) * dot(normed, up_weight)).astype(BF)
            return dot(inner, down_weight).astype(BF)

        here = lax.axis_index("tensor")
        row_start = here * share_rows
        rows_here = row_start + jnp.arange(share_rows)
        outs, squares, tops = [], [], []
        for request in range(requests_here):
            stream = line_gather(hidden[request], "tensor", tensor_count)
            partial = linear_part(request, stream)
            stream = settle(partial, stream, "tensor", tensor_count)
            partial, top = window_part(request, stream)
            stream = settle(partial, stream, "tensor", tensor_count)
            partial = hidden_part(stream)
            total = line_scatter(partial, "tensor", tensor_count)
            mine = lax.dynamic_slice_in_dim(stream, row_start, share_rows, 0).astype(F32)
            mine = (mine + total).astype(BF)
            live = (rows_here < suffix_len[request])[:, None]
            outs.append(jnp.where(live, mine, jnp.zeros_like(mine)))
            floats = mine.astype(F32)
            squares.append(jnp.sum(jnp.where(live, floats * floats, 0.0)))
            tops.append(top)
        scalars = lax.all_gather(jnp.stack(squares + tops), "tensor")
        total = jnp.sum(scalars[:, :requests_here], axis=0)
        top_logit = jnp.max(scalars[:, requests_here:], axis=0)
        return jnp.stack(outs), jnp.sqrt(total / D), top_logit

    return per_device


def solution(mesh):
    return jax.shard_map(
        make_line(mesh.shape["req"]) if mesh.shape["tensor"] == 4 else make_plain(mesh.shape["req"], mesh.shape["tensor"]),
        mesh=mesh,
        in_specs=(
            P("req", "tensor", None),
            P("req"),
            P("req"),
            P(),
            P(),
            P(None, "tensor"),
            P(None, "tensor"),
            P(None, "tensor"),
            P(None, "tensor"),
            P(None, "tensor"),
            P("tensor", None),
            P(),
            P(None, "tensor"),
            P(None, "tensor"),
            P(None, "tensor"),
            P("tensor", None),
            P(),
            P(None, "tensor"),
            P(None, "tensor"),
            P("tensor", None),
            P("req", "tensor", None, None),
            P("req", "tensor", None),
            P("req", None, "tensor"),
            P("req", None, "tensor"),
            P("req", None, "tensor"),
        ),
        out_specs=(P("req", "tensor", None), P("req"), P("req")),
        check_vma=False,
    )
```
